32 devices in a mesh: group: 4 (over z), row: 8 (over y, x, core).
Axes of the slice: x: 2, y: 2, z: 4, core: 2. Of those that a mesh axis runs over, the one named last changes fastest.
Arguments:
- start_basis: float32 [256, 16, 128], P(('group', 'row')), may hold values from -6 to 6
- tiles: bfloat16 [256, 16, 128, 128], P(('group', 'row')), may hold values from -60000 to 60000
- tile_cols: int32 [256, 16], P(('group', 'row')), may hold values from 0 to 27, as said below
- tile_count: int32 [256], P(('group', 'row')), may hold values from 10 to 16, as said below
- recv_list: int32 [4, 8, 8, 2], P('group', 'row'), may hold values from -1 to 255, as said below
Outputs:
- krylov: float32 [3, 256, 16, 128], P(None, ('group', 'row'))
The draws below stay inside these ranges and needn't reach their ends.
Inputs may be any that keep to these rules, and one draw needn't show every extreme that they name: For each reader device and each other device of its range, recv_list names distinct blocks of that peer in its first slots and -1 in the rest; a reader's own entry is all -1; every reader gets exactly 2 blocks from some peer. tile_cols never names an empty receive slot, nor a rim slot of a range that does not exist (before the first or after the last group); every filled receive slot and every existing rim slot is named by some tile slot below 10. `tile_count`: every device has a row block with all 16 tiles live.
All inputs are finite; a program needn't handle non-finite values.
Results may differ from the reference program's by a relative error of at most 0.0003.
Values sent between devices are 32-bit elements; how exact they have to be, the bound alone decides.
No kernel may reach another device: no remote copies, remote signals or barrier semaphores. Data moves between devices by JAX's collectives and lax.ppermute only.
A program may use at most 64 MiB of HBM per device.

```python
import jax
import jax.numpy as jnp
from jax import lax

BLOCK = 128
VECS = 16
BLOCKS_DEV = 8
TILES_ROW = 16
SLOTS = 2
RIM = 2
ITERS = 3
GROUPS = 4
PEERS = 8
NBLOCKS = 256
MINLIVE = 10


def layout(key):
    seeded = jax.random.fold_in(key, 101)
    key_need, key_perm, key_fill, key_count, key_top = jax.random.split(seeded, 5)
    peer_q = jnp.arange(PEERS)[:, None]
    peer_p = jnp.arange(PEERS)[None, :]
    distance = jnp.abs(peer_q - peer_p)
    rolled = jax.random.randint(key_need, (GROUPS, PEERS, PEERS), 0, 2 * SLOTS + 2)
    near_count = jnp.minimum(rolled, SLOTS)
    far_count = jnp.clip(rolled - SLOTS, 0, SLOTS)
    needed = jnp.where(distance[None] <= 4, near_count, far_count)
    needed = jnp.where(distance[None] == 1, SLOTS, needed)
    needed = jnp.where(distance[None] == 0, 0, needed)
    scores = jax.random.randint(key_perm, (GROUPS, PEERS, PEERS, BLOCKS_DEV), 0, 1 << 20) * BLOCKS_DEV + jnp.arange(BLOCKS_DEV)
    ranking = jnp.argsort(scores, axis=-1)[..., :SLOTS]
    slot_ids = jnp.arange(SLOTS)
    taken = slot_ids[None, None, None, :] < needed[..., None]
    owner_dev = jnp.arange(GROUPS)[:, None, None, None] * PEERS + jnp.arange(PEERS)[None, None, :, None]
    received = jnp.where(taken, owner_dev * BLOCKS_DEV + ranking, -1).astype(jnp.int32)
    group_ids = jnp.arange(GROUPS)[:, None, None]
    own_ok = jnp.ones((GROUPS, PEERS, BLOCKS_DEV), jnp.bool_)
    peer_ok = taken.reshape(GROUPS, PEERS, PEERS * SLOTS)
    lower_ok = jnp.broadcast_to(group_ids > 0, (GROUPS, PEERS, RIM))
    upper_ok = jnp.broadcast_to(group_ids < GROUPS - 1, (GROUPS, PEERS, RIM))
    usable = jnp.concatenate([own_ok, peer_ok, lower_ok, upper_ok], axis=-1)
    extent = BLOCKS_DEV + PEERS * SLOTS + 2 * RIM
    sort_keys = jnp.where(usable, 0, extent) + jnp.arange(extent)
    compact = jnp.argsort(sort_keys, axis=-1).astype(jnp.int32)
    usable_count = jnp.sum(usable, axis=-1).astype(jnp.int32)
    cover_rank = jnp.arange(TILES_ROW)[None, :] * BLOCKS_DEV + jnp.arange(BLOCKS_DEV)[:, None]
    covered = cover_rank[None, None] < usable_count[..., None, None]
    fill_pick = jax.random.randint(key_fill, (GROUPS, PEERS, BLOCKS_DEV, TILES_ROW), 0, 1 << 20) % usable_count[..., None, None]
    position = jnp.where(covered, cover_rank[None, None], fill_pick).reshape(GROUPS, PEERS, BLOCKS_DEV * TILES_ROW)
    columns = jnp.take_along_axis(compact, position, axis=-1).reshape(NBLOCKS, TILES_ROW).astype(jnp.int32)
    rolled_count = jax.random.randint(key_count, (GROUPS, PEERS, BLOCKS_DEV), MINLIVE, TILES_ROW + 1)
    top_block = jax.random.randint(key_top, (GROUPS, PEERS, 1), 0, BLOCKS_DEV)
    counts = jnp.where(jnp.arange(BLOCKS_DEV)[None, None, :] == top_block, TILES_ROW, rolled_count)
    return (received, columns, counts.reshape(NBLOCKS).astype(jnp.int32))


def draw_recv_list(key, part):
    return layout(key)[0]


def draw_tile_cols(key, part):
    return layout(key)[1]


def draw_tile_count(key, part):
    return layout(key)[2]


def draw_tiles(key, part):
    seeded = jax.random.fold_in(key, 202)
    key_values, key_rows, key_cols = jax.random.split(seeded, 3)
    shape = (NBLOCKS, TILES_ROW, BLOCK, BLOCK)
    values = jnp.clip(jax.random.normal(key_values, shape, jnp.float32), -6.0, 6.0)
    rising = 9.0 ** (jnp.arange(NBLOCKS, dtype=jnp.float32) / NBLOCKS)
    row_scale = jnp.exp(jax.random.uniform(key_rows, (NBLOCKS, 1, BLOCK, 1), jnp.float32, 0.0, 4.6))
    col_scale = jnp.exp(jax.random.uniform(key_cols, (NBLOCKS, TILES_ROW, 1, BLOCK), jnp.float32, 0.0, 2.3))
    return (values * rising[:, None, None, None] * row_scale * col_scale).astype(jnp.bfloat16)


def block_levels(stream_key, dims, shards, low, top_value):
    factor_of = 1.0
    for dim, shards_of in shards:
        draws = jax.random.uniform(jax.random.fold_in(jax.random.fold_in(stream_key, 6), dim), (shards_of,), jnp.float32, low / len(shards), top_value / len(shards))
        factor_of = factor_of * jnp.repeat(jnp.exp(draws), dims[dim] // shards_of).reshape((-1,) + (1,) * (len(dims) - 1 - dim))
    return factor_of


def noise(key, shape, scale, limit, shards=(), kind=jnp.bfloat16):
    result = scale * jax.random.normal(key, shape, jnp.float32)
    if shards:
        result = result * block_levels(key, shape, shards, -0.22, 0.18)
    return jnp.clip(result, -limit, limit).astype(kind)


def setup_inputs(seed: int = 0) -> dict:
    seeds = jax.random.split(jax.random.key(seed), 6)
    return {
        "start_basis": noise(seeds[0], (NBLOCKS, VECS, BLOCK), 1.0, 6.0, ((0, 32),), jnp.float32),
        "tiles": draw_tiles(jax.random.fold_in(seeds[5], 71), 0),
        "tile_cols": draw_tile_cols(jax.random.fold_in(seeds[5], 71), 0),
        "tile_count": draw_tile_count(jax.random.fold_in(seeds[5], 71), 0),
        "recv_list": draw_recv_list(jax.random.fold_in(seeds[5], 71), 0),
    }


def slot_table(recv_list):
    devices = GROUPS * PEERS
    dev_ids = jnp.arange(devices, dtype=jnp.int32)
    own_ids = dev_ids[:, None] * BLOCKS_DEV + jnp.arange(BLOCKS_DEV, dtype=jnp.int32)[None, :]
    peer_ids = recv_list.reshape(devices, PEERS * SLOTS).astype(jnp.int32)
    group_of = dev_ids // PEERS
    rim_steps = jnp.arange(RIM, dtype=jnp.int32)[None, :]
    lower_ids = jnp.where((group_of > 0)[:, None], (dev_ids[:, None] - PEERS) * BLOCKS_DEV + BLOCKS_DEV - RIM + rim_steps, -1)
    upper_ids = jnp.where((group_of < GROUPS - 1)[:, None], (dev_ids[:, None] + PEERS) * BLOCKS_DEV + rim_steps, -1)
    return jnp.concatenate([own_ids, peer_ids, lower_ids.astype(jnp.int32), upper_ids.astype(jnp.int32)], axis=1)

def apply_op(tiles, global_cols, live_mask, inv_root, basis):
    devices = GROUPS * PEERS
    scaled = basis * inv_root[:, None, :]
    padded = jnp.concatenate([scaled, jnp.zeros((1, VECS, BLOCK), jnp.float32)], axis=0)

    def one_device(operands):
        tile_set, columns, mask_set, root_set = operands
        picked = jnp.take(padded, columns, axis=0) * mask_set[:, :, None, None]
        applied = jnp.einsum('btij,btkj->bki', tile_set.astype(jnp.float32), picked, precision=lax.Precision.HIGHEST)
        return applied * root_set[:, None, :]
    shaped = (tiles.reshape(devices, BLOCKS_DEV, TILES_ROW, BLOCK, BLOCK), global_cols.reshape(devices, BLOCKS_DEV, TILES_ROW), live_mask.reshape(devices, BLOCKS_DEV, TILES_ROW), inv_root.reshape(devices, BLOCKS_DEV, BLOCK))
    return lax.map(one_device, shaped).reshape(NBLOCKS, VECS, BLOCK)

def orthonormal(applied, gram_sum):
    factor = jnp.linalg.cholesky(gram_sum / (NBLOCKS * BLOCK))
    inverse = lax.linalg.triangular_solve(factor, jnp.eye(VECS, dtype=jnp.float32), left_side=True, lower=True)
    return jnp.einsum('kl,bli->bki', inverse, applied, precision=lax.Precision.HIGHEST)

def reference(start_basis, tiles, tile_cols, tile_count, recv_list):
    devices = GROUPS * PEERS
    live_mask = (jnp.arange(TILES_ROW, dtype=jnp.int32)[None, :] < tile_count[:, None]).astype(jnp.float32)

    def squares(operands):
        tile_set, mask_set = operands
        wide_tiles = tile_set.astype(jnp.float32)
        return jnp.einsum('btij,bt->bi', wide_tiles * wide_tiles, mask_set, precision=lax.Precision.HIGHEST)
    sum_sq = lax.map(squares, (tiles.reshape(devices, BLOCKS_DEV, TILES_ROW, BLOCK, BLOCK), live_mask.reshape(devices, BLOCKS_DEV, TILES_ROW))).reshape(NBLOCKS, BLOCK)
    inv_root = (1e-06 + sum_sq) ** (-0.25)
    table = slot_table(recv_list)
    dev_of_block = jnp.arange(NBLOCKS, dtype=jnp.int32) // BLOCKS_DEV
    global_cols = jnp.take_along_axis(table[dev_of_block], tile_cols.astype(jnp.int32), axis=1)
    global_cols = jnp.where(global_cols < 0, NBLOCKS, global_cols).astype(jnp.int32)
    basis = start_basis
    results = []
    for step_at in range(ITERS):
        applied = apply_op(tiles, global_cols, live_mask, inv_root, basis)
        gram_sum = jnp.einsum('bki,bli->kl', applied, applied, precision=lax.Precision.HIGHEST)
        basis = orthonormal(applied, gram_sum)
        results.append(basis)
    return jnp.stack(results)
```

```python
import jax
import jax.numpy as jnp
from jax import lax
from jax.sharding import PartitionSpec as P

SLOTS = 2
RIM = 2
ITERS = 3


def padded(x, sides, width):
    for axis, dim in sides:
        count, length = (lax.axis_size(axis), x.shape[dim])
        up = [(i, (i + 1) % count) for i in range(count - 1)]
        down = [(j, i) for i, j in up]
        last = lax.slice_in_dim(x, length - width, length, axis=dim)
        leading = lax.slice_in_dim(x, 0, width, axis=dim)
        before = lax.ppermute(last, axis, up)
        after = lax.ppermute(leading, axis, down)
        x = jnp.concatenate([before, x, after], axis=dim)
    return x


def orthonormal(applied, gram_sum, row_total):
    vectors = applied.shape[1]
    factor = jnp.linalg.cholesky(gram_sum / row_total)
    inverse = lax.linalg.triangular_solve(
        factor, jnp.eye(vectors, dtype=jnp.float32), left_side=True, lower=True
    )
    return jnp.einsum("kl,bli->bki", inverse, applied, precision=lax.Precision.HIGHEST)


def local(start_basis, tiles, tile_cols, tile_count, recv_list):
    groups = lax.axis_size("group")
    peers = lax.axis_size("row")
    group_at = lax.axis_index("group")
    blocks = tiles.shape[0]
    per_row = tiles.shape[1]
    tile_side = tiles.shape[2]
    row_total = groups * peers * blocks * tile_side
    live_mask = (jnp.arange(per_row, dtype=jnp.int32)[None, :] < tile_count[:, None]).astype(
        jnp.float32
    )
    wide_tiles = tiles.astype(jnp.float32)
    sum_sq = jnp.einsum(
        "btij,bt->bi", wide_tiles * wide_tiles, live_mask, precision=lax.Precision.HIGHEST
    )
    inv_root = (1e-06 + sum_sq) ** (-0.25)
    wanted = recv_list.reshape(peers, SLOTS)
    asked = lax.all_to_all(wanted, "row", 0, 0, tiled=True)
    first_own = (group_at * peers + lax.axis_index("row")) * blocks
    send_pick = jnp.clip(asked - first_own, 0, blocks - 1).reshape(-1)
    results = []
    basis = start_basis
    for step_at in range(ITERS):
        scaled = basis * inv_root[:, None, :]
        rimmed = padded(scaled, (("group", 0),), RIM)
        outgoing = jnp.take(scaled, send_pick, axis=0)
        received = lax.all_to_all(outgoing, "row", 0, 0, tiled=True)
        extended = jnp.concatenate([scaled, received, rimmed[:RIM], rimmed[blocks + RIM :]], axis=0)
        picked = jnp.take(extended, tile_cols, axis=0) * live_mask[:, :, None, None]
        product = jnp.einsum(
            "btij,btkj->bki",
            tiles,
            picked,
            precision=lax.Precision.HIGHEST,
            preferred_element_type=jnp.float32,
        )
        applied = product * inv_root[:, None, :]
        partial_value = jnp.einsum("bki,bli->kl", applied, applied, precision=lax.Precision.HIGHEST)
        gram_sum = jnp.sum(lax.all_gather(partial_value, ("group", "row"), axis=0), axis=0)
        basis = orthonormal(applied, gram_sum, row_total)
        results.append(basis)
    return jnp.stack(results)


def solution(mesh):
    placed = (
        P(("group", "row"), None, None),
        P(("group", "row"), None, None, None),
        P(("group", "row"), None),
        P(("group", "row")),
        P("group", "row", None, None),
    )
    return jax.shard_map(
        local,
        mesh=mesh,
        in_specs=placed,
        out_specs=P(None, ("group", "row"), None, None),
        check_vma=False,
    )
```

```python
import functools

import jax
import jax.numpy as jnp
from jax import lax
from jax.experimental import pallas as pl
from jax.experimental.pallas import tpu as pltpu
from jax.sharding import PartitionSpec as P

SLOTS = 2
RIM = 2
ITERS = 3
LANES = 128
PIECES = 3
VMEM_BYTES = 48 * 1024 * 1024
TRUST = 256.0
TINY = 1e-25

HIGH = lax.Precision.HIGHEST
NT = (((1,), (1,)), ((), ()))


def vmem():
    return pl.BlockSpec(memory_space=pltpu.VMEM)


def smem():
    return pl.BlockSpec(memory_space=pltpu.SMEM)


def f32(*shape):
    return jax.ShapeDtypeStruct(shape, jnp.float32)


def params():
    return pltpu.CompilerParams(vmem_limit_bytes=VMEM_BYTES)


def cost(flops, moved):
    return pl.CostEstimate(flops=flops, bytes_accessed=moved, transcendentals=0)


def roots_kernel(count_ref, tiles_ref, basis_ref, root_ref, scaled_ref):
    blocks, per_row, side, _ = tiles_ref.shape
    vectors = basis_ref.shape[1]
    for b in range(blocks):
        total = jnp.zeros((side, side), jnp.float32)
        for s in range(per_row):
            live = (s < count_ref[b]).astype(jnp.float32)
            wide = tiles_ref[b, s].astype(jnp.float32)
            total = total + wide * wide * live
        sums = jnp.sum(total.T, axis=0, keepdims=True)
        root = lax.rsqrt(jnp.sqrt(1e-06 + sums))
        root_ref[b] = root
        scaled_ref[b] = basis_ref[b] * root


def pick_kernel(me_ref, asked_ref, scaled_ref, out_ref):
    pick_into(me_ref, asked_ref, scaled_ref, out_ref)


def pick_into(me_ref, asked_ref, scaled_ref, out_ref):
    blocks = scaled_ref.shape[0]
    peers = asked_ref.shape[0]
    me, first = me_ref[0], me_ref[1]
    for p in range(peers):
        for c in range(SLOTS):
            at = jnp.clip(asked_ref[p, c, me] - first, 0, blocks - 1)
            out_ref[p * SLOTS + c] = scaled_ref[at]


def split_into(x, out_ref, slot):
    vectors = x.shape[0]
    rest = x
    for piece in range(PIECES):
        part = rest.astype(jnp.bfloat16)
        out_ref[slot, pl.ds(piece * vectors, vectors)] = part
        if piece < PIECES - 1:
            rest = rest - part.astype(jnp.float32)


def pack_grams(grams):
    half = grams[0].shape[0] // 2
    parts = [g[:half] for g in grams] + [g[half:] for g in grams]
    spare = LANES - len(parts) * grams[0].shape[1]
    return jnp.concatenate(parts + [jnp.zeros((half, spare), jnp.float32)], axis=1)


def unpack_grams(packed, vectors):
    upper = [packed[:, t * vectors : (t + 1) * vectors] for t in range(ITERS)]
    lower = [packed[:, (ITERS + t) * vectors : (ITERS + t + 1) * vectors] for t in range(ITERS)]
    return [jnp.concatenate(pair, axis=0) for pair in zip(upper, lower)]


def apply_kernel(last, *refs):
    if last:
        (count_ref, cols_ref, tiles_ref, root_ref, own_ref, recv_ref, low_ref, high_ref,
         *before, applied_ref, gram_ref, table) = refs
    else:
        (count_ref, cols_ref, me_ref, asked_ref, tiles_ref, root_ref, own_ref, recv_ref, low_ref,
         high_ref, applied_ref, gram_ref, scaled_ref, out_ref, table) = refs
    blocks, per_row, side, _ = tiles_ref.shape
    vectors = own_ref.shape[1]
    slot = 0
    for ref in (own_ref, recv_ref, low_ref, high_ref):
        for b in range(ref.shape[0]):
            split_into(ref[b], table, slot)
            slot += 1
    table[slot] = jnp.zeros(table.shape[1:], table.dtype)
    rows = []
    for b in range(blocks):
        picked = []
        for s in range(per_row):
            at = jnp.where(s < count_ref[b], cols_ref[b, s], slot)
            picked.append(table[at])
        x = jnp.concatenate(picked, axis=1)
        t = jnp.concatenate([tiles_ref[b, s] for s in range(per_row)], axis=1)
        product = lax.dot_general(x, t, NT, preferred_element_type=jnp.float32)
        total = product[(PIECES - 1) * vectors :]
        for piece in range(PIECES - 2, -1, -1):
            total = total + product[piece * vectors : (piece + 1) * vectors]
        root = root_ref[b]
        row = total * root
        applied_ref[b] = row
        rows.append(row)
        if not last:
            scaled_ref[b] = row * root
    flat = jnp.concatenate(rows, axis=1)
    gram = lax.dot_general(flat, flat, NT, precision=HIGH, preferred_element_type=jnp.float32)
    if last:
        packed = pack_grams([ref[...] for ref in before] + [gram])
        for n in range(gram_ref.shape[0]):
            gram_ref[n] = packed
    else:
        gram_ref[...] = gram
        pick_into(me_ref, asked_ref, scaled_ref, out_ref)


def finish_kernel(row_total, grams_ref, *refs):
    applied_refs, (out_ref, trust_ref) = refs[:ITERS], refs[ITERS:]
    devices = grams_ref.shape[0]
    blocks, vectors = out_ref.shape[1:3]
    total = grams_ref[0]
    for n in range(1, devices):
        total = total + grams_ref[n]
    rows = lax.broadcasted_iota(jnp.int32, (vectors, vectors), 0)
    lanes = lax.broadcasted_iota(jnp.int32, (vectors, vectors), 1)
    unit = (rows == lanes).astype(jnp.float32)
    row_at = lax.broadcasted_iota(jnp.int32, (vectors, 1), 0)
    grams = unpack_grams(total, vectors)
    work = [jnp.concatenate([gram, unit], axis=1) for gram in grams]
    for j in range(vectors):
        for t in range(ITERS):
            m = work[t]
            ratio = jnp.where(row_at > j, m[:, j : j + 1] / m[j : j + 1, j : j + 1], 0.0)
            work[t] = m - ratio * m[j : j + 1, :]
    good = jnp.bool_(True)
    for t in range(ITERS):
        m = work[t]
        pivots = jnp.sum(m[:, :vectors] * unit, axis=1, keepdims=True)
        inverse = m[:, vectors:] * lax.rsqrt(pivots / row_total)
        squares = jnp.sum(grams[t] * unit, axis=0, keepdims=True)
        norm = jnp.sum(inverse * inverse * squares) / row_total
        good = good & (norm < TRUST) & (jnp.min(squares) > TINY)
        for b in range(blocks):
            out_ref[t, b] = lax.dot_general(
                inverse, applied_refs[t][b], (((1,), (0,)), ((), ())), precision=HIGH,
                preferred_element_type=jnp.float32,
            )
    trust_ref[0] = good.astype(jnp.int32)


def neighbours(scaled):
    count, blocks = lax.axis_size("group"), scaled.shape[0]
    up = [(i, i + 1) for i in range(count - 1)]
    down = [(i + 1, i) for i in range(count - 1)]
    low = lax.ppermute(scaled[blocks - RIM :], "group", up)
    high = lax.ppermute(scaled[:RIM], "group", down)
    return low, high


def exchange(outgoing):
    return lax.all_to_all(outgoing, "row", 0, 0, tiled=True)


def stepwise(start_basis, tiles, tile_cols, tile_count, recv_list):
    groups, peers = lax.axis_size("group"), lax.axis_size("row")
    blocks, per_row, side, _ = tiles.shape
    vectors = start_basis.shape[1]
    row_total = groups * peers * blocks * side
    live = jnp.arange(per_row, dtype=jnp.int32)[None, :] < tile_count[:, None]
    live = live.astype(jnp.float32)
    wide = tiles.astype(jnp.float32)
    sums = jnp.einsum("btij,bt->bi", wide * wide, live, precision=HIGH)
    root = (1e-06 + sums) ** (-0.25)
    wanted = recv_list.reshape(peers * SLOTS)
    take = jnp.clip(wanted - lax.axis_index("group") * peers * blocks, 0, peers * blocks - 1)
    basis, results = start_basis, []
    for _ in range(ITERS):
        scaled = basis * root[:, None, :]
        low, high = neighbours(scaled)
        received = jnp.take(lax.all_gather(scaled, "row", axis=0, tiled=True), take, axis=0)
        extended = jnp.concatenate([scaled, received, low, high], axis=0)
        picked = jnp.take(extended, tile_cols, axis=0) * live[:, :, None, None]
        product = jnp.einsum(
            "btij,btkj->bki", tiles, picked, precision=HIGH, preferred_element_type=jnp.float32
        )
        applied = product * root[:, None, :]
        gram = jnp.einsum("bki,bli->kl", applied, applied, precision=HIGH)
        factor = jnp.linalg.cholesky(lax.psum(gram, ("group", "row")) / row_total)
        inverse = lax.linalg.triangular_solve(
            factor, jnp.eye(vectors, dtype=jnp.float32), left_side=True, lower=True
        )
        basis = jnp.einsum("kl,bli->bki", inverse, applied, precision=HIGH)
        results.append(basis)
    return jnp.stack(results)


def local(start_basis, tiles, tile_cols, tile_count, recv_list):
    groups, peers = lax.axis_size("group"), lax.axis_size("row")
    blocks, per_row, side, _ = tiles.shape
    vectors = start_basis.shape[1]
    row_at = lax.axis_index("row")
    first = (lax.axis_index("group") * peers + row_at) * blocks
    me = jnp.stack([row_at, first]).astype(jnp.int32)
    listed = jnp.transpose(recv_list.reshape(peers, SLOTS))
    asked = lax.all_to_all(
        jnp.broadcast_to(listed[None], (peers, SLOTS, peers)), "row", 0, 0, tiled=True
    )
    tile_bytes = tiles.size * 2
    root, scaled = pl.pallas_call(
        roots_kernel,
        out_shape=(f32(blocks, 1, side), f32(blocks, vectors, side)),
        in_specs=[smem(), vmem(), vmem()],
        out_specs=(vmem(), vmem()),
        compiler_params=params(),
        cost_estimate=cost(tiles.size * 2, tile_bytes),
        name="roots",
    )(tile_count, tiles, start_basis)
    outgoing = pl.pallas_call(
        pick_kernel,
        out_shape=f32(peers * SLOTS, vectors, side),
        in_specs=[smem(), smem(), vmem()],
        out_specs=vmem(),
        compiler_params=params(),
        name="pick",
    )(me, asked, scaled)
    slots = blocks + peers * SLOTS + 2 * RIM
    powers, grams = [], []
    for t in range(ITERS):
        last = t == ITERS - 1
        received = exchange(outgoing)
        low, high = neighbours(scaled)
        shapes = [f32(blocks, vectors, side)]
        scalars = [tile_count, tile_cols]
        arrays = [tiles, root, scaled, received, low, high]
        if last:
            shapes += [f32(groups * peers, vectors // 2, LANES)]
            arrays += grams
        else:
            shapes += [f32(vectors, vectors)]
            shapes += [f32(blocks, vectors, side), f32(peers * SLOTS, vectors, side)]
            scalars += [me, asked]
        result = pl.pallas_call(
            functools.partial(apply_kernel, last),
            out_shape=tuple(shapes),
            in_specs=[smem()] * len(scalars) + [vmem()] * len(arrays),
            out_specs=tuple(vmem() for _ in shapes),
            scratch_shapes=[pltpu.VMEM((slots + 1, PIECES * vectors, side), jnp.bfloat16)],
            compiler_params=params(),
            cost_estimate=cost(tiles.size * 2 * vectors * PIECES, tile_bytes),
            name="apply_last" if last else "apply",
        )(*scalars, *arrays)
        powers.append(result[0])
        grams.append(result[1])
        if not last:
            scaled, outgoing = result[2], result[3]
    gathered = lax.all_to_all(grams[-1], ("group", "row"), 0, 0, tiled=True)
    krylov, trust = pl.pallas_call(
        functools.partial(finish_kernel, float(groups * peers * blocks * side)),
        out_shape=(f32(ITERS, blocks, vectors, side), jax.ShapeDtypeStruct((1,), jnp.int32)),
        in_specs=[vmem()] * (1 + ITERS),
        out_specs=(vmem(), smem()),
        compiler_params=params(),
        name="finish",
    )(gathered, *powers)
    return lax.cond(
        trust[0] > 0,
        lambda *_: krylov,
        stepwise,
        start_basis, tiles, tile_cols, tile_count, recv_list,
    )


def solution(mesh):
    placed = (
        P(("group", "row"), None, None),
        P(("group", "row"), None, None, None),
        P(("group", "row"), None),
        P(("group", "row")),
        P("group", "row", None, None),
    )
    return jax.shard_map(
        local,
        mesh=mesh,
        in_specs=placed,
        out_specs=P(None, ("group", "row"), None, None),
        check_vma=False,
    )
```

```python
import functools

import jax
import jax.numpy as jnp
from jax import lax
from jax.experimental import pallas as pl
from jax.experimental.pallas import tpu as pltpu
from jax.sharding import PartitionSpec as P

SLOTS = 2
RIM = 2
ITERS = 3
LANES = 128
PIECES = 3
VMEM_BYTES = 24 * 1024 * 1024
TRUST = 256.0
TINY = 1e-25

HIGH = lax.Precision.HIGHEST
NT = (((1,), (1,)), ((), ()))


def vmem():
    return pl.BlockSpec(memory_space=pltpu.VMEM)


def smem():
    return pl.BlockSpec(memory_space=pltpu.SMEM)


def anywhere():
    return pl.BlockSpec(memory_space=pl.ANY)


def f32(*shape):
    return jax.ShapeDtypeStruct(shape, jnp.float32)


def params():
    return pltpu.CompilerParams(vmem_limit_bytes=VMEM_BYTES)


def cost(flops, moved):
    return pl.CostEstimate(flops=flops, bytes_accessed=moved, transcendentals=0)


def roots_kernel(group_ref, count_ref, want_ref, tiles_hbm, basis_ref, root_ref, scaled_ref,
                 tiles_ref, spread_hbm, rim_ref, lists, tile_sems, sems):
    blocks, per_row, side, _ = tiles_ref.shape
    peers = spread_hbm.shape[0]
    loads = [
        pltpu.make_async_copy(tiles_hbm.at[b], tiles_ref.at[b], tile_sems.at[b])
        for b in range(blocks)
    ]
    for load in loads:
        load.start()
    half = lists.shape[2] // SLOTS
    for p in range(peers):
        owned = (group_ref[0] * peers + p) * blocks
        for c in range(SLOTS):
            at = jnp.full((half, side), want_ref[c, p] - owned, jnp.int32)
            lists[p, 0, pl.ds(c * half, half)] = at.astype(jnp.float32)
    sends = [pltpu.make_async_copy(lists, spread_hbm.at[:, pl.ds(blocks, 1)], sems.at[peers])]
    sends[0].start()
    for b in range(blocks):
        loads[b].wait()
        total = jnp.zeros((side, side), jnp.float32)
        for s in range(per_row):
            live = (s < count_ref[b]).astype(jnp.float32)
            wide = tiles_ref[b, s].astype(jnp.float32)
            total = total + wide * wide * live
        sums = jnp.sum(total.T, axis=0, keepdims=True)
        root = lax.rsqrt(jnp.sqrt(1e-06 + sums))
        root_ref[b] = root
        scaled_ref[b] = basis_ref[b] * root
    for p in range(peers):
        send = pltpu.make_async_copy(scaled_ref, spread_hbm.at[p, pl.ds(0, blocks)], sems.at[p])
        send.start()
        sends.append(send)
    rims_into(group_ref[0], scaled_ref, rim_ref)
    for send in sends:
        send.wait()


def rims_into(group, scaled_ref, rim_ref):
    blocks = scaled_ref.shape[0]
    for d in range(rim_ref.shape[0]):
        start = jnp.where(d < group, 0, blocks - RIM)
        for h in range(RIM):
            rim_ref[d, h] = scaled_ref[start + h]


def pick_into(asked_ref, scaled_ref, out_ref):
    peers, blocks, vectors, _ = asked_ref.shape
    blocks -= 1
    half = vectors // SLOTS
    for p in range(peers):
        for c in range(SLOTS):
            at = asked_ref[p, blocks, c * half : (c + 1) * half]
            for row in range(0, vectors, half):
                rows = slice(row, row + half)
                value = scaled_ref[0, rows]
                for b in range(1, blocks):
                    value = jnp.where(at == float(b), scaled_ref[b, rows], value)
                out_ref[p * SLOTS + c, rows] = value


def split_into(x, out_ref, slot):
    vectors = x.shape[0]
    rest = x
    for piece in range(PIECES):
        part = rest.astype(jnp.bfloat16)
        out_ref[slot, pl.ds(piece * vectors, vectors)] = part
        if piece < PIECES - 1:
            rest = rest - part.astype(jnp.float32)


def pack_grams(grams):
    half = grams[0].shape[0] // 2
    parts = [g[:half] for g in grams] + [g[half:] for g in grams]
    spare = LANES - len(parts) * grams[0].shape[1]
    return jnp.concatenate(parts + [jnp.zeros((half, spare), jnp.float32)], axis=1)


def unpack_grams(packed, vectors):
    upper = [packed[:, t * vectors : (t + 1) * vectors] for t in range(ITERS)]
    lower = [packed[:, (ITERS + t) * vectors : (ITERS + t + 1) * vectors] for t in range(ITERS)]
    return [jnp.concatenate(pair, axis=0) for pair in zip(upper, lower)]


def apply_kernel(step_at, *refs):
    last, opening = step_at == ITERS - 1, step_at == 0
    group_ref, count_ref, cols_ref, *refs = refs
    if opening:
        want_ref, *refs = refs
    tiles_ref, root_ref, own_ref, recv_ref, recv_rim_ref, *refs = refs
    if last:
        *before, applied_ref, gram_ref, table = refs
    else:
        asked_ref, refs = (recv_ref, refs) if opening else (refs[0], refs[1:])
        applied_ref, gram_ref, scaled_ref, out_hbm, rim_ref, table, picked_ref, sem = refs
    blocks, per_row, side, _ = tiles_ref.shape
    vectors = own_ref.shape[1]
    group = group_ref[0]
    slot = 0
    for b in range(blocks):
        split_into(own_ref[b], table, slot)
        slot += 1
    if opening:
        peers = recv_ref.shape[0]
        for p in range(peers):
            for c in range(SLOTS):
                at = jnp.clip(want_ref[c, p] - (group * peers + p) * blocks, 0, blocks - 1)
                split_into(recv_ref[p, at], table, slot)
                slot += 1
    else:
        for n in range(recv_ref.shape[0]):
            split_into(recv_ref[n], table, slot)
            slot += 1
    groups = recv_rim_ref.shape[0]
    for side_at in (jnp.maximum(group - 1, 0), jnp.minimum(group + 1, groups - 1)):
        for h in range(RIM):
            split_into(recv_rim_ref[side_at, h], table, slot)
            slot += 1
    table[slot] = jnp.zeros(table.shape[1:], table.dtype)
    rows = []
    for b in range(blocks):
        picked = []
        for s in range(per_row):
            at = jnp.where(s < count_ref[b], cols_ref[b, s], slot)
            picked.append(table[at])
        x = jnp.concatenate(picked, axis=1)
        t = jnp.concatenate([tiles_ref[b, s] for s in range(per_row)], axis=1)
        product = lax.dot_general(x, t, NT, preferred_element_type=jnp.float32)
        total = product[(PIECES - 1) * vectors :]
        for piece in range(PIECES - 2, -1, -1):
            total = total + product[piece * vectors : (piece + 1) * vectors]
        root = root_ref[b]
        row = total * root
        applied_ref[b] = row
        rows.append(row)
        if not last:
            scaled_ref[b] = row * root
    if not last:
        pick_into(asked_ref, scaled_ref, picked_ref)
        send = pltpu.make_async_copy(picked_ref, out_hbm, sem)
        send.start()
        rims_into(group, scaled_ref, rim_ref)
    flat = jnp.concatenate(rows, axis=1)
    gram = lax.dot_general(flat, flat, NT, precision=HIGH, preferred_element_type=jnp.float32)
    if last:
        packed = pack_grams([ref[...] for ref in before] + [gram])
        for n in range(gram_ref.shape[0]):
            gram_ref[n] = packed
    else:
        gram_ref[...] = gram
        send.wait()


def finish_kernel(row_total, grams_ref, *refs):
    applied_refs, (out_ref, trust_ref) = refs[:ITERS], refs[ITERS:]
    devices = grams_ref.shape[0]
    blocks, vectors = out_ref.shape[1:3]
    total = grams_ref[0]
    for n in range(1, devices):
        total = total + grams_ref[n]
    rows = lax.broadcasted_iota(jnp.int32, (vectors, vectors), 0)
    lanes = lax.broadcasted_iota(jnp.int32, (vectors, vectors), 1)
    unit = (rows == lanes).astype(jnp.float32)
    row_at = lax.broadcasted_iota(jnp.int32, (vectors, 1), 0)
    grams = unpack_grams(total, vectors)
    work = [jnp.concatenate([gram, unit], axis=1) for gram in grams]
    for j in range(vectors):
        for t in range(ITERS):
            m = work[t]
            ratio = jnp.where(row_at > j, m[:, j : j + 1] / m[j : j + 1, j : j + 1], 0.0)
            work[t] = m - ratio * m[j : j + 1, :]
    good = jnp.bool_(True)
    for t in range(ITERS):
        m = work[t]
        pivots = jnp.sum(m[:, :vectors] * unit, axis=1, keepdims=True)
        inverse = m[:, vectors:] * lax.rsqrt(pivots / row_total)
        squares = jnp.sum(grams[t] * unit, axis=0, keepdims=True)
        norm = jnp.sum(inverse * inverse * squares) / row_total
        good = good & (norm < TRUST) & (jnp.min(squares) > TINY)
        for b in range(blocks):
            out_ref[t, b] = lax.dot_general(
                inverse, applied_refs[t][b], (((1,), (0,)), ((), ())), precision=HIGH,
                preferred_element_type=jnp.float32,
            )
    trust_ref[0] = good.astype(jnp.int32)


def neighbours(scaled):
    count, blocks = lax.axis_size("group"), scaled.shape[0]
    up = [(i, i + 1) for i in range(count - 1)]
    down = [(i + 1, i) for i in range(count - 1)]
    low = lax.ppermute(scaled[blocks - RIM :], "group", up)
    high = lax.ppermute(scaled[:RIM], "group", down)
    return low, high


def exchange(outgoing):
    return lax.all_to_all(outgoing, "row", 0, 0, tiled=True)


def stepwise(start_basis, tiles, tile_cols, tile_count, recv_list):
    groups, peers = lax.axis_size("group"), lax.axis_size("row")
    blocks, per_row, side, _ = tiles.shape
    vectors = start_basis.shape[1]
    row_total = groups * peers * blocks * side
    live = jnp.arange(per_row, dtype=jnp.int32)[None, :] < tile_count[:, None]
    live = live.astype(jnp.float32)
    wide = tiles.astype(jnp.float32)
    sums = jnp.einsum("btij,bt->bi", wide * wide, live, precision=HIGH)
    root = (1e-06 + sums) ** (-0.25)
    wanted = recv_list.reshape(peers * SLOTS)
    take = jnp.clip(wanted - lax.axis_index("group") * peers * blocks, 0, peers * blocks - 1)
    basis, results = start_basis, []
    for _ in range(ITERS):
        scaled = basis * root[:, None, :]
        low, high = neighbours(scaled)
        received = jnp.take(lax.all_gather(scaled, "row", axis=0, tiled=True), take, axis=0)
        extended = jnp.concatenate([scaled, received, low, high], axis=0)
        picked = jnp.take(extended, tile_cols, axis=0) * live[:, :, None, None]
        product = jnp.einsum(
            "btij,btkj->bki", tiles, picked, precision=HIGH, preferred_element_type=jnp.float32
        )
        applied = product * root[:, None, :]
        gram = jnp.einsum("bki,bli->kl", applied, applied, precision=HIGH)
        factor = jnp.linalg.cholesky(lax.psum(gram, ("group", "row")) / row_total)
        inverse = lax.linalg.triangular_solve(
            factor, jnp.eye(vectors, dtype=jnp.float32), left_side=True, lower=True
        )
        basis = jnp.einsum("kl,bli->bki", inverse, applied, precision=HIGH)
        results.append(basis)
    return jnp.stack(results)


def local(start_basis, tiles, tile_cols, tile_count, recv_list):
    groups, peers = lax.axis_size("group"), lax.axis_size("row")
    blocks, per_row, side, _ = tiles.shape
    vectors = start_basis.shape[1]
    group = lax.axis_index("group").astype(jnp.int32).reshape(1)
    wanted = jnp.transpose(recv_list.reshape(peers, SLOTS))
    tile_bytes = tiles.size * 2
    block_shape = (vectors, side)
    picked_shape = (peers * SLOTS,) + block_shape
    rim_shape = f32(groups, RIM, *block_shape)
    root, scaled, held, spread, rims = pl.pallas_call(
        roots_kernel,
        out_shape=(
            f32(blocks, 1, side),
            f32(blocks, *block_shape),
            pltpu.VMEM(tiles.shape, tiles.dtype),
            f32(peers, blocks + 1, *block_shape),
            rim_shape,
        ),
        in_specs=[smem(), smem(), smem(), anywhere(), vmem()],
        out_specs=(vmem(), vmem(), vmem(), anywhere(), vmem()),
        scratch_shapes=[
            pltpu.VMEM((peers, 1) + block_shape, jnp.float32),
            pltpu.SemaphoreType.DMA((blocks,)),
            pltpu.SemaphoreType.DMA((peers + 1,)),
        ],
        compiler_params=params(),
        cost_estimate=cost(tiles.size * 2, tile_bytes),
        name="roots",
    )(group, tile_count, wanted, tiles, start_basis)
    slots = blocks + peers * SLOTS + 2 * RIM
    powers, grams = [], []
    outgoing = spread
    for t in range(ITERS):
        last = t == ITERS - 1
        received = exchange(outgoing)
        if t == 0:
            asked = received
        beside = lax.all_to_all(rims, "group", 0, 0, tiled=True)
        scalars = [group, tile_count, tile_cols] + ([wanted] if t == 0 else [])
        arrays = [held, root, scaled, received, beside]
        shapes = [f32(blocks, *block_shape)]
        specs = [vmem(), vmem()]
        scratch = [pltpu.VMEM((slots + 1, PIECES * vectors, side), jnp.bfloat16)]
        if last:
            shapes += [f32(groups * peers, vectors // 2, LANES)]
            arrays += grams
        else:
            shapes += [f32(vectors, vectors), f32(blocks, *block_shape), f32(*picked_shape), rim_shape]
            specs += [vmem(), anywhere(), vmem()]
            scratch += [pltpu.VMEM(picked_shape, jnp.float32), pltpu.SemaphoreType.DMA]
            arrays += [asked] if t else []
        result = pl.pallas_call(
            functools.partial(apply_kernel, t),
            out_shape=tuple(shapes),
            in_specs=[smem()] * len(scalars) + [vmem()] * len(arrays),
            out_specs=tuple(specs),
            scratch_shapes=scratch,
            compiler_params=params(),
            cost_estimate=cost(tiles.size * 2 * vectors * PIECES, tile_bytes),
            name="apply_last" if last else "apply",
        )(*scalars, *arrays)
        powers.append(result[0])
        grams.append(result[1])
        if not last:
            scaled, outgoing, rims = result[2:]
    gathered = lax.all_to_all(grams[-1], ("group", "row"), 0, 0, tiled=True)
    krylov, trust = pl.pallas_call(
        functools.partial(finish_kernel, float(groups * peers * blocks * side)),
        out_shape=(f32(ITERS, blocks, vectors, side), jax.ShapeDtypeStruct((1,), jnp.int32)),
        in_specs=[vmem()] * (1 + ITERS),
        out_specs=(vmem(), smem()),
        compiler_params=params(),
        name="finish",
    )(gathered, *powers)
    return lax.cond(
        trust[0] > 0,
        lambda *_: krylov,
        stepwise,
        start_basis, tiles, tile_cols, tile_count, recv_list,
    )


def solution(mesh):
    placed = (
        P(("group", "row"), None, None),
        P(("group", "row"), None, None, None),
        P(("group", "row"), None),
        P(("group", "row")),
        P("group", "row", None, None),
    )
    return jax.shard_map(
        local,
        mesh=mesh,
        in_specs=placed,
        out_specs=P(None, ("group", "row"), None, None),
        check_vma=False,
    )
```

```python
import functools

import jax
import jax.numpy as jnp
from jax import lax
from jax.experimental import pallas as pl
from jax.experimental.pallas import tpu as pltpu
from jax.sharding import PartitionSpec as P

SLOTS = 2
RIM = 2
ITERS = 3
LANES = 128
PIECES = 2
VMEM_BYTES = 24 * 1024 * 1024
TRUST = 64.0
TINY = 1e-25

HIGH = lax.Precision.HIGHEST
NT = (((1,), (1,)), ((), ()))


def vmem():
    return pl.BlockSpec(memory_space=pltpu.VMEM)


def smem():
    return pl.BlockSpec(memory_space=pltpu.SMEM)


def hbm():
    return pl.BlockSpec(memory_space=pltpu.HBM)


def f32(*shape):
    return jax.ShapeDtypeStruct(shape, jnp.float32)


def params():
    return pltpu.CompilerParams(vmem_limit_bytes=VMEM_BYTES)


def cost(flops, moved):
    return pl.CostEstimate(flops=flops, bytes_accessed=moved, transcendentals=0)


def stream(tiles_hbm, tiles_ref, sems):
    loads = [
        pltpu.make_async_copy(tiles_hbm.at[b], tiles_ref.at[b], sems.at[b])
        for b in range(tiles_ref.shape[0])
    ]
    for load in loads:
        load.start()
    return loads


def stream_scratch(tiles):
    return [pltpu.VMEM(tiles.shape, tiles.dtype), pltpu.SemaphoreType.DMA((tiles.shape[0],))]


def roots_kernel(place_ref, count_ref, want_ref, tiles_hbm, basis_ref, root_ref, sent_ref,
                 first_ref, second_ref, tiles_ref, load_sems):
    blocks, per_row, side, _ = tiles_ref.shape
    peers = want_ref.shape[1]
    vectors = basis_ref.shape[1]
    loads = stream(tiles_hbm, tiles_ref, load_sems)
    for p in range(peers):
        owned = (place_ref[0] * peers + p) * blocks
        for c in range(SLOTS):
            at = jnp.full((1, side), want_ref[c, p] - owned, jnp.int32).astype(jnp.float32)
            block, row = divmod(p * SLOTS + c, vectors)
            sent_ref[blocks + block, row : row + 1] = at
    rows = lax.broadcasted_iota(jnp.int32, (side, side), 0)
    lanes = lax.broadcasted_iota(jnp.int32, (side, side), 1)
    unit = rows == lanes
    for b in range(blocks):
        loads[b].wait()
        held = [tiles_ref[b, s] for s in range(per_row)]
        live = [
            jnp.where(s < count_ref[b], tile, jnp.zeros_like(tile)) for s, tile in enumerate(held)
        ]
        products = lax.dot_general(
            jnp.concatenate(live, axis=1), jnp.concatenate(held, axis=1), NT,
            preferred_element_type=jnp.float32,
        )
        sums = jnp.sum(jnp.where(unit, products, 0.0), axis=0, keepdims=True)
        root = lax.rsqrt(jnp.sqrt(1e-06 + sums))
        root_ref[b] = root
        sent_ref[b] = basis_ref[b] * root
    swaps_into(place_ref[0], blocks, sent_ref, first_ref, second_ref)


def swaps_into(group, blocks, scaled_ref, first_ref, second_ref):
    odd = group % 2
    for h in range(RIM):
        first_ref[h] = scaled_ref[(1 - odd) * (blocks - RIM) + h]
        second_ref[h] = scaled_ref[odd * (blocks - RIM) + h]


def pick_into(row_at, asked_ref, scaled_ref, out_ref):
    peers = asked_ref.shape[0]
    blocks, vectors, side = scaled_ref.shape
    for p in range(peers):
        for c in range(SLOTS):
            entry = row_at * SLOTS + c
            at = asked_ref[p, blocks + entry // vectors, pl.ds(entry % vectors, 1)]
            at = jnp.broadcast_to(at, (vectors, side))
            value = scaled_ref[0]
            for b in range(1, blocks):
                value = jnp.where(at == float(b), scaled_ref[b], value)
            out_ref[p * SLOTS + c] = value


def split_into(x, out_ref, slot):
    vectors = x.shape[0]
    rest = x
    for piece in range(PIECES):
        part = rest.astype(jnp.bfloat16)
        out_ref[slot, pl.ds(piece * vectors, vectors)] = part
        if piece < PIECES - 1:
            rest = rest - part.astype(jnp.float32)


def pack_grams(grams):
    half = grams[0].shape[0] // 2
    parts = [g[:half] for g in grams] + [g[half:] for g in grams]
    spare = LANES - len(parts) * grams[0].shape[1]
    return jnp.concatenate(parts + [jnp.zeros((half, spare), jnp.float32)], axis=1)


def unpack_grams(packed, vectors):
    upper = [packed[:, t * vectors : (t + 1) * vectors] for t in range(ITERS)]
    lower = [packed[:, (ITERS + t) * vectors : (ITERS + t + 1) * vectors] for t in range(ITERS)]
    return [jnp.concatenate(pair, axis=0) for pair in zip(upper, lower)]


def apply_kernel(step_at, *refs):
    last, opening = step_at == ITERS - 1, step_at == 0
    place_ref, count_ref, cols_ref, *refs = refs
    if opening:
        want_ref, *refs = refs
    tiles_hbm, root_ref, own_ref, recv_ref, swapped_ref, swapped_next_ref, *refs = refs
    *refs, tiles_ref, load_sems = refs
    loads = stream(tiles_hbm, tiles_ref, load_sems)
    if last:
        *before, applied_ref, gram_hbm, table, packed_ref, sems = refs
    else:
        asked_ref, refs = (recv_ref, refs) if opening else (refs[0], refs[1:])
        applied_ref, gram_ref, scaled_ref, out_hbm, first_ref, second_ref, table, picked_ref, sem = refs
    blocks, per_row, side, _ = tiles_ref.shape
    vectors = own_ref.shape[1]
    group = place_ref[0]
    slot = 0
    for b in range(blocks):
        split_into(own_ref[b], table, slot)
        slot += 1
    if opening:
        peers = recv_ref.shape[0]
        for p in range(peers):
            for c in range(SLOTS):
                at = jnp.clip(want_ref[c, p] - (group * peers + p) * blocks, 0, blocks - 1)
                split_into(recv_ref[p, at], table, slot)
                slot += 1
    else:
        for n in range(recv_ref.shape[0]):
            split_into(recv_ref[n], table, slot)
            slot += 1
    odd = group % 2 == 1
    for a_ref, b_ref in ((swapped_ref, swapped_next_ref), (swapped_next_ref, swapped_ref)):
        for h in range(RIM):
            split_into(jnp.where(odd, a_ref[h], b_ref[h]), table, slot)
            slot += 1
    table[slot] = jnp.zeros(table.shape[1:], table.dtype)
    rows = []
    for b in range(blocks):
        picked = []
        for s in range(per_row):
            at = jnp.where(s < count_ref[b], cols_ref[b, s], slot)
            picked.append(table[at])
        x = jnp.concatenate(picked, axis=1)
        loads[b].wait()
        t = jnp.concatenate([tiles_ref[b, s] for s in range(per_row)], axis=1)
        product = lax.dot_general(x, t, NT, preferred_element_type=jnp.float32)
        total = product[(PIECES - 1) * vectors :]
        for piece in range(PIECES - 2, -1, -1):
            total = total + product[piece * vectors : (piece + 1) * vectors]
        root = root_ref[b]
        row = total * root
        applied_ref[b] = row
        rows.append(row)
        if not last:
            scaled_ref[b] = row * root
    if not last:
        pick_into(place_ref[1], asked_ref, scaled_ref, picked_ref)
        send = pltpu.make_async_copy(picked_ref, out_hbm, sem)
        send.start()
        swaps_into(group, blocks, scaled_ref, first_ref, second_ref)
    flat = jnp.concatenate(rows, axis=1)
    gram = lax.dot_general(flat, flat, NT, precision=HIGH, preferred_element_type=jnp.float32)
    if last:
        packed_ref[0] = pack_grams([ref[...] for ref in before] + [gram])
        sends = [
            pltpu.make_async_copy(packed_ref, gram_hbm.at[pl.ds(n, 1)], sems.at[n])
            for n in range(gram_hbm.shape[0])
        ]
        for send in sends:
            send.start()
        for send in sends:
            send.wait()
    else:
        gram_ref[...] = gram
        send.wait()


def finish_kernel(row_total, grams_ref, *refs):
    applied_refs, (out_hbm, trust_ref, out_ref, sems) = refs[:ITERS], refs[ITERS:]
    devices = grams_ref.shape[0]
    blocks, vectors = out_ref.shape[1:3]
    sends = [pltpu.make_async_copy(out_ref.at[t], out_hbm.at[t], sems.at[t]) for t in range(ITERS)]
    total = grams_ref[0]
    for n in range(1, devices):
        total = total + grams_ref[n]
    rows = lax.broadcasted_iota(jnp.int32, (vectors, vectors), 0)
    lanes = lax.broadcasted_iota(jnp.int32, (vectors, vectors), 1)
    unit = (rows == lanes).astype(jnp.float32)
    row_at = lax.broadcasted_iota(jnp.int32, (vectors, 1), 0)
    grams = unpack_grams(total, vectors)
    work = [jnp.concatenate([gram, unit], axis=1) for gram in grams]
    for j in range(vectors):
        for t in range(ITERS):
            m = work[t]
            ratio = jnp.where(row_at > j, m[:, j : j + 1] / m[j : j + 1, j : j + 1], 0.0)
            work[t] = m - ratio * m[j : j + 1, :]
    good = jnp.bool_(True)
    for t in range(ITERS):
        m = work[t]
        pivots = jnp.sum(m[:, :vectors] * unit, axis=1, keepdims=True)
        inverse = m[:, vectors:] * lax.rsqrt(pivots / row_total)
        squares = jnp.sum(grams[t] * unit, axis=0, keepdims=True)
        norm = jnp.sum(inverse * inverse * squares) / row_total
        good = good & (norm < TRUST) & (jnp.min(squares) > TINY)
        for b in range(blocks):
            out_ref[t, b] = lax.dot_general(
                inverse, applied_refs[t][b], (((1,), (0,)), ((), ())), precision=HIGH,
                preferred_element_type=jnp.float32,
            )
        sends[t].start()
    trust_ref[0] = good.astype(jnp.int32)
    for send in sends:
        send.wait()


def neighbours(scaled):
    count, blocks = lax.axis_size("group"), scaled.shape[0]
    up = [(i, i + 1) for i in range(count - 1)]
    down = [(i + 1, i) for i in range(count - 1)]
    low = lax.ppermute(scaled[blocks - RIM :], "group", up)
    high = lax.ppermute(scaled[:RIM], "group", down)
    return low, high


def swap(first, second):
    count = lax.axis_size("group")
    ups = [[(i, i + 1) for i in range(start, count - 1, 2)] for start in (0, 1)]
    pairs = [up + [(j, i) for i, j in up] for up in ups]
    return [lax.ppermute(x, "group", pair) for x, pair in zip((first, second), pairs)]


def stepwise(start_basis, tiles, tile_cols, tile_count, recv_list):
    groups, peers = lax.axis_size("group"), lax.axis_size("row")
    blocks, per_row, side, _ = tiles.shape
    vectors = start_basis.shape[1]
    row_total = groups * peers * blocks * side
    live = jnp.arange(per_row, dtype=jnp.int32)[None, :] < tile_count[:, None]
    live = live.astype(jnp.float32)
    wide = tiles.astype(jnp.float32)
    sums = jnp.einsum("btij,bt->bi", wide * wide, live, precision=HIGH)
    root = (1e-06 + sums) ** (-0.25)
    wanted = recv_list.reshape(peers * SLOTS)
    take = jnp.clip(wanted - lax.axis_index("group") * peers * blocks, 0, peers * blocks - 1)
    basis, results = start_basis, []
    for _ in range(ITERS):
        scaled = basis * root[:, None, :]
        low, high = neighbours(scaled)
        received = jnp.take(lax.all_gather(scaled, "row", axis=0, tiled=True), take, axis=0)
        extended = jnp.concatenate([scaled, received, low, high], axis=0)
        picked = jnp.take(extended, tile_cols, axis=0) * live[:, :, None, None]
        product = jnp.einsum(
            "btij,btkj->bki", tiles, picked, precision=HIGH, preferred_element_type=jnp.float32
        )
        applied = product * root[:, None, :]
        gram = jnp.einsum("bki,bli->kl", applied, applied, precision=HIGH)
        factor = jnp.linalg.cholesky(lax.psum(gram, ("group", "row")) / row_total)
        inverse = lax.linalg.triangular_solve(
            factor, jnp.eye(vectors, dtype=jnp.float32), left_side=True, lower=True
        )
        basis = jnp.einsum("kl,bli->bki", inverse, applied, precision=HIGH)
        results.append(basis)
    return jnp.stack(results)


def local(start_basis, tiles, tile_cols, tile_count, recv_list):
    groups, peers = lax.axis_size("group"), lax.axis_size("row")
    blocks, per_row, side, _ = tiles.shape
    vectors = start_basis.shape[1]
    place = jnp.stack([lax.axis_index("group"), lax.axis_index("row")]).astype(jnp.int32)
    wanted = jnp.transpose(recv_list.reshape(peers, SLOTS))
    lists = pl.cdiv(peers * SLOTS, vectors)
    tile_bytes = tiles.size * 2
    far_tiles = pltpu.with_memory_space_constraint(tiles, pltpu.HBM)
    block_shape = (vectors, side)
    picked_shape = (peers * SLOTS,) + block_shape
    rim_shape = f32(RIM, *block_shape)
    root, scaled, *rims = pl.pallas_call(
        roots_kernel,
        out_shape=(
            f32(blocks, 1, side),
            f32(blocks + lists, *block_shape),
            rim_shape,
            rim_shape,
        ),
        in_specs=[smem(), smem(), smem(), hbm(), vmem()],
        out_specs=(vmem(),) * 4,
        scratch_shapes=stream_scratch(tiles),
        compiler_params=params(),
        cost_estimate=cost(tiles.size * 2, tile_bytes),
        name="roots",
    )(place, tile_count, wanted, far_tiles, start_basis)
    slots = blocks + peers * SLOTS + 2 * RIM
    powers, grams = [], []
    for t in range(ITERS):
        last = t == ITERS - 1
        if t == 0:
            swapped = swap(*rims)
            received = asked = lax.all_gather(scaled, "row", axis=0)
        else:
            received = lax.all_to_all(outgoing, "row", 0, 0, tiled=True)
            swapped = swap(*rims)
        scalars = [place, tile_count, tile_cols] + ([wanted] if t == 0 else [])
        arrays = [far_tiles, root, scaled, received, *swapped]
        shapes = [f32(blocks, *block_shape)]
        specs = [vmem(), vmem()]
        scratch = [pltpu.VMEM((slots + 1, PIECES * vectors, side), jnp.bfloat16)]
        if last:
            shapes += [pltpu.HBM((groups * peers, vectors // 2, LANES), jnp.float32)]
            specs = [vmem(), hbm()]
            scratch += [pltpu.VMEM((1, vectors // 2, LANES), jnp.float32), pltpu.SemaphoreType.DMA((groups * peers,))]
            arrays += grams
        else:
            shapes += [f32(vectors, vectors), f32(blocks, *block_shape), pltpu.HBM(picked_shape, jnp.float32)]
            shapes += [rim_shape] * 2
            specs += [vmem(), hbm(), vmem(), vmem()]
            scratch += [pltpu.VMEM(picked_shape, jnp.float32), pltpu.SemaphoreType.DMA]
            arrays += [asked] if t else []
        result = pl.pallas_call(
            functools.partial(apply_kernel, t),
            out_shape=tuple(shapes),
            in_specs=[smem()] * len(scalars) + [hbm()] + [vmem()] * (len(arrays) - 1),
            out_specs=tuple(specs),
            scratch_shapes=scratch + stream_scratch(tiles),
            compiler_params=params(),
            cost_estimate=cost(tiles.size * 2 * vectors * PIECES, tile_bytes),
            name="apply_last" if last else "apply",
        )(*scalars, *arrays)
        powers.append(result[0])
        grams.append(result[1])
        if not last:
            scaled, outgoing, *rims = result[2:]
    gathered = lax.all_to_all(grams[-1], ("group", "row"), 0, 0, tiled=True)
    krylov, trust = pl.pallas_call(
        functools.partial(finish_kernel, float(groups * peers * blocks * side)),
        out_shape=(pltpu.HBM((ITERS, blocks, vectors, side), jnp.float32), jax.ShapeDtypeStruct((1,), jnp.int32)),
        in_specs=[vmem()] * (1 + ITERS),
        out_specs=(hbm(), smem()),
        scratch_shapes=[
            pltpu.VMEM((ITERS, blocks, vectors, side), jnp.float32),
            pltpu.SemaphoreType.DMA((ITERS,)),
        ],
        compiler_params=params(),
        name="finish",
    )(gathered, *powers)
    return lax.cond(
        trust[0] > 0,
        lambda *_: krylov,
        stepwise,
        start_basis, tiles, tile_cols, tile_count, recv_list,
    )


def solution(mesh):
    placed = (
        P(("group", "row"), None, None),
        P(("group", "row"), None, None, None),
        P(("group", "row"), None),
        P(("group", "row")),
        P("group", "row", None, None),
    )
    return jax.shard_map(
        local,
        mesh=mesh,
        in_specs=placed,
        out_specs=P(None, ("group", "row"), None, None),
        check_vma=False,
    )
```

```python
import functools

import jax
import jax.numpy as jnp
from jax import lax
from jax.experimental import pallas as pl
from jax.experimental.pallas import tpu as pltpu
from jax.sharding import PartitionSpec as P

SLOTS = 2
RIM = 2
ITERS = 3
MINLIVE = 10
LANES = 128
HELD_BYTES = 5 * 1024 * 1024 // 2
PIECES = 2
VMEM_BYTES = 24 * 1024 * 1024
TRUST = 64.0
TINY = 1e-25

HIGH = lax.Precision.HIGHEST
NT = (((1,), (1,)), ((), ()))


def vmem():
    return pl.BlockSpec(memory_space=pltpu.VMEM)


def smem():
    return pl.BlockSpec(memory_space=pltpu.SMEM)


def hbm():
    return pl.BlockSpec(memory_space=pltpu.HBM)


def f32(*shape):
    return jax.ShapeDtypeStruct(shape, jnp.float32)


def params():
    return pltpu.CompilerParams(vmem_limit_bytes=VMEM_BYTES)


def cost(flops, moved):
    return pl.CostEstimate(flops=flops, bytes_accessed=moved, transcendentals=0)


def held_blocks(tiles):
    return min(tiles.shape[0] - 1, HELD_BYTES // (tiles.size // tiles.shape[0] * 2))


def load(tiles_hbm, start, tiles_ref, sem):
    copy = pltpu.make_async_copy(tiles_hbm.at[pl.ds(start, tiles_ref.shape[0])], tiles_ref, sem)
    copy.start()
    return copy


def roots_kernel(place_ref, count_ref, want_ref, tiles_hbm, basis_ref, root_ref, sent_ref,
                 first_ref, second_ref, held_ref, rest_ref, sems):
    held, per_row, side, _ = held_ref.shape
    blocks = held + rest_ref.shape[0]
    peers = want_ref.shape[1]
    vectors = basis_ref.shape[1]
    rest_load = load(tiles_hbm, held, rest_ref, sems.at[0])
    held_load = load(tiles_hbm, 0, held_ref, sems.at[1])
    for p in range(peers):
        owned = (place_ref[0] * peers + p) * blocks
        for c in range(SLOTS):
            at = jnp.full((1, side), want_ref[c, p] - owned, jnp.int32).astype(jnp.float32)
            block, row = divmod(p * SLOTS + c, vectors)
            sent_ref[blocks + block, row : row + 1] = at
    rest_load.wait()
    for b in list(range(held, blocks)) + list(range(held)):
        if b == 0:
            held_load.wait()
        tile_ref = held_ref.at[b] if b < held else rest_ref.at[b - held]
        total = jnp.zeros((side, side), jnp.float32)
        for s in range(per_row):
            wide = tile_ref[s].astype(jnp.float32)
            square = wide * wide
            if s >= MINLIVE:
                square = square * (s < count_ref[b]).astype(jnp.float32)
            total = total + square
        sums = jnp.sum(total.T, axis=0, keepdims=True)
        root = lax.rsqrt(jnp.sqrt(1e-06 + sums))
        root_ref[b] = root
        sent_ref[b] = basis_ref[b] * root
    swaps_into(place_ref[0], blocks, sent_ref, first_ref, second_ref)


def swaps_into(group, blocks, scaled_ref, first_ref, second_ref):
    odd = group % 2
    for h in range(RIM):
        first_ref[h] = scaled_ref[(1 - odd) * (blocks - RIM) + h]
        second_ref[h] = scaled_ref[odd * (blocks - RIM) + h]


def pick_into(asked_ref, scaled_ref, out_ref):
    blocks, vectors, side = scaled_ref.shape
    for n in range(asked_ref.shape[0]):
        at = jnp.broadcast_to(asked_ref[n : n + 1], (vectors, side))
        value = scaled_ref[0]
        for b in range(1, blocks):
            value = jnp.where(at == float(b), scaled_ref[b], value)
        out_ref[n] = value


def split_into(x, out_ref, slot):
    vectors = x.shape[0]
    rest = x
    for piece in range(PIECES):
        part = rest.astype(jnp.bfloat16)
        out_ref[slot, pl.ds(piece * vectors, vectors)] = part
        if piece < PIECES - 1:
            rest = rest - part.astype(jnp.float32)


def pack_grams(grams):
    half = grams[0].shape[0] // 2
    parts = [g[:half] for g in grams] + [g[half:] for g in grams]
    spare = LANES - len(parts) * grams[0].shape[1]
    return jnp.concatenate(parts + [jnp.zeros((half, spare), jnp.float32)], axis=1)


def unpack_grams(packed, vectors):
    upper = [packed[:, t * vectors : (t + 1) * vectors] for t in range(ITERS)]
    lower = [packed[:, (ITERS + t) * vectors : (ITERS + t + 1) * vectors] for t in range(ITERS)]
    return [jnp.concatenate(pair, axis=0) for pair in zip(upper, lower)]


def apply_kernel(step_at, *refs):
    last, opening = step_at == ITERS - 1, step_at == 0
    place_ref, count_ref, cols_ref, *refs = refs
    if opening:
        want_ref, *refs = refs
    tiles_hbm, held_ref, root_ref, own_ref, recv_ref, swapped_ref, swapped_next_ref, *refs = refs
    *refs, table, rest_ref, load_sem = refs
    held, per_row, side, _ = held_ref.shape
    blocks = held + rest_ref.shape[0]
    rest_load = load(tiles_hbm, held, rest_ref, load_sem)
    if last:
        *before, applied_ref, gram_hbm, packed_ref, sems = refs
    else:
        if not opening:
            asked_ref, *refs = refs
        applied_ref, gram_ref, scaled_ref, out_hbm, first_ref, second_ref, *refs = refs
        if opening:
            asked_ref, *refs = refs
        picked_ref, sem = refs
    vectors = own_ref.shape[1]
    group = place_ref[0]
    slot = 0
    for b in range(blocks):
        split_into(own_ref[b], table, slot)
        slot += 1
    if opening:
        peers = recv_ref.shape[0]
        for p in range(peers):
            for c in range(SLOTS):
                at = jnp.clip(want_ref[c, p] - (group * peers + p) * blocks, 0, blocks - 1)
                split_into(recv_ref[p, at], table, slot)
                slot += 1
                entry = place_ref[1] * SLOTS + c
                asked_ref[p * SLOTS + c : p * SLOTS + c + 1] = recv_ref[
                    p, blocks + entry // vectors, pl.ds(entry % vectors, 1)
                ]
    else:
        for n in range(recv_ref.shape[0]):
            split_into(recv_ref[n], table, slot)
            slot += 1
    odd = group % 2 == 1
    for a_ref, b_ref in ((swapped_ref, swapped_next_ref), (swapped_next_ref, swapped_ref)):
        for h in range(RIM):
            split_into(jnp.where(odd, a_ref[h], b_ref[h]), table, slot)
            slot += 1
    table[slot] = jnp.zeros(table.shape[1:], table.dtype)
    rows = []
    for b in range(blocks):
        picked = []
        for s in range(per_row):
            at = jnp.where(s < count_ref[b], cols_ref[b, s], slot)
            picked.append(table[at])
        x = jnp.concatenate(picked, axis=1)
        if b == held:
            rest_load.wait()
        tile_ref = held_ref.at[b] if b < held else rest_ref.at[b - held]
        t = jnp.concatenate([tile_ref[s] for s in range(per_row)], axis=1)
        product = lax.dot_general(x, t, NT, preferred_element_type=jnp.float32)
        total = product[(PIECES - 1) * vectors :]
        for piece in range(PIECES - 2, -1, -1):
            total = total + product[piece * vectors : (piece + 1) * vectors]
        root = root_ref[b]
        row = total * root
        applied_ref[b] = row
        rows.append(row)
        if not last:
            scaled_ref[b] = row * root
    if not last:
        pick_into(asked_ref, scaled_ref, picked_ref)
        send = pltpu.make_async_copy(picked_ref, out_hbm, sem)
        send.start()
        swaps_into(group, blocks, scaled_ref, first_ref, second_ref)
    flat = jnp.concatenate(rows, axis=1)
    gram = lax.dot_general(flat, flat, NT, precision=HIGH, preferred_element_type=jnp.float32)
    if last:
        packed_ref[0] = pack_grams([ref[...] for ref in before] + [gram])
        sends = [
            pltpu.make_async_copy(packed_ref, gram_hbm.at[pl.ds(n, 1)], sems.at[n])
            for n in range(gram_hbm.shape[0])
        ]
        for send in sends:
            send.start()
        for send in sends:
            send.wait()
    else:
        gram_ref[...] = gram
        send.wait()


def finish_kernel(row_total, grams_ref, *refs):
    applied_refs, (out_hbm, trust_ref, out_ref, sems) = refs[:ITERS], refs[ITERS:]
    devices = grams_ref.shape[0]
    blocks, vectors = out_ref.shape[1:3]
    sends = [pltpu.make_async_copy(out_ref.at[t], out_hbm.at[t], sems.at[t]) for t in range(ITERS)]
    total = grams_ref[0]
    for n in range(1, devices):
        total = total + grams_ref[n]
    rows = lax.broadcasted_iota(jnp.int32, (vectors, vectors), 0)
    lanes = lax.broadcasted_iota(jnp.int32, (vectors, vectors), 1)
    unit = (rows == lanes).astype(jnp.float32)
    row_at = lax.broadcasted_iota(jnp.int32, (vectors, 1), 0)
    grams = unpack_grams(total, vectors)
    work = [jnp.concatenate([gram, unit], axis=1) for gram in grams]
    for j in range(vectors):
        for t in range(ITERS):
            m = work[t]
            ratio = jnp.where(row_at > j, m[:, j : j + 1] / m[j : j + 1, j : j + 1], 0.0)
            work[t] = m - ratio * m[j : j + 1, :]
    good = jnp.bool_(True)
    for t in range(ITERS):
        m = work[t]
        pivots = jnp.sum(m[:, :vectors] * unit, axis=1, keepdims=True)
        inverse = m[:, vectors:] * lax.rsqrt(pivots / row_total)
        squares = jnp.sum(grams[t] * unit, axis=0, keepdims=True)
        norm = jnp.sum(inverse * inverse * squares) / row_total
        good = good & (norm < TRUST) & (jnp.min(squares) > TINY)
        for b in range(blocks):
            out_ref[t, b] = lax.dot_general(
                inverse, applied_refs[t][b], (((1,), (0,)), ((), ())), precision=HIGH,
                preferred_element_type=jnp.float32,
            )
        sends[t].start()
    trust_ref[0] = good.astype(jnp.int32)
    for send in sends:
        send.wait()


def neighbours(scaled):
    count, blocks = lax.axis_size("group"), scaled.shape[0]
    up = [(i, i + 1) for i in range(count - 1)]
    down = [(i + 1, i) for i in range(count - 1)]
    low = lax.ppermute(scaled[blocks - RIM :], "group", up)
    high = lax.ppermute(scaled[:RIM], "group", down)
    return low, high


def swap(first, second):
    count = lax.axis_size("group")
    ups = [[(i, i + 1) for i in range(start, count - 1, 2)] for start in (0, 1)]
    pairs = [up + [(j, i) for i, j in up] for up in ups]
    return [lax.ppermute(x, "group", pair) for x, pair in zip((first, second), pairs)]


def stepwise(start_basis, tiles, tile_cols, tile_count, recv_list):
    groups, peers = lax.axis_size("group"), lax.axis_size("row")
    blocks, per_row, side, _ = tiles.shape
    vectors = start_basis.shape[1]
    row_total = groups * peers * blocks * side
    live = jnp.arange(per_row, dtype=jnp.int32)[None, :] < tile_count[:, None]
    live = live.astype(jnp.float32)
    wide = tiles.astype(jnp.float32)
    sums = jnp.einsum("btij,bt->bi", wide * wide, live, precision=HIGH)
    root = (1e-06 + sums) ** (-0.25)
    wanted = recv_list.reshape(peers * SLOTS)
    take = jnp.clip(wanted - lax.axis_index("group") * peers * blocks, 0, peers * blocks - 1)
    basis, results = start_basis, []
    for _ in range(ITERS):
        scaled = basis * root[:, None, :]
        low, high = neighbours(scaled)
        received = jnp.take(lax.all_gather(scaled, "row", axis=0, tiled=True), take, axis=0)
        extended = jnp.concatenate([scaled, received, low, high], axis=0)
        picked = jnp.take(extended, tile_cols, axis=0) * live[:, :, None, None]
        product = jnp.einsum(
            "btij,btkj->bki", tiles, picked, precision=HIGH, preferred_element_type=jnp.float32
        )
        applied = product * root[:, None, :]
        gram = jnp.einsum("bki,bli->kl", applied, applied, precision=HIGH)
        factor = jnp.linalg.cholesky(lax.psum(gram, ("group", "row")) / row_total)
        inverse = lax.linalg.triangular_solve(
            factor, jnp.eye(vectors, dtype=jnp.float32), left_side=True, lower=True
        )
        basis = jnp.einsum("kl,bli->bki", inverse, applied, precision=HIGH)
        results.append(basis)
    return jnp.stack(results)


def local(start_basis, tiles, tile_cols, tile_count, recv_list):
    groups, peers = lax.axis_size("group"), lax.axis_size("row")
    blocks, per_row, side, _ = tiles.shape
    vectors = start_basis.shape[1]
    place = jnp.stack([lax.axis_index("group"), lax.axis_index("row")]).astype(jnp.int32)
    wanted = jnp.transpose(recv_list.reshape(peers, SLOTS))
    lists = pl.cdiv(peers * SLOTS, vectors)
    tile_bytes = tiles.size * 2
    far_tiles = pltpu.with_memory_space_constraint(tiles, pltpu.HBM)
    block_shape = (vectors, side)
    picked_shape = (peers * SLOTS,) + block_shape
    rim_shape = f32(RIM, *block_shape)
    kept = held_blocks(tiles)
    rest = pltpu.VMEM((blocks - kept,) + tiles.shape[1:], tiles.dtype)
    root, scaled, *rims, held = pl.pallas_call(
        roots_kernel,
        out_shape=(
            f32(blocks, 1, side),
            f32(blocks + lists, *block_shape),
            rim_shape,
            rim_shape,
            pltpu.VMEM((kept,) + tiles.shape[1:], tiles.dtype),
        ),
        in_specs=[smem(), smem(), smem(), hbm(), vmem()],
        out_specs=(vmem(),) * 5,
        scratch_shapes=[rest, pltpu.SemaphoreType.DMA((2,))],
        compiler_params=params(),
        cost_estimate=cost(tiles.size * 2, tile_bytes),
        name="roots",
    )(place, tile_count, wanted, far_tiles, start_basis)
    slots = blocks + peers * SLOTS + 2 * RIM
    powers, grams = [], []
    for t in range(ITERS):
        last = t == ITERS - 1
        if t == 0:
            swapped = swap(*rims)
            received = lax.all_gather(scaled, "row", axis=0)
        else:
            received = lax.all_to_all(outgoing, "row", 0, 0, tiled=True)
            swapped = swap(*rims)
        scalars = [place, tile_count, tile_cols] + ([wanted] if t == 0 else [])
        arrays = [far_tiles, held, root, scaled, received, *swapped]
        shapes = [f32(blocks, *block_shape)]
        specs = [vmem(), vmem()]
        if last:
            shapes += [pltpu.HBM((groups * peers, vectors // 2, LANES), jnp.float32)]
            specs = [vmem(), hbm()]
            scratch = [pltpu.VMEM((1, vectors // 2, LANES), jnp.float32), pltpu.SemaphoreType.DMA((groups * peers,))]
            arrays += grams
        else:
            shapes += [f32(vectors, vectors), f32(blocks, *block_shape), pltpu.HBM(picked_shape, jnp.float32)]
            shapes += [rim_shape] * 2
            specs += [vmem(), hbm(), vmem(), vmem()]
            scratch = [pltpu.VMEM(picked_shape, jnp.float32), pltpu.SemaphoreType.DMA]
            if t:
                arrays += [asked]
            else:
                shapes += [f32(peers * SLOTS, side)]
                specs += [vmem()]
        result = pl.pallas_call(
            functools.partial(apply_kernel, t),
            out_shape=tuple(shapes),
            in_specs=[smem()] * len(scalars) + [hbm()] + [vmem()] * (len(arrays) - 1),
            out_specs=tuple(specs),
            scratch_shapes=scratch
            + [
                pltpu.VMEM((slots + 1, PIECES * vectors, side), jnp.bfloat16),
                rest,
                pltpu.SemaphoreType.DMA,
            ],
            compiler_params=params(),
            cost_estimate=cost(tiles.size * 2 * vectors * PIECES, tile_bytes),
            name="apply_last" if last else "apply",
        )(*scalars, *arrays)
        powers.append(result[0])
        grams.append(result[1])
        if not last:
            scaled, outgoing, *rims = result[2:6]
            if t == 0:
                asked = result[6]
    gathered = lax.all_to_all(grams[-1], ("group", "row"), 0, 0, tiled=True)
    krylov, trust = pl.pallas_call(
        functools.partial(finish_kernel, float(groups * peers * blocks * side)),
        out_shape=(pltpu.HBM((ITERS, blocks, vectors, side), jnp.float32), jax.ShapeDtypeStruct((1,), jnp.int32)),
        in_specs=[vmem()] * (1 + ITERS),
        out_specs=(hbm(), smem()),
        scratch_shapes=[
            pltpu.VMEM((ITERS, blocks, vectors, side), jnp.float32),
            pltpu.SemaphoreType.DMA((ITERS,)),
        ],
        compiler_params=params(),
        name="finish",
    )(gathered, *powers)
    return lax.cond(
        trust[0] > 0,
        lambda *_: krylov,
        stepwise,
        start_basis, tiles, tile_cols, tile_count, recv_list,
    )


def solution(mesh):
    placed = (
        P(("group", "row"), None, None),
        P(("group", "row"), None, None, None),
        P(("group", "row"), None),
        P(("group", "row")),
        P("group", "row", None, None),
    )
    return jax.shard_map(
        local,
        mesh=mesh,
        in_specs=placed,
        out_specs=P(None, ("group", "row"), None, None),
        check_vma=False,
    )
```

```python
import functools

import jax
import jax.numpy as jnp
from jax import lax
from jax.experimental import pallas as pl
from jax.experimental.pallas import tpu as pltpu
from jax.sharding import PartitionSpec as P

SLOTS = 2
RIM = 2
ITERS = 3
MINLIVE = 10
LANES = 128
HELD_BYTES = 5 * 1024 * 1024 // 2
PIECES = 2
VMEM_BYTES = 24 * 1024 * 1024
TRUST = 64.0
TINY = 1e-25

HIGH = lax.Precision.HIGHEST
NT = (((1,), (1,)), ((), ()))


def vmem():
    return pl.BlockSpec(memory_space=pltpu.VMEM)


def smem():
    return pl.BlockSpec(memory_space=pltpu.SMEM)


def hbm():
    return pl.BlockSpec(memory_space=pltpu.HBM)


def far(x):
    return pltpu.with_memory_space_constraint(x, pltpu.HBM)


def f32(*shape):
    return jax.ShapeDtypeStruct(shape, jnp.float32)


def params():
    return pltpu.CompilerParams(vmem_limit_bytes=VMEM_BYTES)


def cost(flops, moved):
    return pl.CostEstimate(flops=flops, bytes_accessed=moved, transcendentals=0)


def held_blocks(tiles):
    return min(tiles.shape[0] - 1, HELD_BYTES // (tiles.size // tiles.shape[0] * 2))


def load(tiles_hbm, start, tiles_ref, sem):
    copy = pltpu.make_async_copy(tiles_hbm.at[pl.ds(start, tiles_ref.shape[0])], tiles_ref, sem)
    copy.start()
    return copy


def roots_kernel(place_ref, count_hbm, want_hbm, tiles_hbm, basis_hbm, root_ref, sent_ref,
                 first_ref, second_ref, held_ref, rest_ref, count_ref, want_ref, basis_ref, sems):
    held, per_row, side, _ = held_ref.shape
    blocks = held + rest_ref.shape[0]
    peers = want_ref.shape[1]
    vectors = basis_ref.shape[1]
    rest_load = load(tiles_hbm, held, rest_ref, sems.at[0])
    small = [
        pltpu.make_async_copy(source, target, sems.at[2 + n])
        for n, (source, target) in enumerate(
            ((count_hbm, count_ref), (want_hbm, want_ref), (basis_hbm, basis_ref))
        )
    ]
    for copy in small:
        copy.start()
    held_load = load(tiles_hbm, 0, held_ref, sems.at[1])
    for copy in small:
        copy.wait()
    for p in range(peers):
        owned = (place_ref[0] * peers + p) * blocks
        for c in range(SLOTS):
            at = jnp.full((1, side), want_ref[c, p] - owned, jnp.int32).astype(jnp.float32)
            block, row = divmod(p * SLOTS + c, vectors)
            sent_ref[blocks + block, row : row + 1] = at
    rest_load.wait()
    for b in list(range(held, blocks)) + list(range(held)):
        if b == 0:
            held_load.wait()
        tile_ref = held_ref.at[b] if b < held else rest_ref.at[b - held]
        total = jnp.zeros((side, side), jnp.float32)
        for s in range(per_row):
            wide = tile_ref[s].astype(jnp.float32)
            square = wide * wide
            if s >= MINLIVE:
                square = square * (s < count_ref[b]).astype(jnp.float32)
            total = total + square
        sums = jnp.sum(total.T, axis=0, keepdims=True)
        root = lax.rsqrt(jnp.sqrt(1e-06 + sums))
        root_ref[b] = root
        sent_ref[b] = basis_ref[b] * root
    swaps_into(place_ref[0], blocks, sent_ref, first_ref, second_ref)


def swaps_into(group, blocks, scaled_ref, first_ref, second_ref):
    odd = group % 2
    for h in range(RIM):
        first_ref[h] = scaled_ref[(1 - odd) * (blocks - RIM) + h]
        second_ref[h] = scaled_ref[odd * (blocks - RIM) + h]


def pick_into(asked_ref, scaled_ref, out_ref):
    blocks, vectors, side = scaled_ref.shape
    for n in range(asked_ref.shape[0]):
        at = jnp.broadcast_to(asked_ref[n : n + 1], (vectors, side))
        value = scaled_ref[0]
        for b in range(1, blocks):
            value = jnp.where(at == float(b), scaled_ref[b], value)
        out_ref[n] = value


def pieces_of(x, count):
    parts = []
    for n in range(count):
        part = x.astype(jnp.bfloat16)
        parts.append(part)
        if n < count - 1:
            x = x - part.astype(jnp.float32)
    return parts


def split_into(x, out_ref, slot):
    vectors = x.shape[0]
    for n, part in enumerate(pieces_of(x, PIECES)):
        out_ref[slot, pl.ds(n * vectors, vectors)] = part


def gram_of(flat):
    k = flat.shape[0]
    stack = jnp.concatenate(pieces_of(flat, 3), axis=0)
    full = lax.dot_general(stack, stack, NT, preferred_element_type=jnp.float32)
    term = lambda i, j: full[i * k : (i + 1) * k, j * k : (j + 1) * k]
    small = term(1, 1) + (term(0, 2) + term(2, 0))
    return term(0, 0) + ((term(0, 1) + term(1, 0)) + small)


TERMS = ((0, 0), (0, 1), (1, 0), (1, 1), (0, 2), (2, 0))


def pack_grams(grams):
    half = grams[0].shape[0] // 2
    parts = [g[:half] for g in grams] + [g[half:] for g in grams]
    spare = LANES - len(parts) * grams[0].shape[1]
    return jnp.concatenate(parts + [jnp.zeros((half, spare), jnp.float32)], axis=1)


def unpack_grams(packed, vectors):
    upper = [packed[:, t * vectors : (t + 1) * vectors] for t in range(ITERS)]
    lower = [packed[:, (ITERS + t) * vectors : (ITERS + t + 1) * vectors] for t in range(ITERS)]
    return [jnp.concatenate(pair, axis=0) for pair in zip(upper, lower)]


def apply_kernel(step_at, *refs):
    last, opening = step_at == ITERS - 1, step_at == 0
    place_ref, count_ref, cols_ref, *refs = refs
    if opening:
        want_ref, *refs = refs
    tiles_hbm, held_ref, root_ref, own_ref, recv_ref, swapped_ref, swapped_next_ref, *refs = refs
    *refs, table, rest_ref, load_sem = refs
    held, per_row, side, _ = held_ref.shape
    blocks = held + rest_ref.shape[0]
    rest_load = load(tiles_hbm, held, rest_ref, load_sem)
    if last:
        *before, applied_ref, gram_hbm, packed_ref, sem = refs
    else:
        if not opening:
            asked_ref, *refs = refs
        applied_ref, gram_ref, scaled_ref, out_hbm, first_ref, second_ref, *refs = refs
        if opening:
            asked_ref, *refs = refs
        picked_ref, sem = refs
    vectors = own_ref.shape[1]
    group = place_ref[0]
    slot = 0
    for b in range(blocks):
        split_into(own_ref[b], table, slot)
        slot += 1
    if opening:
        peers = recv_ref.shape[0]
        for p in range(peers):
            for c in range(SLOTS):
                at = jnp.clip(want_ref[c, p] - (group * peers + p) * blocks, 0, blocks - 1)
                split_into(recv_ref[p, at], table, slot)
                slot += 1
                entry = place_ref[1] * SLOTS + c
                asked_ref[p * SLOTS + c : p * SLOTS + c + 1] = recv_ref[
                    p, blocks + entry // vectors, pl.ds(entry % vectors, 1)
                ]
    else:
        for n in range(recv_ref.shape[0]):
            split_into(recv_ref[n], table, slot)
            slot += 1
    odd = group % 2 == 1
    for a_ref, b_ref in ((swapped_ref, swapped_next_ref), (swapped_next_ref, swapped_ref)):
        for h in range(RIM):
            split_into(jnp.where(odd, a_ref[h], b_ref[h]), table, slot)
            slot += 1
    table[slot] = jnp.zeros(table.shape[1:], table.dtype)
    rows = []
    for b in range(blocks):
        picked = []
        for s in range(per_row):
            at = jnp.where(s < count_ref[b], cols_ref[b, s], slot)
            picked.append(table[at])
        x = jnp.concatenate(picked, axis=1)
        if b == held:
            rest_load.wait()
        tile_ref = held_ref.at[b] if b < held else rest_ref.at[b - held]
        t = jnp.concatenate([tile_ref[s] for s in range(per_row)], axis=1)
        product = lax.dot_general(x, t, NT, preferred_element_type=jnp.float32)
        total = product[(PIECES - 1) * vectors :]
        for piece in range(PIECES - 2, -1, -1):
            total = total + product[piece * vectors : (piece + 1) * vectors]
        root = root_ref[b]
        row = total * root
        applied_ref[b] = row
        rows.append(row)
        if not last:
            scaled_ref[b] = row * root
    if not last:
        pick_into(asked_ref, scaled_ref, picked_ref)
        send = pltpu.make_async_copy(picked_ref, out_hbm, sem)
        send.start()
        swaps_into(group, blocks, scaled_ref, first_ref, second_ref)
    flat = jnp.concatenate(rows, axis=1)
    gram = gram_of(flat)
    if last:
        packed = pack_grams([ref[...] for ref in before] + [gram])
        for n in range(packed_ref.shape[0]):
            packed_ref[n] = packed
        send = pltpu.make_async_copy(packed_ref, gram_hbm, sem)
        send.start()
        send.wait()
    else:
        gram_ref[...] = gram
        send.wait()


def finish_kernel(row_total, grams_ref, *refs):
    applied_refs, (out_hbm, trust_ref, out_ref, sems) = refs[:ITERS], refs[ITERS:]
    devices = grams_ref.shape[0]
    blocks, vectors = out_ref.shape[1:3]
    sends = [pltpu.make_async_copy(out_ref.at[t], out_hbm.at[t], sems.at[t]) for t in range(ITERS)]
    total = grams_ref[0]
    for n in range(1, devices):
        total = total + grams_ref[n]
    rows = lax.broadcasted_iota(jnp.int32, (vectors, vectors), 0)
    lanes = lax.broadcasted_iota(jnp.int32, (vectors, vectors), 1)
    unit = (rows == lanes).astype(jnp.float32)
    row_at = lax.broadcasted_iota(jnp.int32, (vectors, 1), 0)
    grams = unpack_grams(total, vectors)
    work = [jnp.concatenate([gram, unit], axis=1) for gram in grams]
    for j in range(vectors):
        for t in range(ITERS):
            m = work[t]
            ratio = jnp.where(row_at > j, m[:, j : j + 1] / m[j : j + 1, j : j + 1], 0.0)
            work[t] = m - ratio * m[j : j + 1, :]
    good = jnp.bool_(True)
    for t in range(ITERS):
        m = work[t]
        pivots = jnp.sum(m[:, :vectors] * unit, axis=1, keepdims=True)
        inverse = m[:, vectors:] * lax.rsqrt(pivots / row_total)
        squares = jnp.sum(grams[t] * unit, axis=0, keepdims=True)
        norm = jnp.sum(inverse * inverse * squares) / row_total
        good = good & (norm < TRUST) & (jnp.min(squares) > TINY)
        left = [part.astype(jnp.float32) for part in pieces_of(inverse, 3)]
        left = jnp.concatenate([left[i] for i, _ in TERMS], axis=1).astype(jnp.bfloat16)
        for b in range(blocks):
            right = pieces_of(applied_refs[t][b], 3)
            right = jnp.concatenate([right[j] for _, j in TERMS], axis=0)
            out_ref[t, b] = jnp.dot(left, right, preferred_element_type=jnp.float32)
        sends[t].start()
    trust_ref[0] = good.astype(jnp.int32)
    for send in sends:
        send.wait()


def neighbours(scaled):
    count, blocks = lax.axis_size("group"), scaled.shape[0]
    up = [(i, i + 1) for i in range(count - 1)]
    down = [(i + 1, i) for i in range(count - 1)]
    low = lax.ppermute(scaled[blocks - RIM :], "group", up)
    high = lax.ppermute(scaled[:RIM], "group", down)
    return low, high


def swap(first, second):
    count = lax.axis_size("group")
    ups = [[(i, i + 1) for i in range(start, count - 1, 2)] for start in (0, 1)]
    pairs = [up + [(j, i) for i, j in up] for up in ups]
    return [lax.ppermute(x, "group", pair) for x, pair in zip((first, second), pairs)]


def stepwise(start_basis, tiles, tile_cols, tile_count, recv_list):
    groups, peers = lax.axis_size("group"), lax.axis_size("row")
    blocks, per_row, side, _ = tiles.shape
    vectors = start_basis.shape[1]
    row_total = groups * peers * blocks * side
    live = jnp.arange(per_row, dtype=jnp.int32)[None, :] < tile_count[:, None]
    live = live.astype(jnp.float32)
    wide = tiles.astype(jnp.float32)
    sums = jnp.einsum("btij,bt->bi", wide * wide, live, precision=HIGH)
    root = (1e-06 + sums) ** (-0.25)
    wanted = recv_list.reshape(peers * SLOTS)
    take = jnp.clip(wanted - lax.axis_index("group") * peers * blocks, 0, peers * blocks - 1)
    basis, results = start_basis, []
    for _ in range(ITERS):
        scaled = basis * root[:, None, :]
        low, high = neighbours(scaled)
        received = jnp.take(lax.all_gather(scaled, "row", axis=0, tiled=True), take, axis=0)
        extended = jnp.concatenate([scaled, received, low, high], axis=0)
        picked = jnp.take(extended, tile_cols, axis=0) * live[:, :, None, None]
        product = jnp.einsum(
            "btij,btkj->bki", tiles, picked, precision=HIGH, preferred_element_type=jnp.float32
        )
        applied = product * root[:, None, :]
        gram = jnp.einsum("bki,bli->kl", applied, applied, precision=HIGH)
        factor = jnp.linalg.cholesky(lax.psum(gram, ("group", "row")) / row_total)
        inverse = lax.linalg.triangular_solve(
            factor, jnp.eye(vectors, dtype=jnp.float32), left_side=True, lower=True
        )
        basis = jnp.einsum("kl,bli->bki", inverse, applied, precision=HIGH)
        results.append(basis)
    return jnp.stack(results)


def local(start_basis, tiles, tile_cols, tile_count, recv_list):
    groups, peers = lax.axis_size("group"), lax.axis_size("row")
    blocks, per_row, side, _ = tiles.shape
    vectors = start_basis.shape[1]
    place = jnp.stack([lax.axis_index("group"), lax.axis_index("row")]).astype(jnp.int32)
    wanted = jnp.transpose(recv_list.reshape(peers, SLOTS))
    lists = pl.cdiv(peers * SLOTS, vectors)
    tile_bytes = tiles.size * 2
    far_tiles = far(tiles)
    block_shape = (vectors, side)
    picked_shape = (peers * SLOTS,) + block_shape
    rim_shape = f32(RIM, *block_shape)
    kept = held_blocks(tiles)
    rest = pltpu.VMEM((blocks - kept,) + tiles.shape[1:], tiles.dtype)
    root, scaled, *rims, held = pl.pallas_call(
        roots_kernel,
        out_shape=(
            f32(blocks, 1, side),
            f32(blocks + lists, *block_shape),
            rim_shape,
            rim_shape,
            pltpu.VMEM((kept,) + tiles.shape[1:], tiles.dtype),
        ),
        in_specs=[smem()] + [hbm()] * 4,
        out_specs=(vmem(),) * 5,
        scratch_shapes=[
            rest,
            pltpu.SMEM((blocks,), jnp.int32),
            pltpu.SMEM((SLOTS, peers), jnp.int32),
            pltpu.VMEM((blocks,) + block_shape, jnp.float32),
            pltpu.SemaphoreType.DMA((5,)),
        ],
        compiler_params=params(),
        cost_estimate=cost(tiles.size * 2, tile_bytes),
        name="roots",
    )(place, far(tile_count), far(wanted), far_tiles, far(start_basis))
    slots = blocks + peers * SLOTS + 2 * RIM
    powers, grams = [], []
    for t in range(ITERS):
        last = t == ITERS - 1
        if t == 0:
            swapped = swap(*rims)
            received = lax.all_gather(scaled, "row", axis=0)
        else:
            received = lax.all_to_all(outgoing, "row", 0, 0, tiled=True)
            swapped = swap(*rims)
        scalars = [place, tile_count, tile_cols] + ([wanted] if t == 0 else [])
        arrays = [far_tiles, held, root, scaled, received, *swapped]
        shapes = [f32(blocks, *block_shape)]
        specs = [vmem(), vmem()]
        if last:
            shapes += [pltpu.HBM((groups * peers, vectors // 2, LANES), jnp.float32)]
            specs = [vmem(), hbm()]
            scratch = [
                pltpu.VMEM((groups * peers, vectors // 2, LANES), jnp.float32),
                pltpu.SemaphoreType.DMA,
            ]
            arrays += grams
        else:
            shapes += [f32(vectors, vectors), f32(blocks, *block_shape), pltpu.HBM(picked_shape, jnp.float32)]
            shapes += [rim_shape] * 2
            specs += [vmem(), hbm(), vmem(), vmem()]
            scratch = [pltpu.VMEM(picked_shape, jnp.float32), pltpu.SemaphoreType.DMA]
            if t:
                arrays += [asked]
            else:
                shapes += [f32(peers * SLOTS, side)]
                specs += [vmem()]
        result = pl.pallas_call(
            functools.partial(apply_kernel, t),
            out_shape=tuple(shapes),
            in_specs=[smem()] * len(scalars) + [hbm()] + [vmem()] * (len(arrays) - 1),
            out_specs=tuple(specs),
            scratch_shapes=scratch
            + [
                pltpu.VMEM((slots + 1, PIECES * vectors, side), jnp.bfloat16),
                rest,
                pltpu.SemaphoreType.DMA,
            ],
            compiler_params=params(),
            cost_estimate=cost(tiles.size * 2 * vectors * PIECES, tile_bytes),
            name="apply_last" if last else "apply",
        )(*scalars, *arrays)
        powers.append(result[0])
        grams.append(result[1])
        if not last:
            scaled, outgoing, *rims = result[2:6]
            if t == 0:
                asked = result[6]
    gathered = lax.all_to_all(grams[-1], ("group", "row"), 0, 0, tiled=True)
    krylov, trust = pl.pallas_call(
        functools.partial(finish_kernel, float(groups * peers * blocks * side)),
        out_shape=(pltpu.HBM((ITERS, blocks, vectors, side), jnp.float32), jax.ShapeDtypeStruct((1,), jnp.int32)),
        in_specs=[vmem()] * (1 + ITERS),
        out_specs=(hbm(), smem()),
        scratch_shapes=[
            pltpu.VMEM((ITERS, blocks, vectors, side), jnp.float32),
            pltpu.SemaphoreType.DMA((ITERS,)),
        ],
        compiler_params=params(),
        name="finish",
    )(gathered, *powers)
    return lax.cond(
        trust[0] > 0,
        lambda *_: krylov,
        stepwise,
        start_basis, tiles, tile_cols, tile_count, recv_list,
    )


def solution(mesh):
    placed = (
        P(("group", "row"), None, None),
        P(("group", "row"), None, None, None),
        P(("group", "row"), None),
        P(("group", "row")),
        P("group", "row", None, None),
    )
    return jax.shard_map(
        local,
        mesh=mesh,
        in_specs=placed,
        out_specs=P(None, ("group", "row"), None, None),
        check_vma=False,
    )
```

```python
import functools

import jax
import jax.numpy as jnp
from jax import lax
from jax.experimental import pallas as pl
from jax.experimental.pallas import tpu as pltpu
from jax.sharding import PartitionSpec as P

SLOTS = 2
RIM = 2
ITERS = 3
MINLIVE = 10
LANES = 128
HELD_BYTES = 5 * 1024 * 1024 // 2
PIECES = 2
VMEM_BYTES = 24 * 1024 * 1024
TRUST = 64.0
TINY = 1e-25

HIGH = lax.Precision.HIGHEST
NT = (((1,), (1,)), ((), ()))


def vmem():
    return pl.BlockSpec(memory_space=pltpu.VMEM)


def smem():
    return pl.BlockSpec(memory_space=pltpu.SMEM)


def hbm():
    return pl.BlockSpec(memory_space=pltpu.HBM)


def far(x):
    return pltpu.with_memory_space_constraint(x, pltpu.HBM)


def f32(*shape):
    return jax.ShapeDtypeStruct(shape, jnp.float32)


def params():
    return pltpu.CompilerParams(vmem_limit_bytes=VMEM_BYTES)


def cost(flops, moved):
    return pl.CostEstimate(flops=flops, bytes_accessed=moved, transcendentals=0)


def held_blocks(tiles):
    return min(tiles.shape[0] - 1, HELD_BYTES // (tiles.size // tiles.shape[0] * 2))


def load(tiles_hbm, start, tiles_ref, sem):
    copy = pltpu.make_async_copy(tiles_hbm.at[pl.ds(start, tiles_ref.shape[0])], tiles_ref, sem)
    copy.start()
    return copy


def roots_kernel(place_ref, count_hbm, want_hbm, tiles_hbm, basis_hbm, root_ref, sent_ref,
                 first_ref, second_ref, held_ref, rest_ref, count_ref, want_ref, basis_ref, sems):
    held, per_row, side, _ = held_ref.shape
    blocks = held + rest_ref.shape[0]
    peers = want_ref.shape[1]
    vectors = basis_ref.shape[1]
    rest_load = load(tiles_hbm, held, rest_ref, sems.at[0])
    small = [
        pltpu.make_async_copy(source, target, sems.at[2 + n])
        for n, (source, target) in enumerate(
            ((count_hbm, count_ref), (want_hbm, want_ref), (basis_hbm, basis_ref))
        )
    ]
    for copy in small:
        copy.start()
    held_load = load(tiles_hbm, 0, held_ref, sems.at[1])
    for copy in small:
        copy.wait()
    for p in range(peers):
        owned = (place_ref[0] * peers + p) * blocks
        for c in range(SLOTS):
            at = jnp.full((1, side), want_ref[c, p] - owned, jnp.int32).astype(jnp.float32)
            block, row = divmod(p * SLOTS + c, vectors)
            sent_ref[blocks + block, row : row + 1] = at
    rest_load.wait()
    for b in list(range(held, blocks)) + list(range(held)):
        if b == 0:
            held_load.wait()
        tile_ref = held_ref.at[b] if b < held else rest_ref.at[b - held]
        total = jnp.zeros((side, side), jnp.float32)
        for s in range(per_row):
            wide = tile_ref[s].astype(jnp.float32)
            square = wide * wide
            if s >= MINLIVE:
                square = square * (s < count_ref[b]).astype(jnp.float32)
            total = total + square
        sums = jnp.sum(total.T, axis=0, keepdims=True)
        root = lax.rsqrt(jnp.sqrt(1e-06 + sums))
        root_ref[b] = root
        sent_ref[b] = basis_ref[b] * root
    swaps_into(place_ref[0], blocks, sent_ref, first_ref, second_ref)


def swaps_into(group, blocks, scaled_ref, first_ref, second_ref):
    odd = group % 2
    for h in range(RIM):
        first_ref[h] = scaled_ref[(1 - odd) * (blocks - RIM) + h]
        second_ref[h] = scaled_ref[odd * (blocks - RIM) + h]


def pick_into(asked_ref, scaled_ref, out_ref):
    blocks, vectors, side = scaled_ref.shape
    for n in range(asked_ref.shape[0]):
        at = jnp.broadcast_to(asked_ref[n : n + 1], (vectors, side))
        value = scaled_ref[0]
        for b in range(1, blocks):
            value = jnp.where(at == float(b), scaled_ref[b], value)
        out_ref[n] = value


def pieces_of(x, count):
    parts = []
    for n in range(count):
        part = x.astype(jnp.bfloat16)
        parts.append(part)
        if n < count - 1:
            x = x - part.astype(jnp.float32)
    return parts


def split_into(x, out_ref, slot):
    vectors = x.shape[0]
    for n, part in enumerate(pieces_of(x, PIECES)):
        out_ref[slot, pl.ds(n * vectors, vectors)] = part


def gram_of(flat):
    k = flat.shape[0]
    stack = jnp.concatenate(pieces_of(flat, 3), axis=0)
    full = lax.dot_general(stack, stack, NT, preferred_element_type=jnp.float32)
    term = lambda i, j: full[i * k : (i + 1) * k, j * k : (j + 1) * k]
    small = term(1, 1) + (term(0, 2) + term(2, 0))
    return term(0, 0) + ((term(0, 1) + term(1, 0)) + small)


TERMS = ((0, 0), (0, 1), (1, 0), (1, 1), (0, 2), (2, 0))


def pack_grams(grams):
    half = grams[0].shape[0] // 2
    parts = [g[:half] for g in grams] + [g[half:] for g in grams]
    spare = LANES - len(parts) * grams[0].shape[1]
    return jnp.concatenate(parts + [jnp.zeros((half, spare), jnp.float32)], axis=1)


def unpack_grams(packed, vectors):
    upper = [packed[:, t * vectors : (t + 1) * vectors] for t in range(ITERS)]
    lower = [packed[:, (ITERS + t) * vectors : (ITERS + t + 1) * vectors] for t in range(ITERS)]
    return [jnp.concatenate(pair, axis=0) for pair in zip(upper, lower)]


def apply_kernel(step_at, *refs):
    last, opening = step_at == ITERS - 1, step_at == 0
    place_ref, count_ref, cols_ref, *refs = refs
    if opening:
        want_ref, *refs = refs
    tiles_hbm, held_ref, root_ref, own_ref, recv_ref, swapped_ref, swapped_next_ref, *refs = refs
    *refs, table, rest_ref, load_sem = refs
    held, per_row, side, _ = held_ref.shape
    blocks = held + rest_ref.shape[0]
    rest_load = load(tiles_hbm, held, rest_ref, load_sem)
    if last:
        *before, applied_ref, gram_ref = refs
    else:
        if not opening:
            asked_ref, *refs = refs
        applied_ref, gram_ref, scaled_ref, out_ref, first_ref, second_ref, *refs = refs
        if opening:
            (asked_ref,) = refs
    vectors = own_ref.shape[1]
    group = place_ref[0]
    slot = 0
    for b in range(blocks):
        split_into(own_ref[b], table, slot)
        slot += 1
    if opening:
        peers = recv_ref.shape[0]
        for p in range(peers):
            for c in range(SLOTS):
                at = jnp.clip(want_ref[c, p] - (group * peers + p) * blocks, 0, blocks - 1)
                split_into(recv_ref[p, at], table, slot)
                slot += 1
                entry = place_ref[1] * SLOTS + c
                asked_ref[p * SLOTS + c : p * SLOTS + c + 1] = recv_ref[
                    p, blocks + entry // vectors, pl.ds(entry % vectors, 1)
                ]
    else:
        for n in range(recv_ref.shape[0]):
            split_into(recv_ref[n], table, slot)
            slot += 1
    odd = group % 2 == 1
    for a_ref, b_ref in ((swapped_ref, swapped_next_ref), (swapped_next_ref, swapped_ref)):
        for h in range(RIM):
            split_into(jnp.where(odd, a_ref[h], b_ref[h]), table, slot)
            slot += 1
    table[slot] = jnp.zeros(table.shape[1:], table.dtype)
    rest_load.wait()
    rows = []
    for b in range(blocks):
        picked = []
        for s in range(per_row):
            at = jnp.where(s < count_ref[b], cols_ref[b, s], slot)
            picked.append(table[at])
        x = jnp.concatenate(picked, axis=1)
        tile_ref = held_ref.at[b] if b < held else rest_ref.at[b - held]
        t = jnp.concatenate([tile_ref[s] for s in range(per_row)], axis=1)
        product = lax.dot_general(x, t, NT, preferred_element_type=jnp.float32)
        total = product[(PIECES - 1) * vectors :]
        for piece in range(PIECES - 2, -1, -1):
            total = total + product[piece * vectors : (piece + 1) * vectors]
        root = root_ref[b]
        row = total * root
        applied_ref[b] = row
        rows.append(row)
        if not last:
            scaled_ref[b] = row * root
    if not last:
        pick_into(asked_ref, scaled_ref, out_ref)
        swaps_into(group, blocks, scaled_ref, first_ref, second_ref)
    flat = jnp.concatenate(rows, axis=1)
    gram = gram_of(flat)
    if last:
        packed = pack_grams([ref[...] for ref in before] + [gram])
        for n in range(gram_ref.shape[0]):
            gram_ref[n] = packed
    else:
        gram_ref[...] = gram


def finish_kernel(row_total, grams_ref, *refs):
    applied_refs, (out_hbm, trust_ref, out_ref, sems) = refs[:ITERS], refs[ITERS:]
    devices = grams_ref.shape[0]
    blocks, vectors = out_ref.shape[1:3]
    sends = [pltpu.make_async_copy(out_ref.at[t], out_hbm.at[t], sems.at[t]) for t in range(ITERS)]
    total = grams_ref[0]
    for n in range(1, devices):
        total = total + grams_ref[n]
    rows = lax.broadcasted_iota(jnp.int32, (vectors, vectors), 0)
    lanes = lax.broadcasted_iota(jnp.int32, (vectors, vectors), 1)
    unit = (rows == lanes).astype(jnp.float32)
    row_at = lax.broadcasted_iota(jnp.int32, (vectors, 1), 0)
    grams = unpack_grams(total, vectors)
    work = [jnp.concatenate([gram, unit], axis=1) for gram in grams]
    for j in range(vectors):
        for t in range(ITERS):
            m = work[t]
            ratio = jnp.where(row_at > j, m[:, j : j + 1] / m[j : j + 1, j : j + 1], 0.0)
            work[t] = m - ratio * m[j : j + 1, :]
    good = jnp.bool_(True)
    for t in range(ITERS):
        m = work[t]
        pivots = jnp.sum(m[:, :vectors] * unit, axis=1, keepdims=True)
        inverse = m[:, vectors:] * lax.rsqrt(pivots / row_total)
        squares = jnp.sum(grams[t] * unit, axis=0, keepdims=True)
        norm = jnp.sum(inverse * inverse * squares) / row_total
        good = good & (norm < TRUST) & (jnp.min(squares) > TINY)
        left = [part.astype(jnp.float32) for part in pieces_of(inverse, 3)]
        left = jnp.concatenate([left[i] for i, _ in TERMS], axis=1).astype(jnp.bfloat16)
        for b in range(blocks):
            right = pieces_of(applied_refs[t][b], 3)
            right = jnp.concatenate([right[j] for _, j in TERMS], axis=0)
            out_ref[t, b] = jnp.dot(left, right, preferred_element_type=jnp.float32)
        sends[t].start()
    trust_ref[0] = good.astype(jnp.int32)
    for send in sends:
        send.wait()


def neighbours(scaled):
    count, blocks = lax.axis_size("group"), scaled.shape[0]
    up = [(i, i + 1) for i in range(count - 1)]
    down = [(i + 1, i) for i in range(count - 1)]
    low = lax.ppermute(scaled[blocks - RIM :], "group", up)
    high = lax.ppermute(scaled[:RIM], "group", down)
    return low, high


def swap(first, second):
    count = lax.axis_size("group")
    ups = [[(i, i + 1) for i in range(start, count - 1, 2)] for start in (0, 1)]
    pairs = [up + [(j, i) for i, j in up] for up in ups]
    return [lax.ppermute(x, "group", pair) for x, pair in zip((first, second), pairs)]


def stepwise(start_basis, tiles, tile_cols, tile_count, recv_list):
    groups, peers = lax.axis_size("group"), lax.axis_size("row")
    blocks, per_row, side, _ = tiles.shape
    vectors = start_basis.shape[1]
    row_total = groups * peers * blocks * side
    live = jnp.arange(per_row, dtype=jnp.int32)[None, :] < tile_count[:, None]
    live = live.astype(jnp.float32)
    wide = tiles.astype(jnp.float32)
    sums = jnp.einsum("btij,bt->bi", wide * wide, live, precision=HIGH)
    root = (1e-06 + sums) ** (-0.25)
    wanted = recv_list.reshape(peers * SLOTS)
    take = jnp.clip(wanted - lax.axis_index("group") * peers * blocks, 0, peers * blocks - 1)
    basis, results = start_basis, []
    for _ in range(ITERS):
        scaled = basis * root[:, None, :]
        low, high = neighbours(scaled)
        received = jnp.take(lax.all_gather(scaled, "row", axis=0, tiled=True), take, axis=0)
        extended = jnp.concatenate([scaled, received, low, high], axis=0)
        picked = jnp.take(extended, tile_cols, axis=0) * live[:, :, None, None]
        product = jnp.einsum(
            "btij,btkj->bki", tiles, picked, precision=HIGH, preferred_element_type=jnp.float32
        )
        applied = product * root[:, None, :]
        gram = jnp.einsum("bki,bli->kl", applied, applied, precision=HIGH)
        factor = jnp.linalg.cholesky(lax.psum(gram, ("group", "row")) / row_total)
        inverse = lax.linalg.triangular_solve(
            factor, jnp.eye(vectors, dtype=jnp.float32), left_side=True, lower=True
        )
        basis = jnp.einsum("kl,bli->bki", inverse, applied, precision=HIGH)
        results.append(basis)
    return jnp.stack(results)


def local(start_basis, tiles, tile_cols, tile_count, recv_list):
    groups, peers = lax.axis_size("group"), lax.axis_size("row")
    blocks, per_row, side, _ = tiles.shape
    vectors = start_basis.shape[1]
    place = jnp.stack([lax.axis_index("group"), lax.axis_index("row")]).astype(jnp.int32)
    wanted = jnp.transpose(recv_list.reshape(peers, SLOTS))
    lists = pl.cdiv(peers * SLOTS, vectors)
    tile_bytes = tiles.size * 2
    far_tiles = far(tiles)
    block_shape = (vectors, side)
    picked_shape = (peers * SLOTS,) + block_shape
    rim_shape = f32(RIM, *block_shape)
    kept = held_blocks(tiles)
    rest = pltpu.VMEM((blocks - kept,) + tiles.shape[1:], tiles.dtype)
    root, scaled, *rims, held = pl.pallas_call(
        roots_kernel,
        out_shape=(
            f32(blocks, 1, side),
            f32(blocks + lists, *block_shape),
            rim_shape,
            rim_shape,
            pltpu.VMEM((kept,) + tiles.shape[1:], tiles.dtype),
        ),
        in_specs=[smem()] + [hbm()] * 4,
        out_specs=(vmem(),) * 5,
        scratch_shapes=[
            rest,
            pltpu.SMEM((blocks,), jnp.int32),
            pltpu.SMEM((SLOTS, peers), jnp.int32),
            pltpu.VMEM((blocks,) + block_shape, jnp.float32),
            pltpu.SemaphoreType.DMA((5,)),
        ],
        compiler_params=params(),
        cost_estimate=cost(tiles.size * 2, tile_bytes),
        name="roots",
    )(place, far(tile_count), far(wanted), far_tiles, far(start_basis))
    slots = blocks + peers * SLOTS + 2 * RIM
    powers, grams = [], []
    for t in range(ITERS):
        last = t == ITERS - 1
        if t == 0:
            swapped = swap(*rims)
            received = lax.all_gather(scaled, "row", axis=0)
        else:
            received = lax.all_to_all(outgoing, "row", 0, 0, tiled=True)
            swapped = swap(*rims)
        scalars = [place, tile_count, tile_cols] + ([wanted] if t == 0 else [])
        arrays = [far_tiles, held, root, scaled, received, *swapped]
        shapes = [f32(blocks, *block_shape)]
        if last:
            shapes += [f32(groups * peers, vectors // 2, LANES)]
            arrays += grams
        else:
            shapes += [f32(vectors, vectors), f32(blocks, *block_shape), f32(*picked_shape)]
            shapes += [rim_shape] * 2
            if t:
                arrays += [asked]
            else:
                shapes += [f32(peers * SLOTS, side)]
        result = pl.pallas_call(
            functools.partial(apply_kernel, t),
            out_shape=tuple(shapes),
            in_specs=[smem()] * len(scalars) + [hbm()] + [vmem()] * (len(arrays) - 1),
            out_specs=tuple(vmem() for _ in shapes),
            scratch_shapes=[
                pltpu.VMEM((slots + 1, PIECES * vectors, side), jnp.bfloat16),
                rest,
                pltpu.SemaphoreType.DMA,
            ],
            compiler_params=params(),
            cost_estimate=cost(tiles.size * 2 * vectors * PIECES, tile_bytes),
            name="apply_last" if last else "apply",
        )(*scalars, *arrays)
        powers.append(result[0])
        grams.append(result[1])
        if not last:
            scaled, outgoing, *rims = result[2:6]
            if t == 0:
                asked = result[6]
    gathered = lax.all_to_all(grams[-1], ("group", "row"), 0, 0, tiled=True)
    krylov, trust = pl.pallas_call(
        functools.partial(finish_kernel, float(groups * peers * blocks * side)),
        out_shape=(pltpu.HBM((ITERS, blocks, vectors, side), jnp.float32), jax.ShapeDtypeStruct((1,), jnp.int32)),
        in_specs=[vmem()] * (1 + ITERS),
        out_specs=(hbm(), smem()),
        scratch_shapes=[
            pltpu.VMEM((ITERS, blocks, vectors, side), jnp.float32),
            pltpu.SemaphoreType.DMA((ITERS,)),
        ],
        compiler_params=params(),
        name="finish",
    )(gathered, *powers)
    return lax.cond(
        trust[0] > 0,
        lambda *_: krylov,
        stepwise,
        start_basis, tiles, tile_cols, tile_count, recv_list,
    )


def solution(mesh):
    placed = (
        P(("group", "row"), None, None),
        P(("group", "row"), None, None, None),
        P(("group", "row"), None),
        P(("group", "row")),
        P("group", "row", None, None),
    )
    return jax.shard_map(
        local,
        mesh=mesh,
        in_specs=placed,
        out_specs=P(None, ("group", "row"), None, None),
        check_vma=False,
    )
```

```python
import functools

import jax
import jax.numpy as jnp
from jax import lax
from jax.experimental import pallas as pl
from jax.experimental.pallas import tpu as pltpu
from jax.sharding import PartitionSpec as P

SLOTS = 2
RIM = 2
ITERS = 3
MINLIVE = 10
LANES = 128
HELD_BYTES = 5 * 1024 * 1024 // 2
PIECES = 2
VMEM_BYTES = 24 * 1024 * 1024
TRUST = 64.0
TINY = 1e-25

HIGH = lax.Precision.HIGHEST
NT = (((1,), (1,)), ((), ()))


def vmem():
    return pl.BlockSpec(memory_space=pltpu.VMEM)


def smem():
    return pl.BlockSpec(memory_space=pltpu.SMEM)


def hbm():
    return pl.BlockSpec(memory_space=pltpu.HBM)


def far(x):
    return pltpu.with_memory_space_constraint(x, pltpu.HBM)


def f32(*shape):
    return jax.ShapeDtypeStruct(shape, jnp.float32)


def params():
    return pltpu.CompilerParams(vmem_limit_bytes=VMEM_BYTES)


def cost(flops, moved):
    return pl.CostEstimate(flops=flops, bytes_accessed=moved, transcendentals=0)


def held_blocks(tiles):
    return min(tiles.shape[0] - 1, HELD_BYTES // (tiles.size // tiles.shape[0] * 2))


def load(tiles_hbm, start, tiles_ref, sems):
    count, per_row = tiles_ref.shape[:2]
    half = per_row // 2
    copies = []
    for b in range(count):
        for n, part in enumerate((pl.ds(0, half), pl.ds(half, per_row - half))):
            copies.append(
                pltpu.make_async_copy(
                    tiles_hbm.at[start + b, part], tiles_ref.at[b, part], sems.at[start + b, n]
                )
            )
    for copy in copies:
        copy.start()
    return copies


def wait_all(copies):
    for copy in copies:
        copy.wait()


def roots_kernel(place_ref, count_hbm, want_hbm, tiles_hbm, basis_hbm, root_ref, sent_ref,
                 first_ref, second_ref, held_ref, rest_ref, count_ref, want_ref, basis_ref,
                 load_sems, sems):
    held, per_row, side, _ = held_ref.shape
    blocks = held + rest_ref.shape[0]
    peers = want_ref.shape[1]
    vectors = basis_ref.shape[1]
    rest_load = load(tiles_hbm, held, rest_ref, load_sems)
    small = [
        pltpu.make_async_copy(source, target, sems.at[n])
        for n, (source, target) in enumerate(
            ((count_hbm, count_ref), (want_hbm, want_ref), (basis_hbm, basis_ref))
        )
    ]
    for copy in small:
        copy.start()
    held_load = load(tiles_hbm, 0, held_ref, load_sems)
    wait_all(small)
    for p in range(peers):
        owned = (place_ref[0] * peers + p) * blocks
        for c in range(SLOTS):
            at = jnp.full((1, side), want_ref[c, p] - owned, jnp.int32).astype(jnp.float32)
            block, row = divmod(p * SLOTS + c, vectors)
            sent_ref[blocks + block, row : row + 1] = at
    wait_all(rest_load)
    for b in list(range(held, blocks)) + list(range(held)):
        if b == 0:
            wait_all(held_load)
        tile_ref = held_ref.at[b] if b < held else rest_ref.at[b - held]
        total = jnp.zeros((side, side), jnp.float32)
        for s in range(per_row):
            wide = tile_ref[s].astype(jnp.float32)
            square = wide * wide
            if s >= MINLIVE:
                square = square * (s < count_ref[b]).astype(jnp.float32)
            total = total + square
        sums = jnp.sum(total.T, axis=0, keepdims=True)
        root = lax.rsqrt(jnp.sqrt(1e-06 + sums))
        root_ref[b] = root
        sent_ref[b] = basis_ref[b] * root
    swaps_into(place_ref[0], blocks, sent_ref, first_ref, second_ref)


def swaps_into(group, blocks, scaled_ref, first_ref, second_ref):
    odd = group % 2
    for h in range(RIM):
        first_ref[h] = scaled_ref[(1 - odd) * (blocks - RIM) + h]
        second_ref[h] = scaled_ref[odd * (blocks - RIM) + h]


def pick_into(asked_ref, scaled_ref, out_ref):
    blocks, vectors, side = scaled_ref.shape
    for n in range(asked_ref.shape[0]):
        at = jnp.broadcast_to(asked_ref[n : n + 1], (vectors, side))
        value = scaled_ref[0]
        for b in range(1, blocks):
            value = jnp.where(at == float(b), scaled_ref[b], value)
        out_ref[n] = value


def pieces_of(x, count):
    parts = []
    for n in range(count):
        part = x.astype(jnp.bfloat16)
        parts.append(part)
        if n < count - 1:
            x = x - part.astype(jnp.float32)
    return parts


def split_into(x, out_ref, slot):
    vectors = x.shape[0]
    for n, part in enumerate(pieces_of(x, PIECES)):
        out_ref[slot, pl.ds(n * vectors, vectors)] = part


def gram_of(flat):
    k = flat.shape[0]
    stack = jnp.concatenate(pieces_of(flat, 3), axis=0)
    full = lax.dot_general(stack, stack, NT, preferred_element_type=jnp.float32)
    term = lambda i, j: full[i * k : (i + 1) * k, j * k : (j + 1) * k]
    small = term(1, 1) + (term(0, 2) + term(2, 0))
    return term(0, 0) + ((term(0, 1) + term(1, 0)) + small)


TERMS = ((0, 0), (0, 1), (1, 0), (1, 1), (0, 2), (2, 0))


def pack_grams(grams):
    half = grams[0].shape[0] // 2
    parts = [g[:half] for g in grams] + [g[half:] for g in grams]
    spare = LANES - len(parts) * grams[0].shape[1]
    return jnp.concatenate(parts + [jnp.zeros((half, spare), jnp.float32)], axis=1)


def unpack_grams(packed, vectors):
    upper = [packed[:, t * vectors : (t + 1) * vectors] for t in range(ITERS)]
    lower = [packed[:, (ITERS + t) * vectors : (ITERS + t + 1) * vectors] for t in range(ITERS)]
    return [jnp.concatenate(pair, axis=0) for pair in zip(upper, lower)]


def apply_kernel(step_at, *refs):
    last, opening = step_at == ITERS - 1, step_at == 0
    place_ref, count_ref, cols_ref, *refs = refs
    if opening:
        want_ref, *refs = refs
    tiles_at, held_ref, root_ref, own_ref, recv_ref, swapped_ref, swapped_next_ref, *refs = refs
    if opening:
        *refs, table = refs
        rest_ref = tiles_at
    else:
        *refs, table, rest_ref, load_sems = refs
    held, per_row, side, _ = held_ref.shape
    blocks = held + rest_ref.shape[0]
    if not opening:
        rest_load = load(tiles_at, held, rest_ref, load_sems)
    if last:
        *before, applied_ref, gram_hbm, packed_ref, sem = refs
    else:
        if not opening:
            asked_ref, *refs = refs
        applied_ref, gram_ref, scaled_ref, out_hbm, first_ref, second_ref, *refs = refs
        if opening:
            asked_ref, *refs = refs
        picked_ref, sem = refs
    vectors = own_ref.shape[1]
    group = place_ref[0]
    slot = 0
    for b in range(blocks):
        split_into(own_ref[b], table, slot)
        slot += 1
    if opening:
        peers = recv_ref.shape[0]
        for p in range(peers):
            for c in range(SLOTS):
                at = jnp.clip(want_ref[c, p] - (group * peers + p) * blocks, 0, blocks - 1)
                split_into(recv_ref[p, at], table, slot)
                slot += 1
                entry = place_ref[1] * SLOTS + c
                asked_ref[p * SLOTS + c : p * SLOTS + c + 1] = recv_ref[
                    p, blocks + entry // vectors, pl.ds(entry % vectors, 1)
                ]
    else:
        for n in range(recv_ref.shape[0]):
            split_into(recv_ref[n], table, slot)
            slot += 1
    odd = group % 2 == 1
    for a_ref, b_ref in ((swapped_ref, swapped_next_ref), (swapped_next_ref, swapped_ref)):
        for h in range(RIM):
            split_into(jnp.where(odd, a_ref[h], b_ref[h]), table, slot)
            slot += 1
    table[slot] = jnp.zeros(table.shape[1:], table.dtype)
    rows = []
    for b in range(blocks):
        picked = []
        for s in range(per_row):
            at = jnp.where(s < count_ref[b], cols_ref[b, s], slot)
            picked.append(table[at])
        x = jnp.concatenate(picked, axis=1)
        if b == held and not opening:
            wait_all(rest_load)
        tile_ref = held_ref.at[b] if b < held else rest_ref.at[b - held]
        t = jnp.concatenate([tile_ref[s] for s in range(per_row)], axis=1)
        product = lax.dot_general(x, t, NT, preferred_element_type=jnp.float32)
        total = product[(PIECES - 1) * vectors :]
        for piece in range(PIECES - 2, -1, -1):
            total = total + product[piece * vectors : (piece + 1) * vectors]
        root = root_ref[b]
        row = total * root
        applied_ref[b] = row
        rows.append(row)
        if not last:
            scaled_ref[b] = row * root
    if not last:
        pick_into(asked_ref, scaled_ref, picked_ref)
        send = pltpu.make_async_copy(picked_ref, out_hbm, sem)
        send.start()
        swaps_into(group, blocks, scaled_ref, first_ref, second_ref)
    flat = jnp.concatenate(rows, axis=1)
    gram = gram_of(flat)
    if last:
        packed = pack_grams([ref[...] for ref in before] + [gram])
        for n in range(packed_ref.shape[0]):
            packed_ref[n] = packed
        send = pltpu.make_async_copy(packed_ref, gram_hbm, sem)
        send.start()
        send.wait()
    else:
        gram_ref[...] = gram
        send.wait()


def finish_kernel(row_total, grams_ref, *refs):
    applied_refs, (out_hbm, trust_ref, out_ref, sems) = refs[:ITERS], refs[ITERS:]
    devices = grams_ref.shape[0]
    blocks, vectors = out_ref.shape[1:3]
    sends = [pltpu.make_async_copy(out_ref.at[t], out_hbm.at[t], sems.at[t]) for t in range(ITERS)]
    total = grams_ref[0]
    for n in range(1, devices):
        total = total + grams_ref[n]
    rows = lax.broadcasted_iota(jnp.int32, (vectors, vectors), 0)
    lanes = lax.broadcasted_iota(jnp.int32, (vectors, vectors), 1)
    unit = (rows == lanes).astype(jnp.float32)
    row_at = lax.broadcasted_iota(jnp.int32, (vectors, 1), 0)
    grams = unpack_grams(total, vectors)
    work = [jnp.concatenate([gram, unit], axis=1) for gram in grams]
    for j in range(vectors):
        for t in range(ITERS):
            m = work[t]
            ratio = jnp.where(row_at > j, m[:, j : j + 1] / m[j : j + 1, j : j + 1], 0.0)
            work[t] = m - ratio * m[j : j + 1, :]
    good = jnp.bool_(True)
    for t in range(ITERS):
        m = work[t]
        pivots = jnp.sum(m[:, :vectors] * unit, axis=1, keepdims=True)
        inverse = m[:, vectors:] * lax.rsqrt(pivots / row_total)
        squares = jnp.sum(grams[t] * unit, axis=0, keepdims=True)
        norm = jnp.sum(inverse * inverse * squares) / row_total
        good = good & (norm < TRUST) & (jnp.min(squares) > TINY)
        left = [part.astype(jnp.float32) for part in pieces_of(inverse, 3)]
        left = jnp.concatenate([left[i] for i, _ in TERMS], axis=1).astype(jnp.bfloat16)
        for b in range(blocks):
            right = pieces_of(applied_refs[t][b], 3)
            right = jnp.concatenate([right[j] for _, j in TERMS], axis=0)
            out_ref[t, b] = jnp.dot(left, right, preferred_element_type=jnp.float32)
        sends[t].start()
    trust_ref[0] = good.astype(jnp.int32)
    for send in sends:
        send.wait()


def neighbours(scaled):
    count, blocks = lax.axis_size("group"), scaled.shape[0]
    up = [(i, i + 1) for i in range(count - 1)]
    down = [(i + 1, i) for i in range(count - 1)]
    low = lax.ppermute(scaled[blocks - RIM :], "group", up)
    high = lax.ppermute(scaled[:RIM], "group", down)
    return low, high


def swap(first, second):
    count = lax.axis_size("group")
    ups = [[(i, i + 1) for i in range(start, count - 1, 2)] for start in (0, 1)]
    pairs = [up + [(j, i) for i, j in up] for up in ups]
    return [lax.ppermute(x, "group", pair) for x, pair in zip((first, second), pairs)]


def stepwise(start_basis, tiles, tile_cols, tile_count, recv_list):
    groups, peers = lax.axis_size("group"), lax.axis_size("row")
    blocks, per_row, side, _ = tiles.shape
    vectors = start_basis.shape[1]
    row_total = groups * peers * blocks * side
    live = jnp.arange(per_row, dtype=jnp.int32)[None, :] < tile_count[:, None]
    live = live.astype(jnp.float32)
    wide = tiles.astype(jnp.float32)
    sums = jnp.einsum("btij,bt->bi", wide * wide, live, precision=HIGH)
    root = (1e-06 + sums) ** (-0.25)
    wanted = recv_list.reshape(peers * SLOTS)
    take = jnp.clip(wanted - lax.axis_index("group") * peers * blocks, 0, peers * blocks - 1)
    basis, results = start_basis, []
    for _ in range(ITERS):
        scaled = basis * root[:, None, :]
        low, high = neighbours(scaled)
        received = jnp.take(lax.all_gather(scaled, "row", axis=0, tiled=True), take, axis=0)
        extended = jnp.concatenate([scaled, received, low, high], axis=0)
        picked = jnp.take(extended, tile_cols, axis=0) * live[:, :, None, None]
        product = jnp.einsum(
            "btij,btkj->bki", tiles, picked, precision=HIGH, preferred_element_type=jnp.float32
        )
        applied = product * root[:, None, :]
        gram = jnp.einsum("bki,bli->kl", applied, applied, precision=HIGH)
        factor = jnp.linalg.cholesky(lax.psum(gram, ("group", "row")) / row_total)
        inverse = lax.linalg.triangular_solve(
            factor, jnp.eye(vectors, dtype=jnp.float32), left_side=True, lower=True
        )
        basis = jnp.einsum("kl,bli->bki", inverse, applied, precision=HIGH)
        results.append(basis)
    return jnp.stack(results)


def local(start_basis, tiles, tile_cols, tile_count, recv_list):
    groups, peers = lax.axis_size("group"), lax.axis_size("row")
    blocks, per_row, side, _ = tiles.shape
    vectors = start_basis.shape[1]
    place = jnp.stack([lax.axis_index("group"), lax.axis_index("row")]).astype(jnp.int32)
    wanted = jnp.transpose(recv_list.reshape(peers, SLOTS))
    lists = pl.cdiv(peers * SLOTS, vectors)
    tile_bytes = tiles.size * 2
    far_tiles = far(tiles)
    block_shape = (vectors, side)
    picked_shape = (peers * SLOTS,) + block_shape
    rim_shape = f32(RIM, *block_shape)
    kept = held_blocks(tiles)
    rest = pltpu.VMEM((blocks - kept,) + tiles.shape[1:], tiles.dtype)
    load_sems = pltpu.SemaphoreType.DMA((blocks, 2))
    root, scaled, *rims, held, opening_rest = pl.pallas_call(
        roots_kernel,
        out_shape=(
            f32(blocks, 1, side),
            f32(blocks + lists, *block_shape),
            rim_shape,
            rim_shape,
            pltpu.VMEM((kept,) + tiles.shape[1:], tiles.dtype),
            rest,
        ),
        in_specs=[smem()] + [hbm()] * 4,
        out_specs=(vmem(),) * 6,
        scratch_shapes=[
            pltpu.SMEM((blocks,), jnp.int32),
            pltpu.SMEM((SLOTS, peers), jnp.int32),
            pltpu.VMEM((blocks,) + block_shape, jnp.float32),
            load_sems,
            pltpu.SemaphoreType.DMA((3,)),
        ],
        compiler_params=params(),
        cost_estimate=cost(tiles.size * 2, tile_bytes),
        name="roots",
    )(place, far(tile_count), far(wanted), far_tiles, far(start_basis))
    slots = blocks + peers * SLOTS + 2 * RIM
    powers, grams = [], []
    for t in range(ITERS):
        last = t == ITERS - 1
        if t == 0:
            swapped = swap(*rims)
            received = lax.all_gather(scaled, "row", axis=0)
        else:
            received = lax.all_to_all(outgoing, "row", 0, 0, tiled=True)
            swapped = swap(*rims)
        scalars = [place, tile_count, tile_cols] + ([wanted] if t == 0 else [])
        arrays = [far_tiles if t else opening_rest, held, root, scaled, received, *swapped]
        shapes = [f32(blocks, *block_shape)]
        specs = [vmem(), vmem()]
        if last:
            shapes += [pltpu.HBM((groups * peers, vectors // 2, LANES), jnp.float32)]
            specs = [vmem(), hbm()]
            scratch = [
                pltpu.VMEM((groups * peers, vectors // 2, LANES), jnp.float32),
                pltpu.SemaphoreType.DMA,
            ]
            arrays += grams
        else:
            shapes += [f32(vectors, vectors), f32(blocks, *block_shape), pltpu.HBM(picked_shape, jnp.float32)]
            shapes += [rim_shape] * 2
            specs += [vmem(), hbm(), vmem(), vmem()]
            scratch = [pltpu.VMEM(picked_shape, jnp.float32), pltpu.SemaphoreType.DMA]
            if t:
                arrays += [asked]
            else:
                shapes += [f32(peers * SLOTS, side)]
                specs += [vmem()]
        result = pl.pallas_call(
            functools.partial(apply_kernel, t),
            out_shape=tuple(shapes),
            in_specs=[smem()] * len(scalars)
            + [hbm() if t else vmem()]
            + [vmem()] * (len(arrays) - 1),
            out_specs=tuple(specs),
            scratch_shapes=scratch
            + [
                pltpu.VMEM((slots + 1, PIECES * vectors, side), jnp.bfloat16),
            ]
            + ([rest, load_sems] if t else []),
            compiler_params=params(),
            cost_estimate=cost(tiles.size * 2 * vectors * PIECES, tile_bytes),
            name="apply_last" if last else "apply",
        )(*scalars, *arrays)
        powers.append(result[0])
        grams.append(result[1])
        if not last:
            scaled, outgoing, *rims = result[2:6]
            if t == 0:
                asked = result[6]
    gathered = lax.all_to_all(grams[-1], ("group", "row"), 0, 0, tiled=True)
    krylov, trust = pl.pallas_call(
        functools.partial(finish_kernel, float(groups * peers * blocks * side)),
        out_shape=(pltpu.HBM((ITERS, blocks, vectors, side), jnp.float32), jax.ShapeDtypeStruct((1,), jnp.int32)),
        in_specs=[vmem()] * (1 + ITERS),
        out_specs=(hbm(), smem()),
        scratch_shapes=[
            pltpu.VMEM((ITERS, blocks, vectors, side), jnp.float32),
            pltpu.SemaphoreType.DMA((ITERS,)),
        ],
        compiler_params=params(),
        name="finish",
    )(gathered, *powers)
    return lax.cond(
        trust[0] > 0,
        lambda *_: krylov,
        stepwise,
        start_basis, tiles, tile_cols, tile_count, recv_list,
    )


def solution(mesh):
    placed = (
        P(("group", "row"), None, None),
        P(("group", "row"), None, None, None),
        P(("group", "row"), None),
        P(("group", "row")),
        P("group", "row", None, None),
    )
    return jax.shard_map(
        local,
        mesh=mesh,
        in_specs=placed,
        out_specs=P(None, ("group", "row"), None, None),
        check_vma=False,
    )
```

```python
import functools

import jax
import jax.numpy as jnp
from jax import lax
from jax.experimental import pallas as pl
from jax.experimental.pallas import tpu as pltpu
from jax.sharding import PartitionSpec as P

SLOTS = 2
RIM = 2
ITERS = 3
MINLIVE = 10
LANES = 128
HELD_BYTES = 3 * 1024 * 1024
PIECES = 2
VMEM_BYTES = 24 * 1024 * 1024
TRUST = 64.0
TINY = 1e-25

HIGH = lax.Precision.HIGHEST
NT = (((1,), (1,)), ((), ()))


def vmem():
    return pl.BlockSpec(memory_space=pltpu.VMEM)


def smem():
    return pl.BlockSpec(memory_space=pltpu.SMEM)


def hbm():
    return pl.BlockSpec(memory_space=pltpu.HBM)


def far(x):
    return pltpu.with_memory_space_constraint(x, pltpu.HBM)


def f32(*shape):
    return jax.ShapeDtypeStruct(shape, jnp.float32)


def params():
    return pltpu.CompilerParams(vmem_limit_bytes=VMEM_BYTES)


def cost(flops, moved):
    return pl.CostEstimate(flops=flops, bytes_accessed=moved, transcendentals=0)


def held_blocks(tiles):
    return min(tiles.shape[0] - 1, HELD_BYTES // (tiles.size // tiles.shape[0] * 2))


def load(tiles_hbm, start, tiles_ref, sem):
    copy = pltpu.make_async_copy(tiles_hbm.at[pl.ds(start, tiles_ref.shape[0])], tiles_ref, sem)
    copy.start()
    return copy


def roots_kernel(place_ref, count_hbm, want_hbm, tiles_hbm, basis_hbm, root_ref, sent_ref,
                 first_ref, second_ref, held_ref, rest_ref, count_ref, want_ref, basis_ref, sems):
    held, per_row, side, _ = held_ref.shape
    blocks = held + rest_ref.shape[0]
    peers = want_ref.shape[1]
    vectors = basis_ref.shape[1]
    rest_load = load(tiles_hbm, held, rest_ref, sems.at[3])
    small = [
        pltpu.make_async_copy(source, target, sems.at[n])
        for n, (source, target) in enumerate(
            ((count_hbm, count_ref), (want_hbm, want_ref), (basis_hbm, basis_ref))
        )
    ]
    for copy in small:
        copy.start()
    held_load = load(tiles_hbm, 0, held_ref, sems.at[4])
    for copy in small:
        copy.wait()
    for p in range(peers):
        owned = (place_ref[0] * peers + p) * blocks
        for c in range(SLOTS):
            at = jnp.full((1, side), want_ref[c, p] - owned, jnp.int32).astype(jnp.float32)
            block, row = divmod(p * SLOTS + c, vectors)
            sent_ref[blocks + block, row : row + 1] = at
    rest_load.wait()
    for b in list(range(held, blocks)) + list(range(held)):
        if b == 0:
            held_load.wait()
        tile_ref = held_ref.at[b] if b < held else rest_ref.at[b - held]
        total = jnp.zeros((side, side), jnp.float32)
        for s in range(per_row):
            wide = tile_ref[s].astype(jnp.float32)
            square = wide * wide
            if s >= MINLIVE:
                square = square * (s < count_ref[b]).astype(jnp.float32)
            total = total + square
        sums = jnp.sum(total.T, axis=0, keepdims=True)
        root = lax.rsqrt(jnp.sqrt(1e-06 + sums))
        root_ref[b] = root
        sent_ref[b] = basis_ref[b] * root
    swaps_into(place_ref[0], blocks, sent_ref, first_ref, second_ref)


def swaps_into(group, blocks, scaled_ref, first_ref, second_ref):
    odd = group % 2
    for h in range(RIM):
        first_ref[h] = scaled_ref[(1 - odd) * (blocks - RIM) + h]
        second_ref[h] = scaled_ref[odd * (blocks - RIM) + h]


def pick_into(asked_ref, scaled_ref, out_ref):
    blocks, vectors, side = scaled_ref.shape
    for n in range(asked_ref.shape[0]):
        at = jnp.broadcast_to(asked_ref[n : n + 1], (vectors, side))
        value = scaled_ref[0]
        for b in range(1, blocks):
            value = jnp.where(at == float(b), scaled_ref[b], value)
        out_ref[n] = value


def pieces_of(x, count):
    parts = []
    for n in range(count):
        part = x.astype(jnp.bfloat16)
        parts.append(part)
        if n < count - 1:
            x = x - part.astype(jnp.float32)
    return parts


def split_into(x, out_ref, slot):
    vectors = x.shape[0]
    for n, part in enumerate(pieces_of(x, PIECES)):
        out_ref[slot, pl.ds(n * vectors, vectors)] = part


def gram_of(flat):
    k = flat.shape[0]
    stack = jnp.concatenate(pieces_of(flat, 3), axis=0)
    full = lax.dot_general(stack, stack, NT, preferred_element_type=jnp.float32)
    term = lambda i, j: full[i * k : (i + 1) * k, j * k : (j + 1) * k]
    small = term(1, 1) + (term(0, 2) + term(2, 0))
    return term(0, 0) + ((term(0, 1) + term(1, 0)) + small)


TERMS = ((0, 0), (0, 1), (1, 0), (1, 1), (0, 2), (2, 0))


def pack_grams(grams):
    half = grams[0].shape[0] // 2
    parts = [g[:half] for g in grams] + [g[half:] for g in grams]
    spare = LANES - len(parts) * grams[0].shape[1]
    return jnp.concatenate(parts + [jnp.zeros((half, spare), jnp.float32)], axis=1)


def unpack_grams(packed, vectors):
    upper = [packed[:, t * vectors : (t + 1) * vectors] for t in range(ITERS)]
    lower = [packed[:, (ITERS + t) * vectors : (ITERS + t + 1) * vectors] for t in range(ITERS)]
    return [jnp.concatenate(pair, axis=0) for pair in zip(upper, lower)]


def apply_kernel(step_at, *refs):
    last, opening = step_at == ITERS - 1, step_at == 0
    place_ref, count_ref, cols_ref, *refs = refs
    if opening:
        want_ref, *refs = refs
    tiles_at, held_ref, root_ref, own_ref, recv_ref, swapped_ref, swapped_next_ref, *refs = refs
    if opening:
        *refs, table = refs
        rest_ref = tiles_at
    else:
        *refs, table, rest_ref, load_sem = refs
    held, per_row, side, _ = held_ref.shape
    blocks = held + rest_ref.shape[0]
    if not opening:
        rest_load = load(tiles_at, held, rest_ref, load_sem)
    if last:
        *before, applied_ref, gram_hbm, packed_ref, sem = refs
    else:
        if not opening:
            asked_ref, *refs = refs
        applied_ref, gram_ref, scaled_ref, out_hbm, first_ref, second_ref, *refs = refs
        if opening:
            asked_ref, *refs = refs
        picked_ref, sem = refs
    vectors = own_ref.shape[1]
    group = place_ref[0]
    slot = 0
    for b in range(blocks):
        split_into(own_ref[b], table, slot)
        slot += 1
    if opening:
        peers = recv_ref.shape[0]
        for p in range(peers):
            for c in range(SLOTS):
                at = jnp.clip(want_ref[c, p] - (group * peers + p) * blocks, 0, blocks - 1)
                split_into(recv_ref[p, at], table, slot)
                slot += 1
                entry = place_ref[1] * SLOTS + c
                asked_ref[p * SLOTS + c : p * SLOTS + c + 1] = recv_ref[
                    p, blocks + entry // vectors, pl.ds(entry % vectors, 1)
                ]
    else:
        for n in range(recv_ref.shape[0]):
            split_into(recv_ref[n], table, slot)
            slot += 1
    odd = group % 2 == 1
    for a_ref, b_ref in ((swapped_ref, swapped_next_ref), (swapped_next_ref, swapped_ref)):
        for h in range(RIM):
            split_into(jnp.where(odd, a_ref[h], b_ref[h]), table, slot)
            slot += 1
    table[slot] = jnp.zeros(table.shape[1:], table.dtype)
    rows = []
    for b in range(blocks):
        picked = []
        for s in range(per_row):
            at = jnp.where(s < count_ref[b], cols_ref[b, s], slot)
            picked.append(table[at])
        x = jnp.concatenate(picked, axis=1)
        if b == held and not opening:
            rest_load.wait()
        tile_ref = held_ref.at[b] if b < held else rest_ref.at[b - held]
        t = jnp.concatenate([tile_ref[s] for s in range(per_row)], axis=1)
        product = lax.dot_general(x, t, NT, preferred_element_type=jnp.float32)
        total = product[(PIECES - 1) * vectors :]
        for piece in range(PIECES - 2, -1, -1):
            total = total + product[piece * vectors : (piece + 1) * vectors]
        root = root_ref[b]
        row = total * root
        applied_ref[b] = row
        rows.append(row)
        if not last:
            scaled_ref[b] = row * root
    if not last:
        pick_into(asked_ref, scaled_ref, picked_ref)
        send = pltpu.make_async_copy(picked_ref, out_hbm, sem)
        send.start()
        swaps_into(group, blocks, scaled_ref, first_ref, second_ref)
    flat = jnp.concatenate(rows, axis=1)
    gram = gram_of(flat)
    if last:
        packed = pack_grams([ref[...] for ref in before] + [gram])
        for n in range(packed_ref.shape[0]):
            packed_ref[n] = packed
        send = pltpu.make_async_copy(packed_ref, gram_hbm, sem)
        send.start()
        send.wait()
    else:
        gram_ref[...] = gram
        send.wait()


def finish_kernel(row_total, grams_ref, *refs):
    *earlier, final_ref, out_hbm, trust_ref, earlier_ref, out_ref, sems, load_sems = refs
    loads = [
        pltpu.make_async_copy(source, earlier_ref.at[t], load_sems.at[t])
        for t, source in enumerate(earlier)
    ]
    for copy in loads:
        copy.start()
    applied_refs = [earlier_ref.at[t] for t in range(ITERS - 1)] + [final_ref]
    devices = grams_ref.shape[0]
    blocks, vectors = out_ref.shape[1:3]
    sends = [pltpu.make_async_copy(out_ref.at[t], out_hbm.at[t], sems.at[t]) for t in range(ITERS)]
    total = grams_ref[0]
    for n in range(1, devices):
        total = total + grams_ref[n]
    rows = lax.broadcasted_iota(jnp.int32, (vectors, vectors), 0)
    lanes = lax.broadcasted_iota(jnp.int32, (vectors, vectors), 1)
    unit = (rows == lanes).astype(jnp.float32)
    grams = unpack_grams(total, vectors)
    columns = [
        [jnp.broadcast_to(gram[:, k : k + 1], (vectors, vectors)) for k in range(vectors)]
        for gram in grams
    ]
    inverses = [unit] * ITERS
    for j in range(vectors):
        for t, column in enumerate(columns):
            ratio = jnp.where(rows > j, column[j] * (1.0 / column[j][j : j + 1]), 0.0)
            for k in range(j + 1, vectors):
                column[k] = column[k] - ratio * column[k][j : j + 1]
            inverses[t] = inverses[t] - ratio * inverses[t][j : j + 1]
    for copy in loads:
        copy.wait()
    good = jnp.bool_(True)
    for t in range(ITERS):
        pivots = columns[t][0]
        for j in range(1, vectors):
            pivots = jnp.where(rows == j, columns[t][j], pivots)
        inverse = inverses[t] * lax.rsqrt(pivots / row_total)
        squares = jnp.sum(grams[t] * unit, axis=0, keepdims=True)
        norm = jnp.sum(inverse * inverse * squares) / row_total
        good = good & (norm < TRUST) & (jnp.min(squares) > TINY)
        left = [part.astype(jnp.float32) for part in pieces_of(inverse, 3)]
        left = jnp.concatenate([left[i] for i, _ in TERMS], axis=1).astype(jnp.bfloat16)
        for b in range(blocks):
            right = pieces_of(applied_refs[t][b], 3)
            right = jnp.concatenate([right[j] for _, j in TERMS], axis=0)
            out_ref[t, b] = jnp.dot(left, right, preferred_element_type=jnp.float32)
        sends[t].start()
    trust_ref[0] = good.astype(jnp.int32)
    for send in sends:
        send.wait()


def neighbours(scaled):
    count, blocks = lax.axis_size("group"), scaled.shape[0]
    up = [(i, i + 1) for i in range(count - 1)]
    down = [(i + 1, i) for i in range(count - 1)]
    low = lax.ppermute(scaled[blocks - RIM :], "group", up)
    high = lax.ppermute(scaled[:RIM], "group", down)
    return low, high


def swap(first, second):
    count = lax.axis_size("group")
    ups = [[(i, i + 1) for i in range(start, count - 1, 2)] for start in (0, 1)]
    pairs = [up + [(j, i) for i, j in up] for up in ups]
    return [lax.ppermute(x, "group", pair) for x, pair in zip((first, second), pairs)]


def stepwise(start_basis, tiles, tile_cols, tile_count, recv_list):
    groups, peers = lax.axis_size("group"), lax.axis_size("row")
    blocks, per_row, side, _ = tiles.shape
    vectors = start_basis.shape[1]
    row_total = groups * peers * blocks * side
    live = jnp.arange(per_row, dtype=jnp.int32)[None, :] < tile_count[:, None]
    live = live.astype(jnp.float32)
    wide = tiles.astype(jnp.float32)
    sums = jnp.einsum("btij,bt->bi", wide * wide, live, precision=HIGH)
    root = (1e-06 + sums) ** (-0.25)
    wanted = recv_list.reshape(peers * SLOTS)
    take = jnp.clip(wanted - lax.axis_index("group") * peers * blocks, 0, peers * blocks - 1)
    basis, results = start_basis, []
    for _ in range(ITERS):
        scaled = basis * root[:, None, :]
        low, high = neighbours(scaled)
        received = jnp.take(lax.all_gather(scaled, "row", axis=0, tiled=True), take, axis=0)
        extended = jnp.concatenate([scaled, received, low, high], axis=0)
        picked = jnp.take(extended, tile_cols, axis=0) * live[:, :, None, None]
        product = jnp.einsum(
            "btij,btkj->bki", tiles, picked, precision=HIGH, preferred_element_type=jnp.float32
        )
        applied = product * root[:, None, :]
        gram = jnp.einsum("bki,bli->kl", applied, applied, precision=HIGH)
        factor = jnp.linalg.cholesky(lax.psum(gram, ("group", "row")) / row_total)
        inverse = lax.linalg.triangular_solve(
            factor, jnp.eye(vectors, dtype=jnp.float32), left_side=True, lower=True
        )
        basis = jnp.einsum("kl,bli->bki", inverse, applied, precision=HIGH)
        results.append(basis)
    return jnp.stack(results)


def local(start_basis, tiles, tile_cols, tile_count, recv_list):
    groups, peers = lax.axis_size("group"), lax.axis_size("row")
    blocks, per_row, side, _ = tiles.shape
    vectors = start_basis.shape[1]
    place = jnp.stack([lax.axis_index("group"), lax.axis_index("row")]).astype(jnp.int32)
    wanted = jnp.transpose(recv_list.reshape(peers, SLOTS))
    lists = pl.cdiv(peers * SLOTS, vectors)
    tile_bytes = tiles.size * 2
    far_tiles = far(tiles)
    block_shape = (vectors, side)
    picked_shape = (peers * SLOTS,) + block_shape
    rim_shape = f32(RIM, *block_shape)
    kept = held_blocks(tiles)
    rest = pltpu.VMEM((blocks - kept,) + tiles.shape[1:], tiles.dtype)
    root, scaled, *rims, held, opening_rest = pl.pallas_call(
        roots_kernel,
        out_shape=(
            f32(blocks, 1, side),
            f32(blocks + lists, *block_shape),
            rim_shape,
            rim_shape,
            pltpu.VMEM((kept,) + tiles.shape[1:], tiles.dtype),
            rest,
        ),
        in_specs=[smem()] + [hbm()] * 4,
        out_specs=(vmem(),) * 6,
        scratch_shapes=[
            pltpu.SMEM((blocks,), jnp.int32),
            pltpu.SMEM((SLOTS, peers), jnp.int32),
            pltpu.VMEM((blocks,) + block_shape, jnp.float32),
            pltpu.SemaphoreType.DMA((5,)),
        ],
        compiler_params=params(),
        cost_estimate=cost(tiles.size * 2, tile_bytes),
        name="roots",
    )(place, far(tile_count), far(wanted), far_tiles, far(start_basis))
    slots = blocks + peers * SLOTS + 2 * RIM
    powers, grams = [], []
    for t in range(ITERS):
        last = t == ITERS - 1
        if t == 0:
            swapped = swap(*rims)
            received = lax.all_gather(scaled, "row", axis=0)
        else:
            received = lax.all_to_all(outgoing, "row", 0, 0, tiled=True)
            swapped = swap(*rims)
        scalars = [place, tile_count, tile_cols] + ([wanted] if t == 0 else [])
        arrays = [far_tiles if t else opening_rest, held, root, scaled, received, *swapped]
        shapes = [f32(blocks, *block_shape) if last else pltpu.HBM((blocks,) + block_shape, jnp.float32)]
        specs = [vmem(), vmem()]
        if last:
            shapes += [pltpu.HBM((groups * peers, vectors // 2, LANES), jnp.float32)]
            specs = [vmem(), hbm()]
            scratch = [
                pltpu.VMEM((groups * peers, vectors // 2, LANES), jnp.float32),
                pltpu.SemaphoreType.DMA,
            ]
            arrays += grams
        else:
            shapes += [f32(vectors, vectors), f32(blocks, *block_shape), pltpu.HBM(picked_shape, jnp.float32)]
            shapes += [rim_shape] * 2
            specs += [vmem(), hbm(), vmem(), vmem()]
            scratch = [pltpu.VMEM(picked_shape, jnp.float32), pltpu.SemaphoreType.DMA]
            if t:
                arrays += [asked]
            else:
                shapes += [f32(peers * SLOTS, side)]
                specs += [vmem()]
        result = pl.pallas_call(
            functools.partial(apply_kernel, t),
            out_shape=tuple(shapes),
            in_specs=[smem()] * len(scalars)
            + [hbm() if t else vmem()]
            + [vmem()] * (len(arrays) - 1),
            out_specs=tuple(specs),
            scratch_shapes=scratch
            + [
                pltpu.VMEM((slots + 1, PIECES * vectors, side), jnp.bfloat16),
            ]
            + ([rest, pltpu.SemaphoreType.DMA] if t else []),
            compiler_params=params(),
            cost_estimate=cost(tiles.size * 2 * vectors * PIECES, tile_bytes),
            name="apply_last" if last else "apply",
        )(*scalars, *arrays)
        powers.append(result[0])
        grams.append(result[1])
        if not last:
            scaled, outgoing, *rims = result[2:6]
            if t == 0:
                asked = result[6]
    gathered = lax.all_to_all(grams[-1], ("group", "row"), 0, 0, tiled=True)
    krylov, trust = pl.pallas_call(
        functools.partial(finish_kernel, float(groups * peers * blocks * side)),
        out_shape=(pltpu.HBM((ITERS, blocks, vectors, side), jnp.float32), jax.ShapeDtypeStruct((1,), jnp.int32)),
        in_specs=[vmem()] + [hbm()] * (ITERS - 1) + [vmem()],
        out_specs=(hbm(), smem()),
        scratch_shapes=[
            pltpu.VMEM((ITERS - 1, blocks, vectors, side), jnp.float32),
            pltpu.VMEM((ITERS, blocks, vectors, side), jnp.float32),
            pltpu.SemaphoreType.DMA((ITERS,)),
            pltpu.SemaphoreType.DMA((ITERS - 1,)),
        ],
        compiler_params=params(),
        name="finish",
    )(gathered, *[far(power) for power in powers[:-1]], powers[-1])
    return lax.cond(
        trust[0] > 0,
        lambda *_: krylov,
        stepwise,
        start_basis, tiles, tile_cols, tile_count, recv_list,
    )


def solution(mesh):
    placed = (
        P(("group", "row"), None, None),
        P(("group", "row"), None, None, None),
        P(("group", "row"), None),
        P(("group", "row")),
        P("group", "row", None, None),
    )
    return jax.shard_map(
        local,
        mesh=mesh,
        in_specs=placed,
        out_specs=P(None, ("group", "row"), None, None),
        check_vma=False,
    )
```

```python
import functools

import jax
import jax.numpy as jnp
from jax import lax
from jax.experimental import pallas as pl
from jax.experimental.pallas import tpu as pltpu
from jax.sharding import PartitionSpec as P

SLOTS = 2
RIM = 2
ITERS = 3
MINLIVE = 10
LANES = 128
HELD_BYTES = 5 * 1024 * 1024 // 2
PIECES = 2
VMEM_BYTES = 24 * 1024 * 1024
TRUST = 64.0
TINY = 1e-25

HIGH = lax.Precision.HIGHEST
NT = (((1,), (1,)), ((), ()))


def vmem():
    return pl.BlockSpec(memory_space=pltpu.VMEM)


def smem():
    return pl.BlockSpec(memory_space=pltpu.SMEM)


def hbm():
    return pl.BlockSpec(memory_space=pltpu.HBM)


def far(x):
    return pltpu.with_memory_space_constraint(x, pltpu.HBM)


def f32(*shape):
    return jax.ShapeDtypeStruct(shape, jnp.float32)


def params():
    return pltpu.CompilerParams(vmem_limit_bytes=VMEM_BYTES)


def cost(flops, moved):
    return pl.CostEstimate(flops=flops, bytes_accessed=moved, transcendentals=0)


def held_blocks(tiles):
    return min(tiles.shape[0] - 1, HELD_BYTES // (tiles.size // tiles.shape[0] * 2))


def load(tiles_hbm, start, tiles_ref, sem):
    copy = pltpu.make_async_copy(tiles_hbm.at[pl.ds(start, tiles_ref.shape[0])], tiles_ref, sem)
    copy.start()
    return copy


def roots_kernel(place_ref, count_hbm, want_hbm, tiles_hbm, basis_hbm, root_ref, sent_ref,
                 first_ref, second_ref, held_ref, rest_ref, count_ref, want_ref, basis_ref, sems):
    held, per_row, side, _ = held_ref.shape
    blocks = held + rest_ref.shape[0]
    peers = want_ref.shape[1]
    vectors = basis_ref.shape[1]
    rest_load = load(tiles_hbm, held, rest_ref, sems.at[3])
    small = [
        pltpu.make_async_copy(source, target, sems.at[n])
        for n, (source, target) in enumerate(
            ((count_hbm, count_ref), (want_hbm, want_ref), (basis_hbm, basis_ref))
        )
    ]
    for copy in small:
        copy.start()
    held_load = load(tiles_hbm, 0, held_ref, sems.at[4])
    for copy in small:
        copy.wait()
    for p in range(peers):
        owned = (place_ref[0] * peers + p) * blocks
        for c in range(SLOTS):
            at = jnp.full((1, side), want_ref[c, p] - owned, jnp.int32).astype(jnp.float32)
            block, row = divmod(p * SLOTS + c, vectors)
            sent_ref[blocks + block, row : row + 1] = at
    rest_load.wait()
    for b in list(range(held, blocks)) + list(range(held)):
        if b == 0:
            held_load.wait()
        tile_ref = held_ref.at[b] if b < held else rest_ref.at[b - held]
        total = jnp.zeros((side, side), jnp.float32)
        for s in range(per_row):
            wide = tile_ref[s].astype(jnp.float32)
            square = wide * wide
            if s >= MINLIVE:
                square = square * (s < count_ref[b]).astype(jnp.float32)
            total = total + square
        sums = jnp.sum(total.T, axis=0, keepdims=True)
        root = lax.rsqrt(jnp.sqrt(1e-06 + sums))
        root_ref[b] = root
        sent_ref[b] = basis_ref[b] * root
    swaps_into(place_ref[0], blocks, sent_ref, first_ref, second_ref)


def swaps_into(group, blocks, scaled_ref, first_ref, second_ref):
    odd = group % 2
    for h in range(RIM):
        first_ref[h] = scaled_ref[(1 - odd) * (blocks - RIM) + h]
        second_ref[h] = scaled_ref[odd * (blocks - RIM) + h]


def pick_into(asked_ref, scaled_ref, out_ref):
    blocks, vectors, side = scaled_ref.shape
    for n in range(asked_ref.shape[0]):
        at = jnp.broadcast_to(asked_ref[n : n + 1], (vectors, side))
        value = scaled_ref[0]
        for b in range(1, blocks):
            value = jnp.where(at == float(b), scaled_ref[b], value)
        out_ref[n] = value


def pieces_of(x, count):
    parts = []
    for n in range(count):
        part = x.astype(jnp.bfloat16)
        parts.append(part)
        if n < count - 1:
            x = x - part.astype(jnp.float32)
    return parts


def split_into(x, out_ref, slot):
    vectors = x.shape[0]
    for n, part in enumerate(pieces_of(x, PIECES)):
        out_ref[slot, pl.ds(n * vectors, vectors)] = part


def gram_of(flat):
    k = flat.shape[0]
    stack = jnp.concatenate(pieces_of(flat, 3), axis=0)
    full = lax.dot_general(stack, stack, NT, preferred_element_type=jnp.float32)
    term = lambda i, j: full[i * k : (i + 1) * k, j * k : (j + 1) * k]
    small = term(1, 1) + (term(0, 2) + term(2, 0))
    return term(0, 0) + ((term(0, 1) + term(1, 0)) + small)


TERMS = ((0, 0), (0, 1), (1, 0), (1, 1), (0, 2), (2, 0))


def pack_grams(grams):
    half = grams[0].shape[0] // 2
    parts = [g[:half] for g in grams] + [g[half:] for g in grams]
    spare = LANES - len(parts) * grams[0].shape[1]
    return jnp.concatenate(parts + [jnp.zeros((half, spare), jnp.float32)], axis=1)


def unpack_grams(packed, vectors):
    upper = [packed[:, t * vectors : (t + 1) * vectors] for t in range(ITERS)]
    lower = [packed[:, (ITERS + t) * vectors : (ITERS + t + 1) * vectors] for t in range(ITERS)]
    return [jnp.concatenate(pair, axis=0) for pair in zip(upper, lower)]


def apply_kernel(step_at, *refs):
    last, opening = step_at == ITERS - 1, step_at == 0
    place_ref, count_ref, cols_ref, *refs = refs
    if opening:
        want_ref, *refs = refs
    tiles_at, held_ref, root_ref, own_ref, recv_ref, *refs = refs
    if opening:
        swapped_ref, swapped_next_ref, *refs = refs
        *refs, table = refs
        rest_ref = tiles_at
    else:
        edges_recv_ref, *refs, table, rest_ref, load_sem = refs
    held, per_row, side, _ = held_ref.shape
    blocks = held + rest_ref.shape[0]
    if not opening:
        rest_load = load(tiles_at, held, rest_ref, load_sem)
    if last:
        *before, applied_ref, gram_hbm, packed_ref, sem = refs
    else:
        if not opening:
            asked_ref, *refs = refs
        applied_ref, gram_ref, scaled_ref, out_hbm, edges_ref, *refs = refs
        if opening:
            asked_ref, *refs = refs
        picked_ref, sem = refs
    vectors = own_ref.shape[1]
    group = place_ref[0]
    slot = 0
    for b in range(blocks):
        split_into(own_ref[b], table, slot)
        slot += 1
    if opening:
        peers = recv_ref.shape[0]
        for p in range(peers):
            for c in range(SLOTS):
                at = jnp.clip(want_ref[c, p] - (group * peers + p) * blocks, 0, blocks - 1)
                split_into(recv_ref[p, at], table, slot)
                slot += 1
                entry = place_ref[1] * SLOTS + c
                asked_ref[p * SLOTS + c : p * SLOTS + c + 1] = recv_ref[
                    p, blocks + entry // vectors, pl.ds(entry % vectors, 1)
                ]
    else:
        for n in range(recv_ref.shape[0]):
            split_into(recv_ref[n], table, slot)
            slot += 1
    if opening:
        odd = group % 2 == 1
        for a_ref, b_ref in ((swapped_ref, swapped_next_ref), (swapped_next_ref, swapped_ref)):
            for h in range(RIM):
                split_into(jnp.where(odd, a_ref[h], b_ref[h]), table, slot)
                slot += 1
    else:
        below = jnp.maximum(group - 1, 0)
        above = jnp.minimum(group + 1, edges_recv_ref.shape[0] - 1)
        for at, first in ((below, RIM), (above, 0)):
            for h in range(RIM):
                split_into(edges_recv_ref[at, first + h], table, slot)
                slot += 1
    table[slot] = jnp.zeros(table.shape[1:], table.dtype)
    rows = []
    for b in range(blocks):
        picked = []
        for s in range(per_row):
            at = jnp.where(s < count_ref[b], cols_ref[b, s], slot)
            picked.append(table[at])
        x = jnp.concatenate(picked, axis=1)
        if b == held and not opening:
            rest_load.wait()
        tile_ref = held_ref.at[b] if b < held else rest_ref.at[b - held]
        t = jnp.concatenate([tile_ref[s] for s in range(per_row)], axis=1)
        product = lax.dot_general(x, t, NT, preferred_element_type=jnp.float32)
        total = product[(PIECES - 1) * vectors :]
        for piece in range(PIECES - 2, -1, -1):
            total = total + product[piece * vectors : (piece + 1) * vectors]
        root = root_ref[b]
        row = total * root
        applied_ref[b] = row
        rows.append(row)
        if not last:
            scaled_ref[b] = row * root
    if not last:
        pick_into(asked_ref, scaled_ref, picked_ref)
        send = pltpu.make_async_copy(picked_ref, out_hbm, sem)
        send.start()
        for h in range(RIM):
            edges_ref[h] = scaled_ref[h]
            edges_ref[RIM + h] = scaled_ref[blocks - RIM + h]
    flat = jnp.concatenate(rows, axis=1)
    gram = gram_of(flat)
    if last:
        packed = pack_grams([ref[...] for ref in before] + [gram])
        for n in range(packed_ref.shape[0]):
            packed_ref[n] = packed
        send = pltpu.make_async_copy(packed_ref, gram_hbm, sem)
        send.start()
        send.wait()
    else:
        gram_ref[...] = gram
        send.wait()


def finish_kernel(row_total, grams_ref, *refs):
    applied_refs, (out_hbm, trust_ref, out_ref, sems) = refs[:ITERS], refs[ITERS:]
    devices = grams_ref.shape[0]
    blocks, vectors = out_ref.shape[1:3]
    sends = [pltpu.make_async_copy(out_ref.at[t], out_hbm.at[t], sems.at[t]) for t in range(ITERS)]
    total = grams_ref[0]
    for n in range(1, devices):
        total = total + grams_ref[n]
    rows = lax.broadcasted_iota(jnp.int32, (vectors, vectors), 0)
    lanes = lax.broadcasted_iota(jnp.int32, (vectors, vectors), 1)
    unit = (rows == lanes).astype(jnp.float32)
    grams = unpack_grams(total, vectors)
    columns = [
        [jnp.broadcast_to(gram[:, k : k + 1], (vectors, vectors)) for k in range(vectors)]
        for gram in grams
    ]
    inverses = [unit] * ITERS
    for j in range(vectors):
        for t, column in enumerate(columns):
            ratio = jnp.where(rows > j, column[j] * (1.0 / column[j][j : j + 1]), 0.0)
            for k in range(j + 1, vectors):
                column[k] = column[k] - ratio * column[k][j : j + 1]
            inverses[t] = inverses[t] - ratio * inverses[t][j : j + 1]
    good = jnp.bool_(True)
    for t in range(ITERS):
        pivots = columns[t][0]
        for j in range(1, vectors):
            pivots = jnp.where(rows == j, columns[t][j], pivots)
        inverse = inverses[t] * lax.rsqrt(pivots / row_total)
        squares = jnp.sum(grams[t] * unit, axis=0, keepdims=True)
        norm = jnp.sum(inverse * inverse * squares) / row_total
        good = good & (norm < TRUST) & (jnp.min(squares) > TINY)
        left = [part.astype(jnp.float32) for part in pieces_of(inverse, 3)]
        left = jnp.concatenate([left[i] for i, _ in TERMS], axis=1).astype(jnp.bfloat16)
        for b in range(blocks):
            right = pieces_of(applied_refs[t][b], 3)
            right = jnp.concatenate([right[j] for _, j in TERMS], axis=0)
            out_ref[t, b] = jnp.dot(left, right, preferred_element_type=jnp.float32)
        sends[t].start()
    trust_ref[0] = good.astype(jnp.int32)
    for send in sends:
        send.wait()


def neighbours(scaled):
    count, blocks = lax.axis_size("group"), scaled.shape[0]
    up = [(i, i + 1) for i in range(count - 1)]
    down = [(i + 1, i) for i in range(count - 1)]
    low = lax.ppermute(scaled[blocks - RIM :], "group", up)
    high = lax.ppermute(scaled[:RIM], "group", down)
    return low, high


def swap(first, second):
    count = lax.axis_size("group")
    ups = [[(i, i + 1) for i in range(start, count - 1, 2)] for start in (0, 1)]
    pairs = [up + [(j, i) for i, j in up] for up in ups]
    return [lax.ppermute(x, "group", pair) for x, pair in zip((first, second), pairs)]


def stepwise(start_basis, tiles, tile_cols, tile_count, recv_list):
    groups, peers = lax.axis_size("group"), lax.axis_size("row")
    blocks, per_row, side, _ = tiles.shape
    vectors = start_basis.shape[1]
    row_total = groups * peers * blocks * side
    live = jnp.arange(per_row, dtype=jnp.int32)[None, :] < tile_count[:, None]
    live = live.astype(jnp.float32)
    wide = tiles.astype(jnp.float32)
    sums = jnp.einsum("btij,bt->bi", wide * wide, live, precision=HIGH)
    root = (1e-06 + sums) ** (-0.25)
    wanted = recv_list.reshape(peers * SLOTS)
    take = jnp.clip(wanted - lax.axis_index("group") * peers * blocks, 0, peers * blocks - 1)
    basis, results = start_basis, []
    for _ in range(ITERS):
        scaled = basis * root[:, None, :]
        low, high = neighbours(scaled)
        received = jnp.take(lax.all_gather(scaled, "row", axis=0, tiled=True), take, axis=0)
        extended = jnp.concatenate([scaled, received, low, high], axis=0)
        picked = jnp.take(extended, tile_cols, axis=0) * live[:, :, None, None]
        product = jnp.einsum(
            "btij,btkj->bki", tiles, picked, precision=HIGH, preferred_element_type=jnp.float32
        )
        applied = product * root[:, None, :]
        gram = jnp.einsum("bki,bli->kl", applied, applied, precision=HIGH)
        factor = jnp.linalg.cholesky(lax.psum(gram, ("group", "row")) / row_total)
        inverse = lax.linalg.triangular_solve(
            factor, jnp.eye(vectors, dtype=jnp.float32), left_side=True, lower=True
        )
        basis = jnp.einsum("kl,bli->bki", inverse, applied, precision=HIGH)
        results.append(basis)
    return jnp.stack(results)


def local(start_basis, tiles, tile_cols, tile_count, recv_list):
    groups, peers = lax.axis_size("group"), lax.axis_size("row")
    blocks, per_row, side, _ = tiles.shape
    vectors = start_basis.shape[1]
    place = jnp.stack([lax.axis_index("group"), lax.axis_index("row")]).astype(jnp.int32)
    wanted = jnp.transpose(recv_list.reshape(peers, SLOTS))
    lists = pl.cdiv(peers * SLOTS, vectors)
    tile_bytes = tiles.size * 2
    far_tiles = far(tiles)
    block_shape = (vectors, side)
    picked_shape = (peers * SLOTS,) + block_shape
    rim_shape = f32(RIM, *block_shape)
    kept = held_blocks(tiles)
    rest = pltpu.VMEM((blocks - kept,) + tiles.shape[1:], tiles.dtype)
    root, scaled, *rims, held, opening_rest = pl.pallas_call(
        roots_kernel,
        out_shape=(
            f32(blocks, 1, side),
            f32(blocks + lists, *block_shape),
            rim_shape,
            rim_shape,
            pltpu.VMEM((kept,) + tiles.shape[1:], tiles.dtype),
            rest,
        ),
        in_specs=[smem()] + [hbm()] * 4,
        out_specs=(vmem(),) * 6,
        scratch_shapes=[
            pltpu.SMEM((blocks,), jnp.int32),
            pltpu.SMEM((SLOTS, peers), jnp.int32),
            pltpu.VMEM((blocks,) + block_shape, jnp.float32),
            pltpu.SemaphoreType.DMA((5,)),
        ],
        compiler_params=params(),
        cost_estimate=cost(tiles.size * 2, tile_bytes),
        name="roots",
    )(place, far(tile_count), far(wanted), far_tiles, far(start_basis))
    slots = blocks + peers * SLOTS + 2 * RIM
    powers, grams = [], []
    for t in range(ITERS):
        last = t == ITERS - 1
        if t == 0:
            beside = swap(*rims)
            received = lax.all_gather(scaled, "row", axis=0)
        else:
            received = lax.all_to_all(outgoing, "row", 0, 0, tiled=True)
            beside = [lax.all_gather(edges, "group", axis=0)]
        scalars = [place, tile_count, tile_cols] + ([wanted] if t == 0 else [])
        arrays = [far_tiles if t else opening_rest, held, root, scaled, received, *beside]
        shapes = [f32(blocks, *block_shape)]
        specs = [vmem(), vmem()]
        if last:
            shapes += [pltpu.HBM((groups * peers, vectors // 2, LANES), jnp.float32)]
            specs = [vmem(), hbm()]
            scratch = [
                pltpu.VMEM((groups * peers, vectors // 2, LANES), jnp.float32),
                pltpu.SemaphoreType.DMA,
            ]
            arrays += grams
        else:
            shapes += [f32(vectors, vectors), f32(blocks, *block_shape), pltpu.HBM(picked_shape, jnp.float32)]
            shapes += [f32(2 * RIM, *block_shape)]
            specs += [vmem(), hbm(), vmem()]
            scratch = [pltpu.VMEM(picked_shape, jnp.float32), pltpu.SemaphoreType.DMA]
            if t:
                arrays += [asked]
            else:
                shapes += [f32(peers * SLOTS, side)]
                specs += [vmem()]
        result = pl.pallas_call(
            functools.partial(apply_kernel, t),
            out_shape=tuple(shapes),
            in_specs=[smem()] * len(scalars)
            + [hbm() if t else vmem()]
            + [vmem()] * (len(arrays) - 1),
            out_specs=tuple(specs),
            scratch_shapes=scratch
            + [
                pltpu.VMEM((slots + 1, PIECES * vectors, side), jnp.bfloat16),
            ]
            + ([rest, pltpu.SemaphoreType.DMA] if t else []),
            compiler_params=params(),
            cost_estimate=cost(tiles.size * 2 * vectors * PIECES, tile_bytes),
            name="apply_last" if last else "apply",
        )(*scalars, *arrays)
        powers.append(result[0])
        grams.append(result[1])
        if not last:
            scaled, outgoing, edges = result[2:5]
            if t == 0:
                asked = result[5]
    gathered = lax.all_to_all(grams[-1], ("group", "row"), 0, 0, tiled=True)
    krylov, trust = pl.pallas_call(
        functools.partial(finish_kernel, float(groups * peers * blocks * side)),
        out_shape=(pltpu.HBM((ITERS, blocks, vectors, side), jnp.float32), jax.ShapeDtypeStruct((1,), jnp.int32)),
        in_specs=[vmem()] * (1 + ITERS),
        out_specs=(hbm(), smem()),
        scratch_shapes=[
            pltpu.VMEM((ITERS, blocks, vectors, side), jnp.float32),
            pltpu.SemaphoreType.DMA((ITERS,)),
        ],
        compiler_params=params(),
        name="finish",
    )(gathered, *powers)
    return lax.cond(
        trust[0] > 0,
        lambda *_: krylov,
        stepwise,
        start_basis, tiles, tile_cols, tile_count, recv_list,
    )


def solution(mesh):
    placed = (
        P(("group", "row"), None, None),
        P(("group", "row"), None, None, None),
        P(("group", "row"), None),
        P(("group", "row")),
        P("group", "row", None, None),
    )
    return jax.shard_map(
        local,
        mesh=mesh,
        in_specs=placed,
        out_specs=P(None, ("group", "row"), None, None),
        check_vma=False,
    )
```

```python
import functools

import jax
import jax.numpy as jnp
from jax import lax
from jax.experimental import pallas as pl
from jax.experimental.pallas import tpu as pltpu
from jax.sharding import PartitionSpec as P

SLOTS = 2
RIM = 2
ITERS = 3
MINLIVE = 10
LANES = 128
HELD_BYTES = 5 * 1024 * 1024 // 2
PIECES = 2
VMEM_BYTES = 24 * 1024 * 1024
TRUST = 64.0
TINY = 1e-25

HIGH = lax.Precision.HIGHEST
NT = (((1,), (1,)), ((), ()))


def vmem():
    return pl.BlockSpec(memory_space=pltpu.VMEM)


def smem():
    return pl.BlockSpec(memory_space=pltpu.SMEM)


def hbm():
    return pl.BlockSpec(memory_space=pltpu.HBM)


def far(x):
    return pltpu.with_memory_space_constraint(x, pltpu.HBM)


def f32(*shape):
    return jax.ShapeDtypeStruct(shape, jnp.float32)


def params():
    return pltpu.CompilerParams(vmem_limit_bytes=VMEM_BYTES)


def cost(flops, moved):
    return pl.CostEstimate(flops=flops, bytes_accessed=moved, transcendentals=0)


def held_blocks(tiles):
    return min(tiles.shape[0] - 1, HELD_BYTES // (tiles.size // tiles.shape[0] * 2))


def load(tiles_hbm, start, tiles_ref, sem):
    copy = pltpu.make_async_copy(tiles_hbm.at[pl.ds(start, tiles_ref.shape[0])], tiles_ref, sem)
    copy.start()
    return copy


def tile(ref, at):
    side = ref.shape[1]
    return ref[at * side : (at + 1) * side]


def roots_kernel(per_row, place_ref, count_hbm, want_hbm, tiles_hbm, basis_hbm, root_ref, sent_ref,
                 first_ref, second_ref, held_ref, rest_ref, count_ref, want_ref, basis_ref, sems):
    blocks, vectors, side = basis_ref.shape
    held = held_ref.shape[0] // (per_row * side)
    peers = want_ref.shape[1]
    rest_load = load(tiles_hbm, held_ref.shape[0], rest_ref, sems.at[3])
    small = [
        pltpu.make_async_copy(source, target, sems.at[n])
        for n, (source, target) in enumerate(
            ((count_hbm, count_ref), (want_hbm, want_ref), (basis_hbm, basis_ref))
        )
    ]
    for copy in small:
        copy.start()
    held_load = load(tiles_hbm, 0, held_ref, sems.at[4])
    for copy in small:
        copy.wait()
    for p in range(peers):
        owned = (place_ref[0] * peers + p) * blocks
        for c in range(SLOTS):
            at = jnp.full((1, side), want_ref[c, p] - owned, jnp.int32).astype(jnp.float32)
            block, row = divmod(p * SLOTS + c, vectors)
            sent_ref[blocks + block, row : row + 1] = at
    rest_load.wait()
    for b in list(range(held, blocks)) + list(range(held)):
        if b == 0:
            held_load.wait()
        tile_ref, first = (held_ref, b * per_row) if b < held else (rest_ref, (b - held) * per_row)
        total = jnp.zeros((side, side), jnp.float32)
        for s in range(per_row):
            wide = tile(tile_ref, first + s).astype(jnp.float32)
            square = wide * wide
            if s >= MINLIVE:
                square = square * (s < count_ref[b]).astype(jnp.float32)
            total = total + square
        sums = jnp.sum(total.T, axis=0, keepdims=True)
        root = lax.rsqrt(jnp.sqrt(1e-06 + sums))
        root_ref[b] = root
        sent_ref[b] = basis_ref[b] * root
    swaps_into(place_ref[0], blocks, sent_ref, first_ref, second_ref)


def swaps_into(group, blocks, scaled_ref, first_ref, second_ref):
    odd = group % 2
    for h in range(RIM):
        first_ref[h] = scaled_ref[(1 - odd) * (blocks - RIM) + h]
        second_ref[h] = scaled_ref[odd * (blocks - RIM) + h]


def pick_into(asked_ref, scaled_ref, out_ref):
    blocks, vectors, side = scaled_ref.shape
    for n in range(asked_ref.shape[0]):
        at = jnp.broadcast_to(asked_ref[n : n + 1], (vectors, side))
        value = scaled_ref[0]
        for b in range(1, blocks):
            value = jnp.where(at == float(b), scaled_ref[b], value)
        out_ref[n] = value


def pieces_of(x, count):
    parts = []
    for n in range(count):
        part = x.astype(jnp.bfloat16)
        parts.append(part)
        if n < count - 1:
            x = x - part.astype(jnp.float32)
    return parts


def split_into(x, out_ref, slot):
    vectors = x.shape[0]
    for n, part in enumerate(pieces_of(x, PIECES)):
        out_ref[slot, pl.ds(n * vectors, vectors)] = part


def gram_of(flat):
    k = flat.shape[0]
    stack = jnp.concatenate(pieces_of(flat, 3), axis=0)
    full = lax.dot_general(stack, stack, NT, preferred_element_type=jnp.float32)
    term = lambda i, j: full[i * k : (i + 1) * k, j * k : (j + 1) * k]
    small = term(1, 1) + (term(0, 2) + term(2, 0))
    return term(0, 0) + ((term(0, 1) + term(1, 0)) + small)


TERMS = ((0, 0), (0, 1), (1, 0), (1, 1), (0, 2), (2, 0))


def pack_grams(grams):
    half = grams[0].shape[0] // 2
    parts = [g[:half] for g in grams] + [g[half:] for g in grams]
    spare = LANES - len(parts) * grams[0].shape[1]
    return jnp.concatenate(parts + [jnp.zeros((half, spare), jnp.float32)], axis=1)


def unpack_grams(packed, vectors):
    upper = [packed[:, t * vectors : (t + 1) * vectors] for t in range(ITERS)]
    lower = [packed[:, (ITERS + t) * vectors : (ITERS + t + 1) * vectors] for t in range(ITERS)]
    return [jnp.concatenate(pair, axis=0) for pair in zip(upper, lower)]


def apply_kernel(step_at, *refs):
    last, opening = step_at == ITERS - 1, step_at == 0
    place_ref, count_ref, cols_ref, *refs = refs
    if opening:
        want_ref, *refs = refs
    tiles_at, held_ref, root_ref, own_ref, recv_ref, swapped_ref, swapped_next_ref, *refs = refs
    if opening:
        *refs, table = refs
        rest_ref = tiles_at
    else:
        *refs, table, rest_ref, load_sem = refs
    blocks, _, side = root_ref.shape
    per_row = cols_ref.shape[1]
    held = held_ref.shape[0] // (per_row * side)
    if not opening:
        rest_load = load(tiles_at, held_ref.shape[0], rest_ref, load_sem)
    if last:
        *before, applied_ref, gram_hbm, packed_ref, sem = refs
    else:
        if not opening:
            asked_ref, *refs = refs
        applied_ref, gram_ref, scaled_ref, out_hbm, first_ref, second_ref, *refs = refs
        if opening:
            asked_ref, *refs = refs
        picked_ref, sem = refs
    vectors = own_ref.shape[1]
    group = place_ref[0]
    slot = 0
    for b in range(blocks):
        split_into(own_ref[b], table, slot)
        slot += 1
    if opening:
        peers = recv_ref.shape[0]
        for p in range(peers):
            for c in range(SLOTS):
                at = jnp.clip(want_ref[c, p] - (group * peers + p) * blocks, 0, blocks - 1)
                split_into(recv_ref[p, at], table, slot)
                slot += 1
                entry = place_ref[1] * SLOTS + c
                asked_ref[p * SLOTS + c : p * SLOTS + c + 1] = recv_ref[
                    p, blocks + entry // vectors, pl.ds(entry % vectors, 1)
                ]
    else:
        for n in range(recv_ref.shape[0]):
            split_into(recv_ref[n], table, slot)
            slot += 1
    odd = group % 2 == 1
    for a_ref, b_ref in ((swapped_ref, swapped_next_ref), (swapped_next_ref, swapped_ref)):
        for h in range(RIM):
            split_into(jnp.where(odd, a_ref[h], b_ref[h]), table, slot)
            slot += 1
    table[slot] = jnp.zeros(table.shape[1:], table.dtype)
    rows = []
    for b in range(blocks):
        picked = []
        for s in range(per_row):
            at = jnp.where(s < count_ref[b], cols_ref[b, s], slot)
            picked.append(table[at])
        x = jnp.concatenate(picked, axis=1)
        if b == held and not opening:
            rest_load.wait()
        tile_ref, first = (held_ref, b * per_row) if b < held else (rest_ref, (b - held) * per_row)
        t = jnp.concatenate([tile(tile_ref, first + s) for s in range(per_row)], axis=1)
        product = lax.dot_general(x, t, NT, preferred_element_type=jnp.float32)
        total = product[(PIECES - 1) * vectors :]
        for piece in range(PIECES - 2, -1, -1):
            total = total + product[piece * vectors : (piece + 1) * vectors]
        root = root_ref[b]
        row = total * root
        applied_ref[b] = row
        rows.append(row)
        if not last:
            scaled_ref[b] = row * root
    if not last:
        pick_into(asked_ref, scaled_ref, picked_ref)
        send = pltpu.make_async_copy(picked_ref, out_hbm, sem)
        send.start()
        swaps_into(group, blocks, scaled_ref, first_ref, second_ref)
    flat = jnp.concatenate(rows, axis=1)
    gram = gram_of(flat)
    if last:
        packed = pack_grams([ref[...] for ref in before] + [gram])
        for n in range(packed_ref.shape[0]):
            packed_ref[n] = packed
        send = pltpu.make_async_copy(packed_ref, gram_hbm, sem)
        send.start()
        send.wait()
    else:
        gram_ref[...] = gram
        send.wait()


def finish_kernel(row_total, grams_ref, *refs):
    applied_refs, (out_hbm, trust_ref, out_ref, sems) = refs[:ITERS], refs[ITERS:]
    devices = grams_ref.shape[0]
    blocks, vectors = out_ref.shape[1:3]
    sends = [pltpu.make_async_copy(out_ref.at[t], out_hbm.at[t], sems.at[t]) for t in range(ITERS)]
    total = grams_ref[0]
    for n in range(1, devices):
        total = total + grams_ref[n]
    rows = lax.broadcasted_iota(jnp.int32, (vectors, vectors), 0)
    lanes = lax.broadcasted_iota(jnp.int32, (vectors, vectors), 1)
    unit = (rows == lanes).astype(jnp.float32)
    grams = unpack_grams(total, vectors)
    columns = [
        [jnp.broadcast_to(gram[:, k : k + 1], (vectors, vectors)) for k in range(vectors)]
        for gram in grams
    ]
    inverses = [unit] * ITERS
    for j in range(vectors):
        for t, column in enumerate(columns):
            ratio = jnp.where(rows > j, column[j] * (1.0 / column[j][j : j + 1]), 0.0)
            for k in range(j + 1, vectors):
                column[k] = column[k] - ratio * column[k][j : j + 1]
            inverses[t] = inverses[t] - ratio * inverses[t][j : j + 1]
    good = jnp.bool_(True)
    for t in range(ITERS):
        pivots = columns[t][0]
        for j in range(1, vectors):
            pivots = jnp.where(rows == j, columns[t][j], pivots)
        inverse = inverses[t] * lax.rsqrt(pivots / row_total)
        squares = jnp.sum(grams[t] * unit, axis=0, keepdims=True)
        norm = jnp.sum(inverse * inverse * squares) / row_total
        good = good & (norm < TRUST) & (jnp.min(squares) > TINY)
        left = [part.astype(jnp.float32) for part in pieces_of(inverse, 3)]
        left = jnp.concatenate([left[i] for i, _ in TERMS], axis=1).astype(jnp.bfloat16)
        for b in range(blocks):
            right = pieces_of(applied_refs[t][b], 3)
            right = jnp.concatenate([right[j] for _, j in TERMS], axis=0)
            out_ref[t, b] = jnp.dot(left, right, preferred_element_type=jnp.float32)
        sends[t].start()
    trust_ref[0] = good.astype(jnp.int32)
    for send in sends:
        send.wait()


def neighbours(scaled):
    count, blocks = lax.axis_size("group"), scaled.shape[0]
    up = [(i, i + 1) for i in range(count - 1)]
    down = [(i + 1, i) for i in range(count - 1)]
    low = lax.ppermute(scaled[blocks - RIM :], "group", up)
    high = lax.ppermute(scaled[:RIM], "group", down)
    return low, high


def swap(first, second):
    count = lax.axis_size("group")
    ups = [[(i, i + 1) for i in range(start, count - 1, 2)] for start in (0, 1)]
    pairs = [up + [(j, i) for i, j in up] for up in ups]
    return [lax.ppermute(x, "group", pair) for x, pair in zip((first, second), pairs)]


def stepwise(start_basis, tiles, tile_cols, tile_count, recv_list):
    groups, peers = lax.axis_size("group"), lax.axis_size("row")
    blocks, per_row, side, _ = tiles.shape
    vectors = start_basis.shape[1]
    row_total = groups * peers * blocks * side
    live = jnp.arange(per_row, dtype=jnp.int32)[None, :] < tile_count[:, None]
    live = live.astype(jnp.float32)
    wide = tiles.astype(jnp.float32)
    sums = jnp.einsum("btij,bt->bi", wide * wide, live, precision=HIGH)
    root = (1e-06 + sums) ** (-0.25)
    wanted = recv_list.reshape(peers * SLOTS)
    take = jnp.clip(wanted - lax.axis_index("group") * peers * blocks, 0, peers * blocks - 1)
    basis, results = start_basis, []
    for _ in range(ITERS):
        scaled = basis * root[:, None, :]
        low, high = neighbours(scaled)
        received = jnp.take(lax.all_gather(scaled, "row", axis=0, tiled=True), take, axis=0)
        extended = jnp.concatenate([scaled, received, low, high], axis=0)
        picked = jnp.take(extended, tile_cols, axis=0) * live[:, :, None, None]
        product = jnp.einsum(
            "btij,btkj->bki", tiles, picked, precision=HIGH, preferred_element_type=jnp.float32
        )
        applied = product * root[:, None, :]
        gram = jnp.einsum("bki,bli->kl", applied, applied, precision=HIGH)
        factor = jnp.linalg.cholesky(lax.psum(gram, ("group", "row")) / row_total)
        inverse = lax.linalg.triangular_solve(
            factor, jnp.eye(vectors, dtype=jnp.float32), left_side=True, lower=True
        )
        basis = jnp.einsum("kl,bli->bki", inverse, applied, precision=HIGH)
        results.append(basis)
    return jnp.stack(results)


def local(start_basis, tiles, tile_cols, tile_count, recv_list):
    groups, peers = lax.axis_size("group"), lax.axis_size("row")
    blocks, per_row, side, _ = tiles.shape
    vectors = start_basis.shape[1]
    place = jnp.stack([lax.axis_index("group"), lax.axis_index("row")]).astype(jnp.int32)
    wanted = jnp.transpose(recv_list.reshape(peers, SLOTS))
    lists = pl.cdiv(peers * SLOTS, vectors)
    tile_bytes = tiles.size * 2
    far_tiles = far(tiles.reshape(-1, side))
    block_shape = (vectors, side)
    picked_shape = (peers * SLOTS,) + block_shape
    rim_shape = f32(RIM, *block_shape)
    kept = held_blocks(tiles)
    rest = pltpu.VMEM(((blocks - kept) * per_row * side, side), tiles.dtype)
    root, scaled, *rims, held, opening_rest = pl.pallas_call(
        functools.partial(roots_kernel, per_row),
        out_shape=(
            f32(blocks, 1, side),
            f32(blocks + lists, *block_shape),
            rim_shape,
            rim_shape,
            pltpu.VMEM((kept * per_row * side, side), tiles.dtype),
            rest,
        ),
        in_specs=[smem()] + [hbm()] * 4,
        out_specs=(vmem(),) * 6,
        scratch_shapes=[
            pltpu.SMEM((blocks,), jnp.int32),
            pltpu.SMEM((SLOTS, peers), jnp.int32),
            pltpu.VMEM((blocks,) + block_shape, jnp.float32),
            pltpu.SemaphoreType.DMA((5,)),
        ],
        compiler_params=params(),
        cost_estimate=cost(tiles.size * 2, tile_bytes),
        name="roots",
    )(place, far(tile_count), far(wanted), far_tiles, far(start_basis))
    slots = blocks + peers * SLOTS + 2 * RIM
    powers, grams = [], []
    for t in range(ITERS):
        last = t == ITERS - 1
        if t == 0:
            beside = swap(*rims)
            received = lax.all_gather(scaled, "row", axis=0)
        else:
            received = lax.all_to_all(outgoing, "row", 0, 0, tiled=True)
            beside = swap(*rims)
        scalars = [place, tile_count, tile_cols] + ([wanted] if t == 0 else [])
        arrays = [far_tiles if t else opening_rest, held, root, scaled, received, *beside]
        shapes = [f32(blocks, *block_shape)]
        specs = [vmem(), vmem()]
        if last:
            shapes += [pltpu.HBM((groups * peers, vectors // 2, LANES), jnp.float32)]
            specs = [vmem(), hbm()]
            scratch = [
                pltpu.VMEM((groups * peers, vectors // 2, LANES), jnp.float32),
                pltpu.SemaphoreType.DMA,
            ]
            arrays += grams
        else:
            shapes += [f32(vectors, vectors), f32(blocks, *block_shape), pltpu.HBM(picked_shape, jnp.float32)]
            shapes += [rim_shape] * 2
            specs += [vmem(), hbm(), vmem(), vmem()]
            scratch = [pltpu.VMEM(picked_shape, jnp.float32), pltpu.SemaphoreType.DMA]
            if t:
                arrays += [asked]
            else:
                shapes += [f32(peers * SLOTS, side)]
                specs += [vmem()]
        result = pl.pallas_call(
            functools.partial(apply_kernel, t),
            out_shape=tuple(shapes),
            in_specs=[smem()] * len(scalars)
            + [hbm() if t else vmem()]
            + [vmem()] * (len(arrays) - 1),
            out_specs=tuple(specs),
            scratch_shapes=scratch
            + [
                pltpu.VMEM((slots + 1, PIECES * vectors, side), jnp.bfloat16),
            ]
            + ([rest, pltpu.SemaphoreType.DMA] if t else []),
            compiler_params=params(),
            cost_estimate=cost(tiles.size * 2 * vectors * PIECES, tile_bytes),
            name="apply_last" if last else "apply",
        )(*scalars, *arrays)
        powers.append(result[0])
        grams.append(result[1])
        if not last:
            scaled, outgoing, *rims = result[2:6]
            if t == 0:
                asked = result[6]
    gathered = lax.all_to_all(grams[-1], ("group", "row"), 0, 0, tiled=True)
    krylov, trust = pl.pallas_call(
        functools.partial(finish_kernel, float(groups * peers * blocks * side)),
        out_shape=(pltpu.HBM((ITERS, blocks, vectors, side), jnp.float32), jax.ShapeDtypeStruct((1,), jnp.int32)),
        in_specs=[vmem()] * (1 + ITERS),
        out_specs=(hbm(), smem()),
        scratch_shapes=[
            pltpu.VMEM((ITERS, blocks, vectors, side), jnp.float32),
            pltpu.SemaphoreType.DMA((ITERS,)),
        ],
        compiler_params=params(),
        name="finish",
    )(gathered, *powers)
    return lax.cond(
        trust[0] > 0,
        lambda *_: krylov,
        stepwise,
        start_basis, tiles, tile_cols, tile_count, recv_list,
    )


def solution(mesh):
    placed = (
        P(("group", "row"), None, None),
        P(("group", "row"), None, None, None),
        P(("group", "row"), None),
        P(("group", "row")),
        P("group", "row", None, None),
    )
    return jax.shard_map(
        local,
        mesh=mesh,
        in_specs=placed,
        out_specs=P(None, ("group", "row"), None, None),
        check_vma=False,
    )
```

```python
import functools

import jax
import jax.numpy as jnp
from jax import lax
from jax.experimental import pallas as pl
from jax.experimental.pallas import tpu as pltpu
from jax.sharding import PartitionSpec as P

SLOTS = 2
RIM = 2
ITERS = 3
MINLIVE = 10
LANES = 128
HELD_BYTES = 5 * 1024 * 1024 // 2
PIECES = 2
VMEM_BYTES = 24 * 1024 * 1024
TRUST = 64.0
TINY = 1e-25

HIGH = lax.Precision.HIGHEST
NT = (((1,), (1,)), ((), ()))


def vmem():
    return pl.BlockSpec(memory_space=pltpu.VMEM)


def smem():
    return pl.BlockSpec(memory_space=pltpu.SMEM)


def hbm():
    return pl.BlockSpec(memory_space=pltpu.HBM)


def far(x):
    return pltpu.with_memory_space_constraint(x, pltpu.HBM)


def f32(*shape):
    return jax.ShapeDtypeStruct(shape, jnp.float32)


def params():
    return pltpu.CompilerParams(vmem_limit_bytes=VMEM_BYTES)


def cost(flops, moved):
    return pl.CostEstimate(flops=flops, bytes_accessed=moved, transcendentals=0)


def held_blocks(tiles):
    return min(tiles.shape[0] - 1, HELD_BYTES // (tiles.size // tiles.shape[0] * 2))


def load(tiles_hbm, start, tiles_ref, sem):
    copy = pltpu.make_async_copy(tiles_hbm.at[pl.ds(start, tiles_ref.shape[0])], tiles_ref, sem)
    copy.start()
    return copy


def start_all(pairs, sems):
    copies = [
        pltpu.make_async_copy(source, target, sems.at[n])
        for n, (source, target) in enumerate(pairs)
    ]
    for copy in copies:
        copy.start()
    return copies


def tile(ref, at):
    side = ref.shape[1]
    return ref[at * side : (at + 1) * side]


def roots_kernel(per_row, count_hbm, want_hbm, tiles_hbm, basis_hbm, root_ref, sent_ref,
                 first_ref, second_ref, held_ref, rest_ref, count_ref, want_ref, basis_ref, sems):
    blocks, vectors, side = basis_ref.shape
    held = held_ref.shape[0] // (per_row * side)
    peers = want_ref.shape[1]
    group = lax.axis_index("group")
    rest_load = load(tiles_hbm, held_ref.shape[0], rest_ref, sems.at[3])
    small = start_all(((count_hbm, count_ref), (want_hbm, want_ref), (basis_hbm, basis_ref)), sems)
    held_load = load(tiles_hbm, 0, held_ref, sems.at[4])
    for copy in small:
        copy.wait()
    for p in range(peers):
        owned = (group * peers + p) * blocks
        for c in range(SLOTS):
            at = jnp.full((1, side), want_ref[c, p] - owned, jnp.int32).astype(jnp.float32)
            block, row = divmod(p * SLOTS + c, vectors)
            sent_ref[blocks + block, row : row + 1] = at
    rest_load.wait()
    for b in list(range(held, blocks)) + list(range(held)):
        if b == 0:
            held_load.wait()
        tile_ref, first = (held_ref, b * per_row) if b < held else (rest_ref, (b - held) * per_row)
        total = jnp.zeros((side, side), jnp.float32)
        for s in range(per_row):
            wide = tile(tile_ref, first + s).astype(jnp.float32)
            square = wide * wide
            if s >= MINLIVE:
                square = square * (s < count_ref[b]).astype(jnp.float32)
            total = total + square
        sums = jnp.sum(total.T, axis=0, keepdims=True)
        root = lax.rsqrt(jnp.sqrt(1e-06 + sums))
        root_ref[b] = root
        sent_ref[b] = basis_ref[b] * root
    swaps_into(group, blocks, sent_ref, first_ref, second_ref)


def swaps_into(group, blocks, scaled_ref, first_ref, second_ref):
    odd = group % 2
    for h in range(RIM):
        first_ref[h] = scaled_ref[(1 - odd) * (blocks - RIM) + h]
        second_ref[h] = scaled_ref[odd * (blocks - RIM) + h]


def pick_into(asked_ref, scaled_ref, out_ref):
    blocks, vectors, side = scaled_ref.shape
    for n in range(asked_ref.shape[0]):
        at = jnp.broadcast_to(asked_ref[n : n + 1], (vectors, side))
        value = scaled_ref[0]
        for b in range(1, blocks):
            value = jnp.where(at == float(b), scaled_ref[b], value)
        out_ref[n] = value


def pieces_of(x, count):
    parts = []
    for n in range(count):
        part = x.astype(jnp.bfloat16)
        parts.append(part)
        if n < count - 1:
            x = x - part.astype(jnp.float32)
    return parts


def split_into(x, out_ref, slot):
    vectors = x.shape[0]
    for n, part in enumerate(pieces_of(x, PIECES)):
        out_ref[slot, pl.ds(n * vectors, vectors)] = part


def gram_of(flat):
    k = flat.shape[0]
    stack = jnp.concatenate(pieces_of(flat, 3), axis=0)
    full = lax.dot_general(stack, stack, NT, preferred_element_type=jnp.float32)
    term = lambda i, j: full[i * k : (i + 1) * k, j * k : (j + 1) * k]
    small = term(1, 1) + (term(0, 2) + term(2, 0))
    return term(0, 0) + ((term(0, 1) + term(1, 0)) + small)


TERMS = ((0, 0), (0, 1), (1, 0), (1, 1), (0, 2), (2, 0))


def pack_grams(grams):
    half = grams[0].shape[0] // 2
    parts = [g[:half] for g in grams] + [g[half:] for g in grams]
    spare = LANES - len(parts) * grams[0].shape[1]
    return jnp.concatenate(parts + [jnp.zeros((half, spare), jnp.float32)], axis=1)


def unpack_grams(packed, vectors):
    upper = [packed[:, t * vectors : (t + 1) * vectors] for t in range(ITERS)]
    lower = [packed[:, (ITERS + t) * vectors : (ITERS + t + 1) * vectors] for t in range(ITERS)]
    return [jnp.concatenate(pair, axis=0) for pair in zip(upper, lower)]


def apply_kernel(step_at, *refs):
    last, opening = step_at == ITERS - 1, step_at == 0
    scalars = 3 if opening else 2
    scalars_hbm, refs = refs[:scalars], refs[scalars:]
    tiles_at, held_ref, root_ref, own_ref, recv_ref, swapped_ref, swapped_next_ref, *refs = refs
    *refs, scalar_sems = refs
    scalar_refs, refs = refs[-scalars:], refs[:-scalars]
    count_ref, cols_ref = scalar_refs[:2]
    if opening:
        want_ref = scalar_refs[2]
        *refs, table = refs
        rest_ref = tiles_at
    else:
        *refs, table, rest_ref, load_sem = refs
        rest_load = load(tiles_at, held_ref.shape[0], rest_ref, load_sem)
    small = start_all(zip(scalars_hbm, scalar_refs), scalar_sems)
    blocks, _, side = root_ref.shape
    per_row = cols_ref.shape[1]
    held = held_ref.shape[0] // (per_row * side)
    if last:
        *before, applied_ref, gram_hbm, packed_ref, sem = refs
    else:
        if not opening:
            asked_ref, *refs = refs
        applied_ref, gram_ref, scaled_ref, out_hbm, first_ref, second_ref, *refs = refs
        if opening:
            asked_ref, *refs = refs
        picked_ref, sem = refs
    vectors = own_ref.shape[1]
    group = lax.axis_index("group")
    slot = 0
    for b in range(blocks):
        split_into(own_ref[b], table, slot)
        slot += 1
    for copy in small:
        copy.wait()
    if opening:
        peers = recv_ref.shape[0]
        for p in range(peers):
            for c in range(SLOTS):
                at = jnp.clip(want_ref[c, p] - (group * peers + p) * blocks, 0, blocks - 1)
                split_into(recv_ref[p, at], table, slot)
                slot += 1
                entry = lax.axis_index("row") * SLOTS + c
                asked_ref[p * SLOTS + c : p * SLOTS + c + 1] = recv_ref[
                    p, blocks + entry // vectors, pl.ds(entry % vectors, 1)
                ]
    else:
        for n in range(recv_ref.shape[0]):
            split_into(recv_ref[n], table, slot)
            slot += 1
    odd = group % 2 == 1
    for a_ref, b_ref in ((swapped_ref, swapped_next_ref), (swapped_next_ref, swapped_ref)):
        for h in range(RIM):
            split_into(jnp.where(odd, a_ref[h], b_ref[h]), table, slot)
            slot += 1
    table[slot] = jnp.zeros(table.shape[1:], table.dtype)
    rows = []
    for b in range(blocks):
        picked = []
        for s in range(per_row):
            at = jnp.where(s < count_ref[b], cols_ref[b, s], slot)
            picked.append(table[at])
        x = jnp.concatenate(picked, axis=1)
        if b == held and not opening:
            rest_load.wait()
        tile_ref, first = (held_ref, b * per_row) if b < held else (rest_ref, (b - held) * per_row)
        t = jnp.concatenate([tile(tile_ref, first + s) for s in range(per_row)], axis=1)
        product = lax.dot_general(x, t, NT, preferred_element_type=jnp.float32)
        total = product[(PIECES - 1) * vectors :]
        for piece in range(PIECES - 2, -1, -1):
            total = total + product[piece * vectors : (piece + 1) * vectors]
        root = root_ref[b]
        row = total * root
        applied_ref[b] = row
        rows.append(row)
        if not last:
            scaled_ref[b] = row * root
    if not last:
        pick_into(asked_ref, scaled_ref, picked_ref)
        send = pltpu.make_async_copy(picked_ref, out_hbm, sem)
        send.start()
        swaps_into(group, blocks, scaled_ref, first_ref, second_ref)
    flat = jnp.concatenate(rows, axis=1)
    gram = gram_of(flat)
    if last:
        packed = pack_grams([ref[...] for ref in before] + [gram])
        for n in range(packed_ref.shape[0]):
            packed_ref[n] = packed
        send = pltpu.make_async_copy(packed_ref, gram_hbm, sem)
        send.start()
        send.wait()
    else:
        gram_ref[...] = gram
        send.wait()


def finish_kernel(row_total, grams_ref, *refs):
    applied_refs, (out_hbm, trust_ref, out_ref, sems) = refs[:ITERS], refs[ITERS:]
    devices = grams_ref.shape[0]
    blocks, vectors = out_ref.shape[1:3]
    sends = [pltpu.make_async_copy(out_ref.at[t], out_hbm.at[t], sems.at[t]) for t in range(ITERS)]
    total = grams_ref[0]
    for n in range(1, devices):
        total = total + grams_ref[n]
    rows = lax.broadcasted_iota(jnp.int32, (vectors, vectors), 0)
    lanes = lax.broadcasted_iota(jnp.int32, (vectors, vectors), 1)
    unit = (rows == lanes).astype(jnp.float32)
    grams = unpack_grams(total, vectors)
    columns = [
        [jnp.broadcast_to(gram[:, k : k + 1], (vectors, vectors)) for k in range(vectors)]
        for gram in grams
    ]
    inverses = [unit] * ITERS
    for j in range(vectors):
        for t, column in enumerate(columns):
            ratio = jnp.where(rows > j, column[j] * (1.0 / column[j][j : j + 1]), 0.0)
            for k in range(j + 1, vectors):
                column[k] = column[k] - ratio * column[k][j : j + 1]
            inverses[t] = inverses[t] - ratio * inverses[t][j : j + 1]
    good = jnp.bool_(True)
    for t in range(ITERS):
        pivots = columns[t][0]
        for j in range(1, vectors):
            pivots = jnp.where(rows == j, columns[t][j], pivots)
        inverse = inverses[t] * lax.rsqrt(pivots / row_total)
        squares = jnp.sum(grams[t] * unit, axis=0, keepdims=True)
        norm = jnp.sum(inverse * inverse * squares) / row_total
        good = good & (norm < TRUST) & (jnp.min(squares) > TINY)
        left = [part.astype(jnp.float32) for part in pieces_of(inverse, 3)]
        left = jnp.concatenate([left[i] for i, _ in TERMS], axis=1).astype(jnp.bfloat16)
        for b in range(blocks):
            right = pieces_of(applied_refs[t][b], 3)
            right = jnp.concatenate([right[j] for _, j in TERMS], axis=0)
            out_ref[t, b] = jnp.dot(left, right, preferred_element_type=jnp.float32)
        sends[t].start()
    trust_ref[0] = good.astype(jnp.int32)
    for send in sends:
        send.wait()


def neighbours(scaled):
    count, blocks = lax.axis_size("group"), scaled.shape[0]
    up = [(i, i + 1) for i in range(count - 1)]
    down = [(i + 1, i) for i in range(count - 1)]
    low = lax.ppermute(scaled[blocks - RIM :], "group", up)
    high = lax.ppermute(scaled[:RIM], "group", down)
    return low, high


def swap(first, second):
    count = lax.axis_size("group")
    ups = [[(i, i + 1) for i in range(start, count - 1, 2)] for start in (0, 1)]
    pairs = [up + [(j, i) for i, j in up] for up in ups]
    return [lax.ppermute(x, "group", pair) for x, pair in zip((first, second), pairs)]


def stepwise(start_basis, tiles, tile_cols, tile_count, recv_list):
    groups, peers = lax.axis_size("group"), lax.axis_size("row")
    blocks, per_row, side, _ = tiles.shape
    vectors = start_basis.shape[1]
    row_total = groups * peers * blocks * side
    live = jnp.arange(per_row, dtype=jnp.int32)[None, :] < tile_count[:, None]
    live = live.astype(jnp.float32)
    wide = tiles.astype(jnp.float32)
    sums = jnp.einsum("btij,bt->bi", wide * wide, live, precision=HIGH)
    root = (1e-06 + sums) ** (-0.25)
    wanted = recv_list.reshape(peers * SLOTS)
    take = jnp.clip(wanted - lax.axis_index("group") * peers * blocks, 0, peers * blocks - 1)
    basis, results = start_basis, []
    for _ in range(ITERS):
        scaled = basis * root[:, None, :]
        low, high = neighbours(scaled)
        received = jnp.take(lax.all_gather(scaled, "row", axis=0, tiled=True), take, axis=0)
        extended = jnp.concatenate([scaled, received, low, high], axis=0)
        picked = jnp.take(extended, tile_cols, axis=0) * live[:, :, None, None]
        product = jnp.einsum(
            "btij,btkj->bki", tiles, picked, precision=HIGH, preferred_element_type=jnp.float32
        )
        applied = product * root[:, None, :]
        gram = jnp.einsum("bki,bli->kl", applied, applied, precision=HIGH)
        factor = jnp.linalg.cholesky(lax.psum(gram, ("group", "row")) / row_total)
        inverse = lax.linalg.triangular_solve(
            factor, jnp.eye(vectors, dtype=jnp.float32), left_side=True, lower=True
        )
        basis = jnp.einsum("kl,bli->bki", inverse, applied, precision=HIGH)
        results.append(basis)
    return jnp.stack(results)


def local(start_basis, tiles, tile_cols, tile_count, recv_list):
    groups, peers = lax.axis_size("group"), lax.axis_size("row")
    blocks, per_row, side, _ = tiles.shape
    vectors = start_basis.shape[1]
    wanted = jnp.transpose(recv_list.reshape(peers, SLOTS))
    lists = pl.cdiv(peers * SLOTS, vectors)
    tile_bytes = tiles.size * 2
    far_tiles = far(tiles.reshape(-1, side))
    block_shape = (vectors, side)
    picked_shape = (peers * SLOTS,) + block_shape
    rim_shape = f32(RIM, *block_shape)
    kept = held_blocks(tiles)
    rest = pltpu.VMEM(((blocks - kept) * per_row * side, side), tiles.dtype)
    root, scaled, *rims, held, opening_rest = pl.pallas_call(
        functools.partial(roots_kernel, per_row),
        out_shape=(
            f32(blocks, 1, side),
            f32(blocks + lists, *block_shape),
            rim_shape,
            rim_shape,
            pltpu.VMEM((kept * per_row * side, side), tiles.dtype),
            rest,
        ),
        in_specs=[hbm()] * 4,
        out_specs=(vmem(),) * 6,
        scratch_shapes=[
            pltpu.SMEM((blocks,), jnp.int32),
            pltpu.SMEM((SLOTS, peers), jnp.int32),
            pltpu.VMEM((blocks,) + block_shape, jnp.float32),
            pltpu.SemaphoreType.DMA((5,)),
        ],
        compiler_params=params(),
        cost_estimate=cost(tiles.size * 2, tile_bytes),
        name="roots",
    )(far(tile_count), far(wanted), far_tiles, far(start_basis))
    slots = blocks + peers * SLOTS + 2 * RIM
    powers, grams = [], []
    for t in range(ITERS):
        last = t == ITERS - 1
        if t == 0:
            beside = swap(*rims)
            received = lax.all_gather(scaled, "row", axis=0)
        else:
            received = lax.all_to_all(outgoing, "row", 0, 0, tiled=True)
            beside = swap(*rims)
        scalars = [tile_count, tile_cols] + ([wanted] if t == 0 else [])
        arrays = [far_tiles if t else opening_rest, held, root, scaled, received, *beside]
        shapes = [f32(blocks, *block_shape)]
        specs = [vmem(), vmem()]
        if last:
            shapes += [pltpu.HBM((groups * peers, vectors // 2, LANES), jnp.float32)]
            specs = [vmem(), hbm()]
            scratch = [
                pltpu.VMEM((groups * peers, vectors // 2, LANES), jnp.float32),
                pltpu.SemaphoreType.DMA,
            ]
            arrays += grams
        else:
            shapes += [f32(vectors, vectors), f32(blocks, *block_shape), pltpu.HBM(picked_shape, jnp.float32)]
            shapes += [rim_shape] * 2
            specs += [vmem(), hbm(), vmem(), vmem()]
            scratch = [pltpu.VMEM(picked_shape, jnp.float32), pltpu.SemaphoreType.DMA]
            if t:
                arrays += [asked]
            else:
                shapes += [f32(peers * SLOTS, side)]
                specs += [vmem()]
        result = pl.pallas_call(
            functools.partial(apply_kernel, t),
            out_shape=tuple(shapes),
            in_specs=[hbm()] * len(scalars)
            + [hbm() if t else vmem()]
            + [vmem()] * (len(arrays) - 1),
            out_specs=tuple(specs),
            scratch_shapes=scratch
            + [
                pltpu.VMEM((slots + 1, PIECES * vectors, side), jnp.bfloat16),
            ]
            + ([rest, pltpu.SemaphoreType.DMA] if t else [])
            + [pltpu.SMEM(x.shape, jnp.int32) for x in scalars]
            + [pltpu.SemaphoreType.DMA((len(scalars),))],
            compiler_params=params(),
            cost_estimate=cost(tiles.size * 2 * vectors * PIECES, tile_bytes),
            name="apply_last" if last else "apply",
        )(*[far(x) for x in scalars], *arrays)
        powers.append(result[0])
        grams.append(result[1])
        if not last:
            scaled, outgoing, *rims = result[2:6]
            if t == 0:
                asked = result[6]
    gathered = lax.all_to_all(grams[-1], ("group", "row"), 0, 0, tiled=True)
    krylov, trust = pl.pallas_call(
        functools.partial(finish_kernel, float(groups * peers * blocks * side)),
        out_shape=(pltpu.HBM((ITERS, blocks, vectors, side), jnp.float32), jax.ShapeDtypeStruct((1,), jnp.int32)),
        in_specs=[vmem()] * (1 + ITERS),
        out_specs=(hbm(), smem()),
        scratch_shapes=[
            pltpu.VMEM((ITERS, blocks, vectors, side), jnp.float32),
            pltpu.SemaphoreType.DMA((ITERS,)),
        ],
        compiler_params=params(),
        name="finish",
    )(gathered, *powers)
    return lax.cond(
        trust[0] > 0,
        lambda *_: krylov,
        stepwise,
        start_basis, tiles, tile_cols, tile_count, recv_list,
    )


def solution(mesh):
    placed = (
        P(("group", "row"), None, None),
        P(("group", "row"), None, None, None),
        P(("group", "row"), None),
        P(("group", "row")),
        P("group", "row", None, None),
    )
    return jax.shard_map(
        local,
        mesh=mesh,
        in_specs=placed,
        out_specs=P(None, ("group", "row"), None, None),
        check_vma=False,
    )
```

```python
import functools

import jax
import jax.numpy as jnp
from jax import lax
from jax.experimental import pallas as pl
from jax.experimental.pallas import tpu as pltpu
from jax.sharding import PartitionSpec as P

SLOTS = 2
RIM = 2
ITERS = 3
MINLIVE = 10
LANES = 128
HELD_BYTES = 11 * 1024 * 1024 // 4
PIECES = 2
VMEM_BYTES = 24 * 1024 * 1024
TRUST = 64.0
TINY = 1e-25

HIGH = lax.Precision.HIGHEST
NT = (((1,), (1,)), ((), ()))


def vmem():
    return pl.BlockSpec(memory_space=pltpu.VMEM)


def smem():
    return pl.BlockSpec(memory_space=pltpu.SMEM)


def hbm():
    return pl.BlockSpec(memory_space=pltpu.HBM)


def far(x):
    return pltpu.with_memory_space_constraint(x, pltpu.HBM)


def f32(*shape):
    return jax.ShapeDtypeStruct(shape, jnp.float32)


def params():
    return pltpu.CompilerParams(vmem_limit_bytes=VMEM_BYTES)


def cost(flops, moved):
    return pl.CostEstimate(flops=flops, bytes_accessed=moved, transcendentals=0)


def held_tiles(tiles):
    count = tiles.shape[0] * tiles.shape[1]
    return min(count - 1, HELD_BYTES // (tiles.size // count * 2))


def load(tiles_hbm, start, tiles_ref, sem):
    copy = pltpu.make_async_copy(tiles_hbm.at[pl.ds(start, tiles_ref.shape[0])], tiles_ref, sem)
    copy.start()
    return copy


def start_all(pairs, sems):
    copies = [
        pltpu.make_async_copy(source, target, sems.at[n])
        for n, (source, target) in enumerate(pairs)
    ]
    for copy in copies:
        copy.start()
    return copies


def tile(held_ref, rest_ref, at):
    side = held_ref.shape[1]
    held = held_ref.shape[0] // side
    ref, at = (held_ref, at) if at < held else (rest_ref, at - held)
    return ref[at * side : (at + 1) * side]


def roots_kernel(per_row, count_hbm, want_hbm, tiles_hbm, basis_hbm, root_ref, sent_ref,
                 first_ref, second_ref, held_ref, rest_ref, count_ref, want_ref, basis_ref, sems):
    blocks, vectors, side = basis_ref.shape
    touched = pl.cdiv(held_ref.shape[0], per_row * side)
    peers = want_ref.shape[1]
    group = lax.axis_index("group")
    rest_load = load(tiles_hbm, held_ref.shape[0], rest_ref, sems.at[3])
    small = start_all(((count_hbm, count_ref), (want_hbm, want_ref), (basis_hbm, basis_ref)), sems)
    held_load = load(tiles_hbm, 0, held_ref, sems.at[4])
    for copy in small:
        copy.wait()
    for p in range(peers):
        owned = (group * peers + p) * blocks
        for c in range(SLOTS):
            at = jnp.full((1, side), want_ref[c, p] - owned, jnp.int32).astype(jnp.float32)
            block, row = divmod(p * SLOTS + c, vectors)
            sent_ref[blocks + block, row : row + 1] = at
    rest_load.wait()
    for b in list(range(touched, blocks)) + list(range(touched)):
        if b == 0:
            held_load.wait()
        total = jnp.zeros((side, side), jnp.float32)
        for s in range(per_row):
            wide = tile(held_ref, rest_ref, b * per_row + s).astype(jnp.float32)
            square = wide * wide
            if s >= MINLIVE:
                square = square * (s < count_ref[b]).astype(jnp.float32)
            total = total + square
        sums = jnp.sum(total.T, axis=0, keepdims=True)
        root = lax.rsqrt(jnp.sqrt(1e-06 + sums))
        root_ref[b] = root
        sent_ref[b] = basis_ref[b] * root
    swaps_into(group, blocks, sent_ref, first_ref, second_ref)


def swaps_into(group, blocks, scaled_ref, first_ref, second_ref):
    odd = group % 2
    for h in range(RIM):
        first_ref[h] = scaled_ref[(1 - odd) * (blocks - RIM) + h]
        second_ref[h] = scaled_ref[odd * (blocks - RIM) + h]


def pick_into(asked_ref, scaled_ref, out_ref):
    blocks, vectors, side = scaled_ref.shape
    for n in range(asked_ref.shape[0]):
        at = jnp.broadcast_to(asked_ref[n : n + 1], (vectors, side))
        value = scaled_ref[0]
        for b in range(1, blocks):
            value = jnp.where(at == float(b), scaled_ref[b], value)
        out_ref[n] = value


def pieces_of(x, count):
    parts = []
    for n in range(count):
        part = x.astype(jnp.bfloat16)
        parts.append(part)
        if n < count - 1:
            x = x - part.astype(jnp.float32)
    return parts


def split_into(x, out_ref, slot):
    vectors = x.shape[0]
    for n, part in enumerate(pieces_of(x, PIECES)):
        out_ref[slot, pl.ds(n * vectors, vectors)] = part


def gram_of(flat):
    k = flat.shape[0]
    stack = jnp.concatenate(pieces_of(flat, 3), axis=0)
    full = lax.dot_general(stack, stack, NT, preferred_element_type=jnp.float32)
    term = lambda i, j: full[i * k : (i + 1) * k, j * k : (j + 1) * k]
    small = term(1, 1) + (term(0, 2) + term(2, 0))
    return term(0, 0) + ((term(0, 1) + term(1, 0)) + small)


TERMS = ((0, 0), (0, 1), (1, 0), (1, 1), (0, 2), (2, 0))


def pack_grams(grams):
    half = grams[0].shape[0] // 2
    parts = [g[:half] for g in grams] + [g[half:] for g in grams]
    spare = LANES - len(parts) * grams[0].shape[1]
    return jnp.concatenate(parts + [jnp.zeros((half, spare), jnp.float32)], axis=1)


def unpack_grams(packed, vectors):
    upper = [packed[:, t * vectors : (t + 1) * vectors] for t in range(ITERS)]
    lower = [packed[:, (ITERS + t) * vectors : (ITERS + t + 1) * vectors] for t in range(ITERS)]
    return [jnp.concatenate(pair, axis=0) for pair in zip(upper, lower)]


def apply_kernel(step_at, *refs):
    last, opening = step_at == ITERS - 1, step_at == 0
    scalars = 3 if opening else 2
    scalars_hbm, refs = refs[:scalars], refs[scalars:]
    tiles_at, held_ref, root_ref, own_ref, recv_ref, swapped_ref, swapped_next_ref, *refs = refs
    *refs, scalar_sems = refs
    scalar_refs, refs = refs[-scalars:], refs[:-scalars]
    count_ref, cols_ref = scalar_refs[:2]
    if opening:
        want_ref = scalar_refs[2]
        *refs, table = refs
        rest_ref = tiles_at
    else:
        *refs, table, rest_ref, load_sem = refs
        rest_load = load(tiles_at, held_ref.shape[0], rest_ref, load_sem)
    small = start_all(zip(scalars_hbm, scalar_refs), scalar_sems)
    blocks, _, side = root_ref.shape
    per_row = cols_ref.shape[1]
    held = held_ref.shape[0] // (per_row * side)
    if last:
        *before, applied_ref, gram_hbm, packed_ref, sem = refs
    else:
        if not opening:
            asked_ref, *refs = refs
        applied_ref, gram_ref, scaled_ref, out_hbm, first_ref, second_ref, *refs = refs
        if opening:
            asked_ref, *refs = refs
        picked_ref, sem = refs
    vectors = own_ref.shape[1]
    group = lax.axis_index("group")
    slot = 0
    for b in range(blocks):
        split_into(own_ref[b], table, slot)
        slot += 1
    for copy in small:
        copy.wait()
    if opening:
        peers = recv_ref.shape[0]
        for p in range(peers):
            for c in range(SLOTS):
                at = jnp.clip(want_ref[c, p] - (group * peers + p) * blocks, 0, blocks - 1)
                split_into(recv_ref[p, at], table, slot)
                slot += 1
                entry = lax.axis_index("row") * SLOTS + c
                asked_ref[p * SLOTS + c : p * SLOTS + c + 1] = recv_ref[
                    p, blocks + entry // vectors, pl.ds(entry % vectors, 1)
                ]
    else:
        for n in range(recv_ref.shape[0]):
            split_into(recv_ref[n], table, slot)
            slot += 1
    odd = group % 2 == 1
    for a_ref, b_ref in ((swapped_ref, swapped_next_ref), (swapped_next_ref, swapped_ref)):
        for h in range(RIM):
            split_into(jnp.where(odd, a_ref[h], b_ref[h]), table, slot)
            slot += 1
    table[slot] = jnp.zeros(table.shape[1:], table.dtype)
    rows = []
    for b in range(blocks):
        picked = []
        for s in range(per_row):
            at = jnp.where(s < count_ref[b], cols_ref[b, s], slot)
            picked.append(table[at])
        x = jnp.concatenate(picked, axis=1)
        if b == held and not opening:
            rest_load.wait()
        t = [tile(held_ref, rest_ref, b * per_row + s) for s in range(per_row)]
        t = jnp.concatenate(t, axis=1)
        product = lax.dot_general(x, t, NT, preferred_element_type=jnp.float32)
        total = product[(PIECES - 1) * vectors :]
        for piece in range(PIECES - 2, -1, -1):
            total = total + product[piece * vectors : (piece + 1) * vectors]
        root = root_ref[b]
        row = total * root
        applied_ref[b] = row
        rows.append(row)
        if not last:
            scaled_ref[b] = row * root
    if not last:
        pick_into(asked_ref, scaled_ref, picked_ref)
        send = pltpu.make_async_copy(picked_ref, out_hbm, sem)
        send.start()
        swaps_into(group, blocks, scaled_ref, first_ref, second_ref)
    flat = jnp.concatenate(rows, axis=1)
    gram = gram_of(flat)
    if last:
        packed = pack_grams([ref[...] for ref in before] + [gram])
        for n in range(packed_ref.shape[0]):
            packed_ref[n] = packed
        send = pltpu.make_async_copy(packed_ref, gram_hbm, sem)
        send.start()
        send.wait()
    else:
        gram_ref[...] = gram
        send.wait()


def finish_kernel(row_total, grams_ref, *refs):
    applied_refs, (out_hbm, trust_ref, out_ref, sems) = refs[:ITERS], refs[ITERS:]
    devices = grams_ref.shape[0]
    blocks, vectors = out_ref.shape[1:3]
    sends = [pltpu.make_async_copy(out_ref.at[t], out_hbm.at[t], sems.at[t]) for t in range(ITERS)]
    total = grams_ref[0]
    for n in range(1, devices):
        total = total + grams_ref[n]
    rows = lax.broadcasted_iota(jnp.int32, (vectors, vectors), 0)
    lanes = lax.broadcasted_iota(jnp.int32, (vectors, vectors), 1)
    unit = (rows == lanes).astype(jnp.float32)
    grams = unpack_grams(total, vectors)
    columns = [
        [jnp.broadcast_to(gram[:, k : k + 1], (vectors, vectors)) for k in range(vectors)]
        for gram in grams
    ]
    inverses = [unit] * ITERS
    for j in range(vectors):
        for t, column in enumerate(columns):
            ratio = jnp.where(rows > j, column[j] * (1.0 / column[j][j : j + 1]), 0.0)
            for k in range(j + 1, vectors):
                column[k] = column[k] - ratio * column[k][j : j + 1]
            inverses[t] = inverses[t] - ratio * inverses[t][j : j + 1]
    good = jnp.bool_(True)
    for t in range(ITERS):
        pivots = columns[t][0]
        for j in range(1, vectors):
            pivots = jnp.where(rows == j, columns[t][j], pivots)
        inverse = inverses[t] * lax.rsqrt(pivots / row_total)
        squares = jnp.sum(grams[t] * unit, axis=0, keepdims=True)
        norm = jnp.sum(inverse * inverse * squares) / row_total
        good = good & (norm < TRUST) & (jnp.min(squares) > TINY)
        left = [part.astype(jnp.float32) for part in pieces_of(inverse, 3)]
        left = jnp.concatenate([left[i] for i, _ in TERMS], axis=1).astype(jnp.bfloat16)
        for b in range(blocks):
            right = pieces_of(applied_refs[t][b], 3)
            right = jnp.concatenate([right[j] for _, j in TERMS], axis=0)
            out_ref[t, b] = jnp.dot(left, right, preferred_element_type=jnp.float32)
        sends[t].start()
    trust_ref[0] = good.astype(jnp.int32)
    for send in sends:
        send.wait()


def neighbours(scaled):
    count, blocks = lax.axis_size("group"), scaled.shape[0]
    up = [(i, i + 1) for i in range(count - 1)]
    down = [(i + 1, i) for i in range(count - 1)]
    low = lax.ppermute(scaled[blocks - RIM :], "group", up)
    high = lax.ppermute(scaled[:RIM], "group", down)
    return low, high


def swap(first, second):
    count = lax.axis_size("group")
    ups = [[(i, i + 1) for i in range(start, count - 1, 2)] for start in (0, 1)]
    pairs = [up + [(j, i) for i, j in up] for up in ups]
    return [lax.ppermute(x, "group", pair) for x, pair in zip((first, second), pairs)]


def stepwise(start_basis, tiles, tile_cols, tile_count, recv_list):
    groups, peers = lax.axis_size("group"), lax.axis_size("row")
    blocks, per_row, side, _ = tiles.shape
    vectors = start_basis.shape[1]
    row_total = groups * peers * blocks * side
    live = jnp.arange(per_row, dtype=jnp.int32)[None, :] < tile_count[:, None]
    live = live.astype(jnp.float32)
    wide = tiles.astype(jnp.float32)
    sums = jnp.einsum("btij,bt->bi", wide * wide, live, precision=HIGH)
    root = (1e-06 + sums) ** (-0.25)
    wanted = recv_list.reshape(peers * SLOTS)
    take = jnp.clip(wanted - lax.axis_index("group") * peers * blocks, 0, peers * blocks - 1)
    basis, results = start_basis, []
    for _ in range(ITERS):
        scaled = basis * root[:, None, :]
        low, high = neighbours(scaled)
        received = jnp.take(lax.all_gather(scaled, "row", axis=0, tiled=True), take, axis=0)
        extended = jnp.concatenate([scaled, received, low, high], axis=0)
        picked = jnp.take(extended, tile_cols, axis=0) * live[:, :, None, None]
        product = jnp.einsum(
            "btij,btkj->bki", tiles, picked, precision=HIGH, preferred_element_type=jnp.float32
        )
        applied = product * root[:, None, :]
        gram = jnp.einsum("bki,bli->kl", applied, applied, precision=HIGH)
        factor = jnp.linalg.cholesky(lax.psum(gram, ("group", "row")) / row_total)
        inverse = lax.linalg.triangular_solve(
            factor, jnp.eye(vectors, dtype=jnp.float32), left_side=True, lower=True
        )
        basis = jnp.einsum("kl,bli->bki", inverse, applied, precision=HIGH)
        results.append(basis)
    return jnp.stack(results)


def local(start_basis, tiles, tile_cols, tile_count, recv_list):
    groups, peers = lax.axis_size("group"), lax.axis_size("row")
    blocks, per_row, side, _ = tiles.shape
    vectors = start_basis.shape[1]
    wanted = jnp.transpose(recv_list.reshape(peers, SLOTS))
    lists = pl.cdiv(peers * SLOTS, vectors)
    tile_bytes = tiles.size * 2
    far_tiles = far(tiles.reshape(-1, side))
    block_shape = (vectors, side)
    picked_shape = (peers * SLOTS,) + block_shape
    rim_shape = f32(RIM, *block_shape)
    kept = held_tiles(tiles)
    rest = pltpu.VMEM(((blocks * per_row - kept) * side, side), tiles.dtype)
    root, scaled, *rims, held, opening_rest = pl.pallas_call(
        functools.partial(roots_kernel, per_row),
        out_shape=(
            f32(blocks, 1, side),
            f32(blocks + lists, *block_shape),
            rim_shape,
            rim_shape,
            pltpu.VMEM((kept * side, side), tiles.dtype),
            rest,
        ),
        in_specs=[hbm()] * 4,
        out_specs=(vmem(),) * 6,
        scratch_shapes=[
            pltpu.SMEM((blocks,), jnp.int32),
            pltpu.SMEM((SLOTS, peers), jnp.int32),
            pltpu.VMEM((blocks,) + block_shape, jnp.float32),
            pltpu.SemaphoreType.DMA((5,)),
        ],
        compiler_params=params(),
        cost_estimate=cost(tiles.size * 2, tile_bytes),
        name="roots",
    )(far(tile_count), far(wanted), far_tiles, far(start_basis))
    slots = blocks + peers * SLOTS + 2 * RIM
    powers, grams = [], []
    for t in range(ITERS):
        last = t == ITERS - 1
        if t == 0:
            beside = swap(*rims)
            received = lax.all_gather(scaled, "row", axis=0)
        else:
            received = lax.all_to_all(outgoing, "row", 0, 0, tiled=True)
            beside = swap(*rims)
        scalars = [tile_count, tile_cols] + ([wanted] if t == 0 else [])
        arrays = [far_tiles if t else opening_rest, held, root, scaled, received, *beside]
        shapes = [f32(blocks, *block_shape)]
        specs = [vmem(), vmem()]
        if last:
            shapes += [pltpu.HBM((groups * peers, vectors // 2, LANES), jnp.float32)]
            specs = [vmem(), hbm()]
            scratch = [
                pltpu.VMEM((groups * peers, vectors // 2, LANES), jnp.float32),
                pltpu.SemaphoreType.DMA,
            ]
            arrays += grams
        else:
            shapes += [f32(vectors, vectors), f32(blocks, *block_shape), pltpu.HBM(picked_shape, jnp.float32)]
            shapes += [rim_shape] * 2
            specs += [vmem(), hbm(), vmem(), vmem()]
            scratch = [pltpu.VMEM(picked_shape, jnp.float32), pltpu.SemaphoreType.DMA]
            if t:
                arrays += [asked]
            else:
                shapes += [f32(peers * SLOTS, side)]
                specs += [vmem()]
        result = pl.pallas_call(
            functools.partial(apply_kernel, t),
            out_shape=tuple(shapes),
            in_specs=[hbm()] * len(scalars)
            + [hbm() if t else vmem()]
            + [vmem()] * (len(arrays) - 1),
            out_specs=tuple(specs),
            scratch_shapes=scratch
            + [
                pltpu.VMEM((slots + 1, PIECES * vectors, side), jnp.bfloat16),
            ]
            + ([rest, pltpu.SemaphoreType.DMA] if t else [])
            + [pltpu.SMEM(x.shape, jnp.int32) for x in scalars]
            + [pltpu.SemaphoreType.DMA((len(scalars),))],
            compiler_params=params(),
            cost_estimate=cost(tiles.size * 2 * vectors * PIECES, tile_bytes),
            name="apply_last" if last else "apply",
        )(*[far(x) for x in scalars], *arrays)
        powers.append(result[0])
        grams.append(result[1])
        if not last:
            scaled, outgoing, *rims = result[2:6]
            if t == 0:
                asked = result[6]
    gathered = lax.all_to_all(grams[-1], ("group", "row"), 0, 0, tiled=True)
    krylov, trust = pl.pallas_call(
        functools.partial(finish_kernel, float(groups * peers * blocks * side)),
        out_shape=(pltpu.HBM((ITERS, blocks, vectors, side), jnp.float32), jax.ShapeDtypeStruct((1,), jnp.int32)),
        in_specs=[vmem()] * (1 + ITERS),
        out_specs=(hbm(), smem()),
        scratch_shapes=[
            pltpu.VMEM((ITERS, blocks, vectors, side), jnp.float32),
            pltpu.SemaphoreType.DMA((ITERS,)),
        ],
        compiler_params=params(),
        name="finish",
    )(gathered, *powers)
    return lax.cond(
        trust[0] > 0,
        lambda *_: krylov,
        stepwise,
        start_basis, tiles, tile_cols, tile_count, recv_list,
    )


def solution(mesh):
    placed = (
        P(("group", "row"), None, None),
        P(("group", "row"), None, None, None),
        P(("group", "row"), None),
        P(("group", "row")),
        P("group", "row", None, None),
    )
    return jax.shard_map(
        local,
        mesh=mesh,
        in_specs=placed,
        out_specs=P(None, ("group", "row"), None, None),
        check_vma=False,
    )
```
